32 devices in a mesh: member: 2 (over y), lon: 8 (over z, x), lat: 2 (over core).
Axes of the slice: x: 2, y: 2, z: 4, core: 2. Of those that a mesh axis runs over, the one named last changes fastest.
Arguments:
- saved: float32 [128, 32, 640], P(('member', 'lat'), 'lon'), parts along dimension 0, may hold values from -6 to 6
- cotangent: float32 [128, 32, 640], P(('member', 'lat'), 'lon'), parts along dimension 0, may hold values from -6 to 6
- weight: float32 [640, 640], replicated, may hold values from -0.25 to 0.25
- coefs: float32 [27, 64, 640], P(None, None, 'lon'), may hold values from -1.25 to 1.25
- lon_step: int32 [64], replicated, may hold values from 1 to 8
- row_reach: int32 [64], replicated, may hold values from 1 to 4
Outputs:
- grad_input: float32 [640, 128, 32], P('lon', ('member', 'lat')), parts along dimension 1
- grad_weight: float32 [1280, 640], P(('member', 'lon'), 'lat'), parts along dimension 0
The draws below stay inside these ranges and needn't reach their ends.
There are 2 independent parts, one for each index of `member`. The reference program is written for one: setup_inputs(seed, part) draws one part's arguments, and reference() takes and returns one part's arrays. A program takes and returns all parts, laid end to end along the dimension named above; an argument that names none is the same for every part. Nothing has to cross between parts.
All inputs are finite; a program needn't handle non-finite values.
Results may differ from the reference program's by a relative error of at most 0.00007.
Values sent between devices are 32-bit elements; how exact they have to be, the bound alone decides.
A program may use at most 64 MiB of HBM per device.

```python
import math
import jax
import jax.numpy as jnp
from jax import lax

C = 640
TAPS = 27
NLAT = 64
NLON = 32


def with_ends(values, own_key, smallest, high):
    longest = values.shape.index(max(values.shape))
    spots = []
    for shift in (0, 1):
        where = [jax.random.randint(jax.random.fold_in(own_key, axis), (), 0, length) for axis, length in enumerate(values.shape)]
        where[longest] = (where[longest] + shift) % values.shape[longest]
        spots.append(tuple(where))
    return values.at[spots[0]].set(smallest).at[spots[1]].set(high)


def levels(rng, shape, split, least, high):
    loudness = 1.0
    for axis_at, blocks in split:
        steps = jax.random.uniform(jax.random.fold_in(jax.random.fold_in(rng, 6), axis_at), (blocks,), jnp.float32, least / len(split), high / len(split))
        loudness = loudness * jnp.repeat(jnp.exp(steps), shape[axis_at] // blocks).reshape((-1,) + (1,) * (len(shape) - 1 - axis_at))
    return loudness


def centred(own_key, dims, deviation, most, pieces=(), dtype=jnp.bfloat16):
    array = deviation * jax.random.normal(own_key, dims, jnp.float32)
    if pieces:
        array = array * levels(own_key, dims, pieces, -0.22, 0.18)
    return jnp.clip(array, -most, most).astype(dtype)


def setup_inputs(seed: int = 0, part: int = 0) -> dict:
    streams_of = jax.random.split(jax.random.key(seed), 7)
    part_keys = jax.random.split(jax.random.fold_in(streams_of[6], part), 7)
    return {
        "saved": centred(part_keys[0], (NLAT, NLON, C), 1.0, 6.0, ((0, 2), (1, 8)), jnp.float32),
        "cotangent": centred(part_keys[1], (NLAT, NLON, C), 1.0, 6.0, ((0, 2), (1, 8)), jnp.float32),
        "weight": centred(streams_of[2], (C, C), C ** -0.5, 0.25, (), jnp.float32),
        "coefs": centred(streams_of[3], (TAPS, NLAT, C), TAPS ** -0.5, 1.25, ((2, 8),), jnp.float32),
        "lon_step": with_ends(jax.random.randint(streams_of[4], (NLAT,), 1, 9), jax.random.fold_in(streams_of[4], 1), 1, 8).astype(jnp.int32),
        "row_reach": with_ends(jax.random.randint(streams_of[5], (NLAT,), 1, 5), jax.random.fold_in(streams_of[5], 1), 1, 4).astype(jnp.int32),
    }


def gelu_slope(values):
    cumulative = 0.5 * (1.0 + lax.erf(values * (1.0 / math.sqrt(2.0))))
    density = jnp.exp(-0.5 * values * values) * (1.0 / math.sqrt(2.0 * math.pi))
    return cumulative + values * density

def roll_rows(gradient, shifts):
    return jax.vmap(lambda one_row, amount: jnp.roll(one_row, amount, axis=-1), in_axes=(1, 0), out_axes=1)(gradient, shifts)

def tap_term(rolled, coefs, row_reach, offset):
    summed = jnp.zeros_like(rolled[0])
    for lon_side in range(3):
        tap_index = (offset + 4) * 3 + lon_side
        summed = summed + jnp.transpose(coefs[tap_index])[:, :, None] * rolled[lon_side]
    live_rows = (abs(offset) <= row_reach).astype(jnp.float32)
    return summed * live_rows[None, :, None]

def reference(saved, cotangent, weight, coefs, lon_step, row_reach):
    flat_rows = saved.reshape(NLAT * NLON, C)
    hidden = jnp.dot(flat_rows, weight, precision=lax.Precision.HIGHEST, preferred_element_type=jnp.float32)
    pre_grad = cotangent.reshape(NLAT * NLON, C) * gelu_slope(hidden)
    grad_weight = lax.dot_general(flat_rows, pre_grad, (((0,), (0,)), ((), ())), precision=lax.Precision.HIGHEST, preferred_element_type=jnp.float32)
    grad_weight = grad_weight * (1.0 / math.sqrt(NLAT * NLON))
    cell_grad = lax.dot_general(weight, pre_grad, (((1,), (1,)), ((), ())), precision=lax.Precision.HIGHEST, preferred_element_type=jnp.float32)
    cell_grad = cell_grad.reshape(C, NLAT, NLON)
    rolled = [roll_rows(cell_grad, lon_side * lon_step) for lon_side in (-1, 0, 1)]
    padded = jnp.zeros((C, NLAT + 8, NLON), jnp.float32)
    for offset in range(-4, 5):
        padded = padded.at[:, 4 + offset:4 + offset + NLAT].add(tap_term(rolled, coefs, row_reach, offset))
    return (padded[:, 4:4 + NLAT], grad_weight)
```

```python
import functools
import math

import jax
import jax.numpy as jnp
from jax import lax
from jax.experimental import pallas as pl
from jax.experimental.pallas import tpu as pltpu
from jax.sharding import PartitionSpec as P

MESH = pl.DeviceIdType.MESH
REACH = 4
MOST_STEP = 8


def gelu_slope(values):
    cumulative = 0.5 * (1.0 + lax.erf(values * (1.0 / math.sqrt(2.0))))
    density = jnp.exp(-0.5 * values * values) * (1.0 / math.sqrt(2.0 * math.pi))
    return cumulative + values * density


def halves(x):
    high = x.astype(jnp.bfloat16)
    low = (x - high.astype(jnp.float32)).astype(jnp.bfloat16)
    return high, low


def dot3(a, b, dims):
    (ah, al), (bh, bl) = a, b
    dot = lambda p, q: lax.dot_general(p, q, (dims, ((), ())), preferred_element_type=jnp.float32)
    return dot(ah, bh) + (dot(ah, bl) + dot(al, bh))


def flipped(me, j, n):
    result = 0
    bit = 1
    while bit < n:
        mine = lax.rem(lax.div(me, bit), 2)
        result = result + bit * ((1 - mine) if j & bit else mine)
        bit *= 2
    return result


def zeros_below(j):
    return (j & -j).bit_length() - 1


def kernel(
    n,
    step_ref, reach_ref, saved_ref, cot_ref, weight_ref, coefs_ref,
    acc_out, gw_out,
    s_t, s_t_peer, pg_t, pg_t_peer, cell, arrived, part, landed, grid_ref, halo, acc,
    lat_send, lat_recv, a2a_send, a2a_recv, gw_send, gw_recv,
):
    me = lax.axis_index("lon")
    lat = lax.axis_index("lat")
    other = 1 - lat
    rows, cols, channels = saved_ref.shape
    cells = rows * cols
    own = channels // n
    half = channels // 2
    all_lon = n * cols
    bits = n.bit_length() - 1

    barrier = pltpu.get_barrier_semaphore()
    for s in range(1, n):
        pl.semaphore_signal(barrier, inc=1, device_id={"lon": lax.rem(me + s, n)}, device_id_type=MESH)
    pl.semaphore_signal(barrier, inc=1, device_id={"lat": other}, device_id_type=MESH)

    saved = saved_ref[...].reshape(cells, channels)
    s_t[...] = saved.T.reshape(n, own, cells)
    pl.semaphore_wait(barrier, n)

    def to_peer(src, dst, slot):
        return pltpu.make_async_remote_copy(
            src_ref=src, dst_ref=dst, send_sem=lat_send.at[slot], recv_sem=lat_recv.at[slot],
            device_id={"lat": other}, device_id_type=MESH,
        )

    saved_copy = to_peer(s_t, s_t_peer, 0)
    saved_copy.start()

    weight = halves(weight_ref[...])
    hidden = dot3(halves(saved), weight, ((1,), (0,)))
    pre_grad = cot_ref[...].reshape(cells, channels) * gelu_slope(hidden)
    turned = pre_grad.T
    pg_t[...] = turned.reshape(2, half, cells)
    pg_copy = to_peer(pg_t.at[other], pg_t_peer, 1)
    pg_copy.start()

    cell[...] = dot3(weight, halves(turned), ((1,), (0,))).reshape(n, own, cells)

    def across(s):
        dest = lax.rem(me + s, n)
        return pltpu.make_async_remote_copy(
            src_ref=cell.at[dest], dst_ref=arrived.at[me], send_sem=a2a_send.at[s - 1], recv_sem=a2a_recv.at[s - 1],
            device_id={"lon": dest}, device_id_type=MESH,
        )

    moves = [across(s) for s in range(1, n)]
    for move in moves:
        move.start()

    def slot_of(stage, j):
        return n - (n >> stage) + j // (2 << stage)

    def hand_on(j):
        stage = zeros_below(j)
        slot = slot_of(stage, j)
        return pltpu.make_async_remote_copy(
            src_ref=part.at[j], dst_ref=landed.at[slot], send_sem=gw_send.at[slot], recv_sem=gw_recv.at[slot],
            device_id={"lon": flipped(me, 1 << stage, n)}, device_id_type=MESH,
        )

    order = sorted(range(n), key=lambda j: -int(format(j, "b").zfill(bits)[::-1], 2))
    sends = {j: hand_on(j) for j in range(1, n)}
    mine = halves(pg_t[lat])
    saved_copy.wait_recv()
    pg_copy.wait_recv()
    theirs = halves(pg_t_peer[...])
    for j in order:
        owner = flipped(me, j, n)
        part[j] = dot3(halves(s_t[owner]), mine, ((1,), (1,))) + dot3(halves(s_t_peer[owner]), theirs, ((1,), (1,)))
        if j % 2:
            sends[j].start()

    def gather(j):
        total = part[j]
        for stage in range(bits if j == 0 else zeros_below(j)):
            came = j + (1 << stage)
            sends[came].wait_recv()
            total = total + landed[slot_of(stage, j)]
        return total

    later = [j for j in order if j % 2 == 0 and j]
    first = [j for j in later if j % 4]
    rest = [j for j in later if not j % 4]
    for j in first:
        part[j] = gather(j)
        sends[j].start()

    acc[...] = jnp.zeros_like(acc)
    arrived[me] = cell[me]
    for move in moves:
        move.wait_recv()
    for source in range(n):
        grid_ref[:, source * cols : (source + 1) * cols, :] = arrived[source].T.reshape(rows, cols, own)

    halo_copy = pltpu.make_async_remote_copy(
        src_ref=grid_ref.at[pl.ds((rows - REACH) * other, REACH)], dst_ref=halo,
        send_sem=lat_send.at[2], recv_sem=lat_recv.at[2],
        device_id={"lat": other}, device_id_type=MESH,
    )
    halo_copy.start()

    for j in rest:
        part[j] = gather(j)
        sends[j].start()

    def scatter(values, row, local):
        step = jnp.full(values.shape, step_ref[row], jnp.int32)
        reach = reach_ref[row]
        up = values
        down = values
        bit = 1
        while bit <= MOST_STEP:
            chosen = (step & bit) != 0
            up = jnp.where(chosen, jnp.roll(up, bit, axis=0), up)
            down = jnp.where(chosen, jnp.roll(down, -bit, axis=0), down)
            bit *= 2
        rolled = (down, values, up)
        for offset in range(-REACH, REACH + 1):
            live = jnp.where(abs(offset) <= reach, 1.0, 0.0).astype(jnp.float32)
            summed = None
            for side in range(3):
                term = coefs_ref[3 * (offset + REACH) + side, pl.ds(row, 1), :] * live * rolled[side]
                summed = term if summed is None else summed + term
            acc[local + offset + 2 * REACH] += summed

    @pl.loop(0, rows)
    def _(i):
        scatter(grid_ref[i], lat * rows + i, i)

    halo_copy.wait_recv()

    @pl.loop(0, REACH)
    def _(i):
        local = rows * other - REACH * lat + i
        scatter(halo[i], lat * rows + local, local)

    acc_out[...] = acc[2 * REACH : 2 * REACH + rows]
    gw_out[...] = gather(0)

    saved_copy.wait_send()
    pg_copy.wait_send()
    halo_copy.wait_send()
    for move in moves:
        move.wait_send()
    for j in range(1, n):
        sends[j].wait_send()


def kernel_body(saved, cotangent, weight, coefs, lon_step, row_reach):
    rows, cols, channels = saved.shape
    n = lax.axis_size("lon")
    own = channels // n
    half = channels // 2
    cells = rows * cols
    f32 = jnp.float32
    vmem = pl.BlockSpec(memory_space=pltpu.VMEM)
    smem = pl.BlockSpec(memory_space=pltpu.SMEM)
    acc, grad = pl.pallas_call(
        functools.partial(kernel, n),
        out_shape=(
            jax.ShapeDtypeStruct((rows, n * cols, own), f32),
            jax.ShapeDtypeStruct((own, half), f32),
        ),
        in_specs=[smem, smem, vmem, vmem, vmem, vmem],
        out_specs=(vmem, vmem),
        scratch_shapes=[
            pltpu.VMEM((n, own, cells), f32),
            pltpu.VMEM((n, own, cells), f32),
            pltpu.VMEM((2, half, cells), f32),
            pltpu.VMEM((half, cells), f32),
            pltpu.VMEM((n, own, cells), f32),
            pltpu.VMEM((n, own, cells), f32),
            pltpu.VMEM((n, own, half), f32),
            pltpu.VMEM((n - 1, own, half), f32),
            pltpu.VMEM((rows, n * cols, own), f32),
            pltpu.VMEM((REACH, n * cols, own), f32),
            pltpu.VMEM((rows + 4 * REACH, n * cols, own), f32),
            pltpu.SemaphoreType.DMA((3,)),
            pltpu.SemaphoreType.DMA((3,)),
            pltpu.SemaphoreType.DMA((n - 1,)),
            pltpu.SemaphoreType.DMA((n - 1,)),
            pltpu.SemaphoreType.DMA((n - 1,)),
            pltpu.SemaphoreType.DMA((n - 1,)),
        ],
        compiler_params=pltpu.CompilerParams(
            collective_id=0, has_side_effects=True, vmem_limit_bytes=40 * 1024 * 1024
        ),
    )(lon_step, row_reach, saved, cotangent, weight, coefs)
    scale = 1.0 / math.sqrt(rows * 2 * n * cols)
    return jnp.transpose(acc, (2, 0, 1)), grad * scale


def with_halo(x, sides, width):
    for axis, dim in sides:
        peers, length = (lax.axis_size(axis), x.shape[dim])
        up = [(i, (i + 1) % peers) for i in range(peers - 1)]
        down = [(j, i) for i, j in up]
        last = lax.slice_in_dim(x, length - width, length, axis=dim)
        initial = lax.slice_in_dim(x, 0, width, axis=dim)
        before = lax.ppermute(last, axis, up)
        after = lax.ppermute(initial, axis, down)
        x = jnp.concatenate([before, x, after], axis=dim)
    return x


def shift_rows(gradient, shifts, direction):
    width = gradient.shape[2]
    if direction == 0:
        return gradient
    wrapped = jnp.concatenate([gradient[:, :, width - 8 :], gradient, gradient[:, :, :8]], axis=2)
    result = gradient
    for amount in range(1, 9):
        begin = 8 - direction * amount
        piece = wrapped[:, :, begin : begin + width]
        result = jnp.where((shifts == amount)[None, :, None], piece, result)
    return result


def tap_term(rolled, coefs, row_reach, offset):
    summed = jnp.zeros_like(rolled[0])
    for lon_side in range(3):
        tap_index = (offset + 4) * 3 + lon_side
        summed = summed + jnp.transpose(coefs[tap_index])[:, :, None] * rolled[lon_side]
    live_rows = (abs(offset) <= row_reach).astype(jnp.float32)
    return summed * live_rows[None, :, None]


def collective_body(saved, cotangent, weight, coefs, lon_step, row_reach):
    lat_rows, lon_cols, channels = saved.shape
    lon_devices = lax.axis_size("lon")
    lat_devices = lax.axis_size("lat")
    own_channels = channels // lon_devices
    all_lon = lon_devices * lon_cols
    flat_rows = saved.reshape(lat_rows * lon_cols, channels)
    hidden = jnp.dot(
        flat_rows, weight, precision=lax.Precision.HIGHEST, preferred_element_type=jnp.float32
    )
    pre_grad = cotangent.reshape(lat_rows * lon_cols, channels) * gelu_slope(hidden)
    scale_factor = 1.0 / math.sqrt(lat_rows * lat_devices * all_lon)
    cell_grad = lax.dot_general(
        weight,
        pre_grad,
        (((1,), (1,)), ((), ())),
        precision=lax.Precision.HIGHEST,
        preferred_element_type=jnp.float32,
    )
    moved = lax.all_to_all(cell_grad, "lon", split_axis=0, concat_axis=1, tiled=True)
    gradient = (
        moved.reshape(own_channels, lon_devices, lat_rows, lon_cols)
        .transpose(0, 2, 1, 3)
        .reshape(own_channels, lat_rows, all_lon)
    )
    own_block = lax.psum_scatter(
        lax.dot_general(
            flat_rows,
            pre_grad,
            (((0,), (0,)), ((), ())),
            precision=lax.Precision.HIGHEST,
            preferred_element_type=jnp.float32,
        ),
        "lon",
        scatter_dimension=0,
        tiled=True,
    )
    grad_weight = lax.psum_scatter(own_block, "lat", scatter_dimension=1, tiled=True) * scale_factor
    row_start = lax.axis_index("lat") * lat_rows
    extended = with_halo(gradient, (("lat", 1),), 4)
    steps_padded = jnp.pad(lon_step, 4, constant_values=1)
    reach_padded = jnp.pad(row_reach, 4)
    coefs_padded = jnp.pad(coefs, ((0, 0), (4, 4), (0, 0)))
    wide_steps = lax.dynamic_slice_in_dim(steps_padded, row_start, lat_rows + 8)
    wide_reach = lax.dynamic_slice_in_dim(reach_padded, row_start, lat_rows + 8)
    wide_coefs = lax.dynamic_slice_in_dim(coefs_padded, row_start, lat_rows + 8, 1)
    rolled = [shift_rows(extended, wide_steps, lon_side) for lon_side in (-1, 0, 1)]
    result = jnp.zeros((own_channels, lat_rows, all_lon), jnp.float32)
    for offset in range(-4, 5):
        tap_sum = tap_term(rolled, wide_coefs, wide_reach, offset)
        result = result + tap_sum[:, 4 - offset : 4 - offset + lat_rows]
    return (result, grad_weight)


def body(saved, cotangent, weight, coefs, lon_step, row_reach):
    rows, cols, channels = saved.shape
    n = lax.axis_size("lon")
    fits = (
        lax.axis_size("lat") == 2
        and 4 <= n <= 16
        and n & (n - 1) == 0
        and channels % (16 * n) == 0
        and (rows * cols) % 128 == 0
        and rows >= REACH
        and n * cols >= MOST_STEP
    )
    run = kernel_body if fits else collective_body
    return run(saved, cotangent, weight, coefs, lon_step, row_reach)


def solution(mesh):
    placed = (
        P(("member", "lat"), "lon", None),
        P(("member", "lat"), "lon", None),
        P(),
        P(None, None, "lon"),
        P(),
        P(),
    )
    return jax.shard_map(
        body,
        mesh=mesh,
        in_specs=placed,
        out_specs=(P("lon", ("member", "lat"), None), P(("member", "lon"), "lat")),
        check_vma=False,
    )
```

```python
import functools
import math

import jax
import jax.numpy as jnp
from jax import lax
from jax.experimental import pallas as pl
from jax.experimental.pallas import tpu as pltpu
from jax.sharding import PartitionSpec as P

MESH = pl.DeviceIdType.MESH
REACH = 4
MOST_STEP = 8
LANES = 128


def gelu_slope(values):
    cumulative = 0.5 * (1.0 + lax.erf(values * (1.0 / math.sqrt(2.0))))
    density = jnp.exp(-0.5 * values * values) * (1.0 / math.sqrt(2.0 * math.pi))
    return cumulative + values * density


def halves(x):
    high = x.astype(jnp.bfloat16)
    low = (x - high.astype(jnp.float32)).astype(jnp.bfloat16)
    return high, low


def dot3(a, b, dims):
    (ah, al), (bh, bl) = a, b
    dot = lambda p, q: lax.dot_general(p, q, (dims, ((), ())), preferred_element_type=jnp.float32)
    return dot(ah, bh) + (dot(ah, bl) + dot(al, bh))


def flipped(me, j, n):
    result = 0
    bit = 1
    while bit < n:
        mine = lax.rem(lax.div(me, bit), 2)
        result = result + bit * ((1 - mine) if j & bit else mine)
        bit *= 2
    return result


def zeros_below(j):
    return (j & -j).bit_length() - 1


def kernel(
    n,
    step_in, reach_in, saved_in, cot_in, weight_in, coefs_in,
    acc_out, gw_out,
    step_ref, reach_ref, saved_ref, cot_ref, weight_ref, coefs_ref, load_sem,
    s_t, s_t_peer, pg_t, pg_t_peer, cell, arrived, part, landed, grid_ref, halo, acc,
    lat_send, lat_recv, a2a_send, a2a_recv, gw_send, gw_recv,
):
    me = lax.axis_index("lon")
    lat = lax.axis_index("lat")
    other = 1 - lat
    rows, cols, channels = saved_ref.shape
    cells = rows * cols
    own = channels // n
    half = channels // 2
    all_lon = n * cols
    bits = n.bit_length() - 1
    full, tail = divmod(half, LANES)

    pairs = (
        (saved_in, saved_ref), (weight_in, weight_ref), (cot_in, cot_ref),
        (coefs_in, coefs_ref), (step_in, step_ref), (reach_in, reach_ref),
    )
    loads = [pltpu.make_async_copy(src, dst, load_sem.at[i]) for i, (src, dst) in enumerate(pairs)]
    for load in loads:
        load.start()

    barrier = pltpu.get_barrier_semaphore()
    for s in range(1, n):
        pl.semaphore_signal(barrier, inc=1, device_id={"lon": lax.rem(me + s, n)}, device_id_type=MESH)
    pl.semaphore_signal(barrier, inc=1, device_id={"lat": other}, device_id_type=MESH)

    acc[...] = jnp.zeros_like(acc)
    loads[0].wait()
    saved = saved_ref[...].reshape(cells, channels)
    s_t[...] = saved.T.reshape(n, own, cells)
    loads[1].wait()
    weight = halves(weight_ref[...])
    hidden = dot3(halves(saved), weight, ((1,), (0,)))
    pl.semaphore_wait(barrier, n)

    def to_peer(src, dst, slot):
        return pltpu.make_async_remote_copy(
            src_ref=src, dst_ref=dst, send_sem=lat_send.at[slot], recv_sem=lat_recv.at[slot],
            device_id={"lat": other}, device_id_type=MESH,
        )

    saved_copy = to_peer(s_t, s_t_peer, 0)
    saved_copy.start()

    loads[2].wait()
    pre_grad = cot_ref[...].reshape(cells, channels) * gelu_slope(hidden)
    turned = pre_grad.T
    pg_t[...] = turned.reshape(2, half, cells)
    pg_copy = to_peer(pg_t.at[other], pg_t_peer, 1)
    pg_copy.start()

    cell[...] = dot3(weight, halves(turned), ((1,), (0,))).reshape(n, own, cells)

    def across(s):
        dest = lax.rem(me + s, n)
        return pltpu.make_async_remote_copy(
            src_ref=cell.at[dest], dst_ref=arrived.at[me], send_sem=a2a_send.at[s - 1], recv_sem=a2a_recv.at[s - 1],
            device_id={"lon": dest}, device_id_type=MESH,
        )

    moves = [across(s) for s in range(1, n)]
    for move in moves:
        move.start()

    def slot_of(stage, j):
        return n - (n >> stage) + j // (2 << stage)

    def hand_on(j):
        stage = zeros_below(j)
        slot = slot_of(stage, j)
        return pltpu.make_async_remote_copy(
            src_ref=part.at[j], dst_ref=landed.at[slot], send_sem=gw_send.at[slot], recv_sem=gw_recv.at[slot],
            device_id={"lon": flipped(me, 1 << stage, n)}, device_id_type=MESH,
        )

    order = sorted(range(n), key=lambda j: -int(format(j, "b").zfill(bits)[::-1], 2))
    sends = {j: hand_on(j) for j in range(1, n)}
    saved_copy.wait_recv()
    pg_copy.wait_recv()
    columns = halves(jnp.concatenate([pg_t[lat], pg_t_peer[...]], axis=1))
    for members in (order[: n // 2], order[n // 2 :]):
        owners = [flipped(me, j, n) for j in members]
        own_cells = jnp.concatenate([s_t[k] for k in owners], axis=0)
        peer_cells = jnp.concatenate([s_t_peer[k] for k in owners], axis=0)
        product = dot3(halves(jnp.concatenate([own_cells, peer_cells], axis=1)), columns, ((1,), (1,)))
        for at, j in enumerate(members):
            block = product[at * own : (at + 1) * own]
            for i in range(full):
                part[j, i * own : (i + 1) * own] = block[:, i * LANES : (i + 1) * LANES]
            if tail:
                rest = block[:, full * LANES :]
                part[j, full * own :] = jnp.concatenate([rest[: own // 2], rest[own // 2 :]], axis=1)
            if j % 2:
                sends[j].start()

    def gather(j):
        total = part[j]
        for stage in range(bits if j == 0 else zeros_below(j)):
            came = j + (1 << stage)
            sends[came].wait_recv()
            total = total + landed[slot_of(stage, j)]
        return total

    later = [j for j in order if j % 2 == 0 and j]
    first = [j for j in later if j % 4]
    rest = [j for j in later if not j % 4]
    for j in first:
        part[j] = gather(j)
        sends[j].start()

    arrived[me] = cell[me]
    for move in moves:
        move.wait_recv()
    for source in range(n):
        grid_ref[:, source * cols : (source + 1) * cols, :] = arrived[source].T.reshape(rows, cols, own)

    halo_copy = pltpu.make_async_remote_copy(
        src_ref=grid_ref.at[pl.ds((rows - REACH) * other, REACH)], dst_ref=halo,
        send_sem=lat_send.at[2], recv_sem=lat_recv.at[2],
        device_id={"lat": other}, device_id_type=MESH,
    )
    halo_copy.start()

    for j in rest:
        part[j] = gather(j)
        sends[j].start()

    def scatter(values, row, local):
        step = jnp.full(values.shape, step_ref[row], jnp.int32)
        reach = reach_ref[row]
        up = values
        down = values
        bit = 1
        while bit <= MOST_STEP:
            chosen = (step & bit) != 0
            up = jnp.where(chosen, jnp.roll(up, bit, axis=0), up)
            down = jnp.where(chosen, jnp.roll(down, -bit, axis=0), down)
            bit *= 2
        rolled = (down, values, up)
        for offset in range(-REACH, REACH + 1):
            live = jnp.where(abs(offset) <= reach, 1.0, 0.0).astype(jnp.float32)
            summed = None
            for side in range(3):
                term = coefs_ref[3 * (offset + REACH) + side, pl.ds(row, 1), :] * live * rolled[side]
                summed = term if summed is None else summed + term
            acc[local + offset + 2 * REACH] += summed

    for load in loads[3:]:
        load.wait()

    @pl.loop(0, rows, unroll=2)
    def _(i):
        scatter(grid_ref[i], lat * rows + i, i)

    halo_copy.wait_recv()

    @pl.loop(0, REACH)
    def _(i):
        local = rows * other - REACH * lat + i
        scatter(halo[i], lat * rows + local, local)

    acc_out[...] = acc[2 * REACH : 2 * REACH + rows]
    total = gather(0)
    for i in range(full):
        gw_out[:, i * LANES : (i + 1) * LANES] = total[i * own : (i + 1) * own]
    if tail:
        packed = total[full * own :]
        gw_out[: own // 2, full * LANES :] = packed[:, :tail]
        gw_out[own // 2 :, full * LANES :] = packed[:, tail:]

    saved_copy.wait_send()
    pg_copy.wait_send()
    halo_copy.wait_send()
    for move in moves:
        move.wait_send()
    for j in range(1, n):
        sends[j].wait_send()


def kernel_body(saved, cotangent, weight, coefs, lon_step, row_reach):
    rows, cols, channels = saved.shape
    n = lax.axis_size("lon")
    own = channels // n
    half = channels // 2
    cells = rows * cols
    f32 = jnp.float32
    vmem = pl.BlockSpec(memory_space=pltpu.VMEM)
    anywhere = pl.BlockSpec(memory_space=pl.ANY)
    packed_rows = own * half // LANES
    acc, grad = pl.pallas_call(
        functools.partial(kernel, n),
        out_shape=(
            jax.ShapeDtypeStruct((rows, n * cols, own), f32),
            jax.ShapeDtypeStruct((own, half), f32),
        ),
        in_specs=[anywhere] * 6,
        out_specs=(vmem, vmem),
        scratch_shapes=[
            pltpu.SMEM(lon_step.shape, lon_step.dtype),
            pltpu.SMEM(row_reach.shape, row_reach.dtype),
            pltpu.VMEM(saved.shape, f32),
            pltpu.VMEM(cotangent.shape, f32),
            pltpu.VMEM(weight.shape, f32),
            pltpu.VMEM(coefs.shape, f32),
            pltpu.SemaphoreType.DMA((6,)),
            pltpu.VMEM((n, own, cells), f32),
            pltpu.VMEM((n, own, cells), f32),
            pltpu.VMEM((2, half, cells), f32),
            pltpu.VMEM((half, cells), f32),
            pltpu.VMEM((n, own, cells), f32),
            pltpu.VMEM((n, own, cells), f32),
            pltpu.VMEM((n, packed_rows, LANES), f32),
            pltpu.VMEM((n - 1, packed_rows, LANES), f32),
            pltpu.VMEM((rows, n * cols, own), f32),
            pltpu.VMEM((REACH, n * cols, own), f32),
            pltpu.VMEM((rows + 4 * REACH, n * cols, own), f32),
            pltpu.SemaphoreType.DMA((3,)),
            pltpu.SemaphoreType.DMA((3,)),
            pltpu.SemaphoreType.DMA((n - 1,)),
            pltpu.SemaphoreType.DMA((n - 1,)),
            pltpu.SemaphoreType.DMA((n - 1,)),
            pltpu.SemaphoreType.DMA((n - 1,)),
        ],
        compiler_params=pltpu.CompilerParams(
            collective_id=0, has_side_effects=True, vmem_limit_bytes=63 * 1024 * 1024
        ),
    )(lon_step, row_reach, saved, cotangent, weight, coefs)
    scale = 1.0 / math.sqrt(rows * 2 * n * cols)
    return jnp.transpose(acc, (2, 0, 1)), grad * scale


def with_halo(x, sides, width):
    for axis, dim in sides:
        peers, length = (lax.axis_size(axis), x.shape[dim])
        up = [(i, (i + 1) % peers) for i in range(peers - 1)]
        down = [(j, i) for i, j in up]
        last = lax.slice_in_dim(x, length - width, length, axis=dim)
        initial = lax.slice_in_dim(x, 0, width, axis=dim)
        before = lax.ppermute(last, axis, up)
        after = lax.ppermute(initial, axis, down)
        x = jnp.concatenate([before, x, after], axis=dim)
    return x


def shift_rows(gradient, shifts, direction):
    width = gradient.shape[2]
    if direction == 0:
        return gradient
    wrapped = jnp.concatenate([gradient[:, :, width - 8 :], gradient, gradient[:, :, :8]], axis=2)
    result = gradient
    for amount in range(1, 9):
        begin = 8 - direction * amount
        piece = wrapped[:, :, begin : begin + width]
        result = jnp.where((shifts == amount)[None, :, None], piece, result)
    return result


def tap_term(rolled, coefs, row_reach, offset):
    summed = jnp.zeros_like(rolled[0])
    for lon_side in range(3):
        tap_index = (offset + 4) * 3 + lon_side
        summed = summed + jnp.transpose(coefs[tap_index])[:, :, None] * rolled[lon_side]
    live_rows = (abs(offset) <= row_reach).astype(jnp.float32)
    return summed * live_rows[None, :, None]


def collective_body(saved, cotangent, weight, coefs, lon_step, row_reach):
    lat_rows, lon_cols, channels = saved.shape
    lon_devices = lax.axis_size("lon")
    lat_devices = lax.axis_size("lat")
    own_channels = channels // lon_devices
    all_lon = lon_devices * lon_cols
    flat_rows = saved.reshape(lat_rows * lon_cols, channels)
    hidden = jnp.dot(
        flat_rows, weight, precision=lax.Precision.HIGHEST, preferred_element_type=jnp.float32
    )
    pre_grad = cotangent.reshape(lat_rows * lon_cols, channels) * gelu_slope(hidden)
    scale_factor = 1.0 / math.sqrt(lat_rows * lat_devices * all_lon)
    cell_grad = lax.dot_general(
        weight,
        pre_grad,
        (((1,), (1,)), ((), ())),
        precision=lax.Precision.HIGHEST,
        preferred_element_type=jnp.float32,
    )
    moved = lax.all_to_all(cell_grad, "lon", split_axis=0, concat_axis=1, tiled=True)
    gradient = (
        moved.reshape(own_channels, lon_devices, lat_rows, lon_cols)
        .transpose(0, 2, 1, 3)
        .reshape(own_channels, lat_rows, all_lon)
    )
    own_block = lax.psum_scatter(
        lax.dot_general(
            flat_rows,
            pre_grad,
            (((0,), (0,)), ((), ())),
            precision=lax.Precision.HIGHEST,
            preferred_element_type=jnp.float32,
        ),
        "lon",
        scatter_dimension=0,
        tiled=True,
    )
    grad_weight = lax.psum_scatter(own_block, "lat", scatter_dimension=1, tiled=True) * scale_factor
    row_start = lax.axis_index("lat") * lat_rows
    extended = with_halo(gradient, (("lat", 1),), 4)
    steps_padded = jnp.pad(lon_step, 4, constant_values=1)
    reach_padded = jnp.pad(row_reach, 4)
    coefs_padded = jnp.pad(coefs, ((0, 0), (4, 4), (0, 0)))
    wide_steps = lax.dynamic_slice_in_dim(steps_padded, row_start, lat_rows + 8)
    wide_reach = lax.dynamic_slice_in_dim(reach_padded, row_start, lat_rows + 8)
    wide_coefs = lax.dynamic_slice_in_dim(coefs_padded, row_start, lat_rows + 8, 1)
    rolled = [shift_rows(extended, wide_steps, lon_side) for lon_side in (-1, 0, 1)]
    result = jnp.zeros((own_channels, lat_rows, all_lon), jnp.float32)
    for offset in range(-4, 5):
        tap_sum = tap_term(rolled, wide_coefs, wide_reach, offset)
        result = result + tap_sum[:, 4 - offset : 4 - offset + lat_rows]
    return (result, grad_weight)


def body(saved, cotangent, weight, coefs, lon_step, row_reach):
    rows, cols, channels = saved.shape
    n = lax.axis_size("lon")
    fits = (
        lax.axis_size("lat") == 2
        and 4 <= n <= 16
        and n & (n - 1) == 0
        and channels % (16 * n) == 0
        and channels % LANES == 0
        and (rows * cols) % 128 == 0
        and rows >= REACH
        and n * cols >= MOST_STEP
    )
    run = kernel_body if fits else collective_body
    return run(saved, cotangent, weight, coefs, lon_step, row_reach)


def solution(mesh):
    placed = (
        P(("member", "lat"), "lon", None),
        P(("member", "lat"), "lon", None),
        P(),
        P(None, None, "lon"),
        P(),
        P(),
    )
    return jax.shard_map(
        body,
        mesh=mesh,
        in_specs=placed,
        out_specs=(P("lon", ("member", "lat"), None), P(("member", "lon"), "lat")),
        check_vma=False,
    )
```

```python
import functools
import math

import jax
import jax.numpy as jnp
from jax import lax
from jax.experimental import pallas as pl
from jax.experimental.pallas import tpu as pltpu
from jax.sharding import PartitionSpec as P

MESH = pl.DeviceIdType.MESH
REACH = 4
MOST_STEP = 8
LANES = 128


def gelu_slope(values):
    cumulative = 0.5 * (1.0 + lax.erf(values * (1.0 / math.sqrt(2.0))))
    density = jnp.exp(-0.5 * values * values) * (1.0 / math.sqrt(2.0 * math.pi))
    return cumulative + values * density


def halves(x):
    high = x.astype(jnp.bfloat16)
    low = (x - high.astype(jnp.float32)).astype(jnp.bfloat16)
    return high, low


def dot3(a, b, dims):
    (ah, al), (bh, bl) = a, b
    dot = lambda p, q: lax.dot_general(p, q, (dims, ((), ())), preferred_element_type=jnp.float32)
    return dot(ah, bh) + (dot(ah, bl) + dot(al, bh))


def flipped(me, j, n):
    result = 0
    bit = 1
    while bit < n:
        mine = lax.rem(lax.div(me, bit), 2)
        result = result + bit * ((1 - mine) if j & bit else mine)
        bit *= 2
    return result


def zeros_below(j):
    return (j & -j).bit_length() - 1


def kernel(
    n,
    step_in, reach_in, saved_in, cot_in, weight_in, coefs_in,
    acc_out, gw_out,
    step_ref, reach_ref, saved_ref, cot_ref, weight_ref, coefs_ref, load_sem,
    s_t, s_t_peer, pg_t, pg_t_peer, cell, arrived, part, landed, grid_ref, halo, acc,
    lat_send, lat_recv, a2a_send, a2a_recv, gw_send, gw_recv,
):
    me = lax.axis_index("lon")
    lat = lax.axis_index("lat")
    other = 1 - lat
    rows, cols, channels = saved_ref.shape
    cells = rows * cols
    own = channels // n
    half = channels // 2
    all_lon = n * cols
    bits = n.bit_length() - 1
    full, tail = divmod(half, LANES)

    pairs = (
        (saved_in, saved_ref), (weight_in, weight_ref), (cot_in, cot_ref),
        (coefs_in, coefs_ref), (step_in, step_ref), (reach_in, reach_ref),
    )
    loads = [pltpu.make_async_copy(src, dst, load_sem.at[i]) for i, (src, dst) in enumerate(pairs)]
    for load in loads:
        load.start()

    barrier = pltpu.get_barrier_semaphore()
    for s in range(1, n):
        pl.semaphore_signal(barrier, inc=1, device_id={"lon": lax.rem(me + s, n)}, device_id_type=MESH)
    pl.semaphore_signal(barrier, inc=1, device_id={"lat": other}, device_id_type=MESH)

    acc[...] = jnp.zeros_like(acc)
    loads[0].wait()
    saved = saved_ref[...].reshape(cells, channels)
    s_t[...] = saved.T.reshape(n, own, cells)
    loads[1].wait()
    weight = halves(weight_ref[...])
    hidden = dot3(halves(saved), weight, ((1,), (0,)))
    pl.semaphore_wait(barrier, n)

    def to_peer(src, dst, slot):
        return pltpu.make_async_remote_copy(
            src_ref=src, dst_ref=dst, send_sem=lat_send.at[slot], recv_sem=lat_recv.at[slot],
            device_id={"lat": other}, device_id_type=MESH,
        )

    saved_copy = to_peer(s_t, s_t_peer, 0)
    saved_copy.start()

    loads[2].wait()
    pre_grad = cot_ref[...].reshape(cells, channels) * gelu_slope(hidden)
    turned = pre_grad.T
    pg_t[...] = turned.reshape(2, half, cells)
    pg_copy = to_peer(pg_t.at[other], pg_t_peer, 1)
    pg_copy.start()

    cell[...] = dot3(weight, halves(turned), ((1,), (0,))).reshape(n, own, cells)

    def across(s):
        dest = lax.rem(me + s, n)
        return pltpu.make_async_remote_copy(
            src_ref=cell.at[dest], dst_ref=arrived.at[me], send_sem=a2a_send.at[s - 1], recv_sem=a2a_recv.at[s - 1],
            device_id={"lon": dest}, device_id_type=MESH,
        )

    moves = [across(s) for s in range(1, n)]
    for move in moves:
        move.start()

    def slot_of(stage, j):
        return n - (n >> stage) + j // (2 << stage)

    def hand_on(j):
        stage = zeros_below(j)
        slot = slot_of(stage, j)
        return pltpu.make_async_remote_copy(
            src_ref=part.at[j], dst_ref=landed.at[slot], send_sem=gw_send.at[slot], recv_sem=gw_recv.at[slot],
            device_id={"lon": flipped(me, 1 << stage, n)}, device_id_type=MESH,
        )

    order = sorted(range(n), key=lambda j: -int(format(j, "b").zfill(bits)[::-1], 2))
    sends = {j: hand_on(j) for j in range(1, n)}
    saved_copy.wait_recv()
    pg_copy.wait_recv()
    columns = halves(jnp.concatenate([pg_t[lat], pg_t_peer[...]], axis=1))
    for members in (order[: n // 2], order[n // 2 :]):
        owners = [flipped(me, j, n) for j in members]
        own_cells = jnp.concatenate([s_t[k] for k in owners], axis=0)
        peer_cells = jnp.concatenate([s_t_peer[k] for k in owners], axis=0)
        product = dot3(halves(jnp.concatenate([own_cells, peer_cells], axis=1)), columns, ((1,), (1,)))
        for at, j in enumerate(members):
            block = product[at * own : (at + 1) * own]
            for i in range(full):
                part[j, i * own : (i + 1) * own] = block[:, i * LANES : (i + 1) * LANES]
            if tail:
                rest = block[:, full * LANES :]
                part[j, full * own :] = jnp.concatenate([rest[: own // 2], rest[own // 2 :]], axis=1)
            if j % 2:
                sends[j].start()

    def gather(j):
        total = part[j]
        for stage in range(bits if j == 0 else zeros_below(j)):
            came = j + (1 << stage)
            sends[came].wait_recv()
            total = total + landed[slot_of(stage, j)]
        return total

    later = [j for j in order if j % 2 == 0 and j]
    first = [j for j in later if j % 4]
    rest = [j for j in later if not j % 4]
    for j in first:
        part[j] = gather(j)
        sends[j].start()

    arrived[me] = cell[me]
    for move in moves:
        move.wait_recv()
    for source in range(n):
        grid_ref[:, source * cols : (source + 1) * cols, :] = arrived[source].T.reshape(rows, cols, own)

    halo_copy = pltpu.make_async_remote_copy(
        src_ref=grid_ref.at[pl.ds((rows - REACH) * other, REACH)], dst_ref=halo,
        send_sem=lat_send.at[2], recv_sem=lat_recv.at[2],
        device_id={"lat": other}, device_id_type=MESH,
    )
    halo_copy.start()

    for j in rest:
        part[j] = gather(j)
        sends[j].start()

    def scatter(values, row, local):
        step = jnp.full(values.shape, step_ref[row], jnp.int32)
        reach = reach_ref[row]
        up = values
        down = values
        bit = 1
        while bit <= MOST_STEP:
            chosen = (step & bit) != 0
            up = jnp.where(chosen, jnp.roll(up, bit, axis=0), up)
            down = jnp.where(chosen, jnp.roll(down, -bit, axis=0), down)
            bit *= 2
        rolled = (down, values, up)
        for offset in range(-REACH, REACH + 1):
            live = jnp.where(abs(offset) <= reach, 1.0, 0.0).astype(jnp.float32)
            summed = None
            for side in range(3):
                term = coefs_ref[3 * (offset + REACH) + side, pl.ds(row, 1), :] * live * rolled[side]
                summed = term if summed is None else summed + term
            acc[local + offset + 2 * REACH] += summed

    for load in loads[3:]:
        load.wait()

    @pl.loop(0, rows, unroll=2)
    def _(i):
        scatter(grid_ref[i], lat * rows + i, i)

    halo_copy.wait_recv()

    @pl.loop(0, REACH)
    def _(i):
        local = rows * other - REACH * lat + i
        scatter(halo[i], lat * rows + local, local)

    acc_out[...] = acc[2 * REACH : 2 * REACH + rows]
    total = gather(0) * (1.0 / math.sqrt(2 * rows * all_lon))
    for i in range(full):
        gw_out[:, i * LANES : (i + 1) * LANES] = total[i * own : (i + 1) * own]
    if tail:
        packed = total[full * own :]
        gw_out[: own // 2, full * LANES :] = packed[:, :tail]
        gw_out[own // 2 :, full * LANES :] = packed[:, tail:]

    saved_copy.wait_send()
    pg_copy.wait_send()
    halo_copy.wait_send()
    for move in moves:
        move.wait_send()
    for j in range(1, n):
        sends[j].wait_send()


def write_out(acc_in, grad_in, acc_out, grad_out, sem):
    copies = [
        pltpu.make_async_copy(acc_in, acc_out, sem.at[0]),
        pltpu.make_async_copy(grad_in, grad_out, sem.at[1]),
    ]
    for copy in copies:
        copy.start()
    for copy in copies:
        copy.wait()


def kernel_body(saved, cotangent, weight, coefs, lon_step, row_reach):
    rows, cols, channels = saved.shape
    n = lax.axis_size("lon")
    own = channels // n
    half = channels // 2
    cells = rows * cols
    f32 = jnp.float32
    vmem = pl.BlockSpec(memory_space=pltpu.VMEM)
    anywhere = pl.BlockSpec(memory_space=pl.ANY)
    packed_rows = own * half // LANES
    acc, grad = pl.pallas_call(
        functools.partial(kernel, n),
        out_shape=(
            pltpu.VMEM((rows, n * cols, own), f32),
            pltpu.VMEM((own, half), f32),
        ),
        in_specs=[anywhere] * 6,
        out_specs=(vmem, vmem),
        scratch_shapes=[
            pltpu.SMEM(lon_step.shape, lon_step.dtype),
            pltpu.SMEM(row_reach.shape, row_reach.dtype),
            pltpu.VMEM(saved.shape, f32),
            pltpu.VMEM(cotangent.shape, f32),
            pltpu.VMEM(weight.shape, f32),
            pltpu.VMEM(coefs.shape, f32),
            pltpu.SemaphoreType.DMA((6,)),
            pltpu.VMEM((n, own, cells), f32),
            pltpu.VMEM((n, own, cells), f32),
            pltpu.VMEM((2, half, cells), f32),
            pltpu.VMEM((half, cells), f32),
            pltpu.VMEM((n, own, cells), f32),
            pltpu.VMEM((n, own, cells), f32),
            pltpu.VMEM((n, packed_rows, LANES), f32),
            pltpu.VMEM((n - 1, packed_rows, LANES), f32),
            pltpu.VMEM((rows, n * cols, own), f32),
            pltpu.VMEM((REACH, n * cols, own), f32),
            pltpu.VMEM((rows + 4 * REACH, n * cols, own), f32),
            pltpu.SemaphoreType.DMA((3,)),
            pltpu.SemaphoreType.DMA((3,)),
            pltpu.SemaphoreType.DMA((n - 1,)),
            pltpu.SemaphoreType.DMA((n - 1,)),
            pltpu.SemaphoreType.DMA((n - 1,)),
            pltpu.SemaphoreType.DMA((n - 1,)),
        ],
        compiler_params=pltpu.CompilerParams(
            collective_id=0, has_side_effects=True, vmem_limit_bytes=40 * 1024 * 1024
        ),
    )(*[
        pltpu.with_memory_space_constraint(x, pltpu.HBM)
        for x in (lon_step, row_reach, saved, cotangent, weight, coefs)
    ])
    acc, grad = pl.pallas_call(
        write_out,
        out_shape=(jax.ShapeDtypeStruct(acc.shape, f32), jax.ShapeDtypeStruct(grad.shape, f32)),
        in_specs=[anywhere] * 2,
        out_specs=(anywhere,) * 2,
        scratch_shapes=[pltpu.SemaphoreType.DMA((2,))],
    )(acc, grad)
    return jnp.transpose(acc, (2, 0, 1)), grad


def with_halo(x, sides, width):
    for axis, dim in sides:
        peers, length = (lax.axis_size(axis), x.shape[dim])
        up = [(i, (i + 1) % peers) for i in range(peers - 1)]
        down = [(j, i) for i, j in up]
        last = lax.slice_in_dim(x, length - width, length, axis=dim)
        initial = lax.slice_in_dim(x, 0, width, axis=dim)
        before = lax.ppermute(last, axis, up)
        after = lax.ppermute(initial, axis, down)
        x = jnp.concatenate([before, x, after], axis=dim)
    return x


def shift_rows(gradient, shifts, direction):
    width = gradient.shape[2]
    if direction == 0:
        return gradient
    wrapped = jnp.concatenate([gradient[:, :, width - 8 :], gradient, gradient[:, :, :8]], axis=2)
    result = gradient
    for amount in range(1, 9):
        begin = 8 - direction * amount
        piece = wrapped[:, :, begin : begin + width]
        result = jnp.where((shifts == amount)[None, :, None], piece, result)
    return result


def tap_term(rolled, coefs, row_reach, offset):
    summed = jnp.zeros_like(rolled[0])
    for lon_side in range(3):
        tap_index = (offset + 4) * 3 + lon_side
        summed = summed + jnp.transpose(coefs[tap_index])[:, :, None] * rolled[lon_side]
    live_rows = (abs(offset) <= row_reach).astype(jnp.float32)
    return summed * live_rows[None, :, None]


def collective_body(saved, cotangent, weight, coefs, lon_step, row_reach):
    lat_rows, lon_cols, channels = saved.shape
    lon_devices = lax.axis_size("lon")
    lat_devices = lax.axis_size("lat")
    own_channels = channels // lon_devices
    all_lon = lon_devices * lon_cols
    flat_rows = saved.reshape(lat_rows * lon_cols, channels)
    hidden = jnp.dot(
        flat_rows, weight, precision=lax.Precision.HIGHEST, preferred_element_type=jnp.float32
    )
    pre_grad = cotangent.reshape(lat_rows * lon_cols, channels) * gelu_slope(hidden)
    scale_factor = 1.0 / math.sqrt(lat_rows * lat_devices * all_lon)
    cell_grad = lax.dot_general(
        weight,
        pre_grad,
        (((1,), (1,)), ((), ())),
        precision=lax.Precision.HIGHEST,
        preferred_element_type=jnp.float32,
    )
    moved = lax.all_to_all(cell_grad, "lon", split_axis=0, concat_axis=1, tiled=True)
    gradient = (
        moved.reshape(own_channels, lon_devices, lat_rows, lon_cols)
        .transpose(0, 2, 1, 3)
        .reshape(own_channels, lat_rows, all_lon)
    )
    own_block = lax.psum_scatter(
        lax.dot_general(
            flat_rows,
            pre_grad,
            (((0,), (0,)), ((), ())),
            precision=lax.Precision.HIGHEST,
            preferred_element_type=jnp.float32,
        ),
        "lon",
        scatter_dimension=0,
        tiled=True,
    )
    grad_weight = lax.psum_scatter(own_block, "lat", scatter_dimension=1, tiled=True) * scale_factor
    row_start = lax.axis_index("lat") * lat_rows
    extended = with_halo(gradient, (("lat", 1),), 4)
    steps_padded = jnp.pad(lon_step, 4, constant_values=1)
    reach_padded = jnp.pad(row_reach, 4)
    coefs_padded = jnp.pad(coefs, ((0, 0), (4, 4), (0, 0)))
    wide_steps = lax.dynamic_slice_in_dim(steps_padded, row_start, lat_rows + 8)
    wide_reach = lax.dynamic_slice_in_dim(reach_padded, row_start, lat_rows + 8)
    wide_coefs = lax.dynamic_slice_in_dim(coefs_padded, row_start, lat_rows + 8, 1)
    rolled = [shift_rows(extended, wide_steps, lon_side) for lon_side in (-1, 0, 1)]
    result = jnp.zeros((own_channels, lat_rows, all_lon), jnp.float32)
    for offset in range(-4, 5):
        tap_sum = tap_term(rolled, wide_coefs, wide_reach, offset)
        result = result + tap_sum[:, 4 - offset : 4 - offset + lat_rows]
    return (result, grad_weight)


def body(saved, cotangent, weight, coefs, lon_step, row_reach):
    rows, cols, channels = saved.shape
    n = lax.axis_size("lon")
    fits = (
        lax.axis_size("lat") == 2
        and 4 <= n <= 16
        and n & (n - 1) == 0
        and channels % (16 * n) == 0
        and channels % LANES == 0
        and (rows * cols) % 128 == 0
        and rows >= REACH
        and n * cols >= MOST_STEP
    )
    run = kernel_body if fits else collective_body
    return run(saved, cotangent, weight, coefs, lon_step, row_reach)


def solution(mesh):
    placed = (
        P(("member", "lat"), "lon", None),
        P(("member", "lat"), "lon", None),
        P(),
        P(None, None, "lon"),
        P(),
        P(),
    )
    return jax.shard_map(
        body,
        mesh=mesh,
        in_specs=placed,
        out_specs=(P("lon", ("member", "lat"), None), P(("member", "lon"), "lat")),
        check_vma=False,
    )
```

```python
import functools
import math

import jax
import jax.numpy as jnp
from jax import lax
from jax.experimental import pallas as pl
from jax.experimental.pallas import tpu as pltpu
from jax.sharding import PartitionSpec as P

MESH = pl.DeviceIdType.MESH
REACH = 4
MOST_STEP = 8
LANES = 128


def gelu_slope(values):
    cumulative = 0.5 * (1.0 + lax.erf(values * (1.0 / math.sqrt(2.0))))
    density = jnp.exp(-0.5 * values * values) * (1.0 / math.sqrt(2.0 * math.pi))
    return cumulative + values * density


def halves(x):
    high = x.astype(jnp.bfloat16)
    low = (x - high.astype(jnp.float32)).astype(jnp.bfloat16)
    return high, low


def dot3(a, b, dims):
    (ah, al), (bh, bl) = a, b
    dot = lambda p, q: lax.dot_general(p, q, (dims, ((), ())), preferred_element_type=jnp.float32)
    return dot(ah, bh) + (dot(ah, bl) + dot(al, bh))


def flipped(me, j, n):
    result = 0
    bit = 1
    while bit < n:
        mine = lax.rem(lax.div(me, bit), 2)
        result = result + bit * ((1 - mine) if j & bit else mine)
        bit *= 2
    return result


def zeros_below(j):
    return (j & -j).bit_length() - 1


def kernel(
    n,
    step_in, reach_in, saved_in, cot_in, weight_in, coefs_in,
    acc_out, gw_out,
    step_ref, reach_ref, saved_ref, cot_ref, weight_ref, coefs_ref, load_sem,
    hid_half, cot_half, s_t, s_t_peer, pg_t, pg_t_peer, cell, arrived, part, landed, grid_ref, halo, acc,
    lat_send, lat_recv, a2a_send, a2a_recv, gw_send, gw_recv,
):
    me = lax.axis_index("lon")
    lat = lax.axis_index("lat")
    other = 1 - lat
    rows, cols, channels = saved_ref.shape
    cells = rows * cols
    own = channels // n
    half = channels // 2
    all_lon = n * cols
    bits = n.bit_length() - 1
    full, tail = divmod(half, LANES)

    pairs = (
        (saved_in, saved_ref), (weight_in, weight_ref), (cot_in, cot_ref),
        (coefs_in, coefs_ref), (step_in, step_ref), (reach_in, reach_ref),
    )
    loads = [pltpu.make_async_copy(src, dst, load_sem.at[i]) for i, (src, dst) in enumerate(pairs)]
    for load in loads:
        load.start()

    barrier = pltpu.get_barrier_semaphore()
    for s in range(1, n):
        pl.semaphore_signal(barrier, inc=1, device_id={"lon": lax.rem(me + s, n)}, device_id_type=MESH)
    pl.semaphore_signal(barrier, inc=1, device_id={"lat": other}, device_id_type=MESH)

    acc[...] = jnp.zeros_like(acc)
    loads[0].wait()
    saved = saved_ref[...].reshape(cells, channels)
    s_t[...] = saved.T.reshape(n, own, cells)
    loads[1].wait()
    weight = halves(weight_ref[...])
    hidden = dot3(halves(saved), weight, ((1,), (0,)))
    pl.semaphore_wait(barrier, n)

    def to_peer(src, dst, slot):
        return pltpu.make_async_remote_copy(
            src_ref=src, dst_ref=dst, send_sem=lat_send.at[slot], recv_sem=lat_recv.at[slot],
            device_id={"lat": other}, device_id_type=MESH,
        )

    saved_copy = to_peer(s_t, s_t_peer, 0)
    saved_copy.start()

    loads[2].wait()
    cot = cot_ref[...].reshape(cells, channels)
    for side in range(2):
        hid_half[side] = hidden[:, side * half : (side + 1) * half]
        cot_half[side] = cot[:, side * half : (side + 1) * half]
    pg_copy = to_peer(pg_t.at[other], pg_t_peer, 1)
    pg_t[other] = (cot_half[other] * gelu_slope(hid_half[other])).T
    pg_copy.start()
    pg_t[lat] = (cot_half[lat] * gelu_slope(hid_half[lat])).T

    def slot_of(stage, j):
        return n - (n >> stage) + j // (2 << stage)

    def hand_on(j):
        stage = zeros_below(j)
        slot = slot_of(stage, j)
        return pltpu.make_async_remote_copy(
            src_ref=part.at[j], dst_ref=landed.at[slot], send_sem=gw_send.at[slot], recv_sem=gw_recv.at[slot],
            device_id={"lon": flipped(me, 1 << stage, n)}, device_id_type=MESH,
        )

    order = sorted(range(n), key=lambda j: -int(format(j, "b").zfill(bits)[::-1], 2))
    sends = {j: hand_on(j) for j in range(1, n)}
    saved_copy.wait_recv()
    pg_copy.wait_recv()
    columns = halves(jnp.concatenate([pg_t[lat], pg_t_peer[...]], axis=1))

    def multiply(members):
        owners = [flipped(me, j, n) for j in members]
        own_cells = jnp.concatenate([s_t[k] for k in owners], axis=0)
        peer_cells = jnp.concatenate([s_t_peer[k] for k in owners], axis=0)
        product = dot3(halves(jnp.concatenate([own_cells, peer_cells], axis=1)), columns, ((1,), (1,)))
        for at, j in enumerate(members):
            block = product[at * own : (at + 1) * own]
            for i in range(full):
                part[j, i * own : (i + 1) * own] = block[:, i * LANES : (i + 1) * LANES]
            if tail:
                rest = block[:, full * LANES :]
                part[j, full * own :] = jnp.concatenate([rest[: own // 2], rest[own // 2 :]], axis=1)

    odd = order[: n // 2]
    multiply(odd)
    sends[odd[0]].start()

    turned = halves(pg_t[...].reshape(channels, cells))
    cell[...] = dot3(weight, turned, ((1,), (0,))).reshape(n, own, cells)

    def across(s):
        dest = lax.rem(me + s, n)
        return pltpu.make_async_remote_copy(
            src_ref=cell.at[dest], dst_ref=arrived.at[me], send_sem=a2a_send.at[s - 1], recv_sem=a2a_recv.at[s - 1],
            device_id={"lon": dest}, device_id_type=MESH,
        )

    moves = [across(s) for s in range(1, n)]
    for move in moves:
        move.start()
    for j in odd[1:]:
        sends[j].start()
    multiply(order[n // 2 :])

    def gather(j):
        total = part[j]
        for stage in range(bits if j == 0 else zeros_below(j)):
            came = j + (1 << stage)
            sends[came].wait_recv()
            total = total + landed[slot_of(stage, j)]
        return total

    later = [j for j in order if j % 2 == 0 and j]
    first = [j for j in later if j % 4]
    rest = [j for j in later if not j % 4]
    for j in first:
        part[j] = gather(j)
        sends[j].start()

    arrived[me] = cell[me]
    for move in moves:
        move.wait_recv()
    for source in range(n):
        grid_ref[:, source * cols : (source + 1) * cols, :] = arrived[source].T.reshape(rows, cols, own)

    halo_copy = pltpu.make_async_remote_copy(
        src_ref=grid_ref.at[pl.ds((rows - REACH) * other, REACH)], dst_ref=halo,
        send_sem=lat_send.at[2], recv_sem=lat_recv.at[2],
        device_id={"lat": other}, device_id_type=MESH,
    )
    halo_copy.start()

    for j in rest:
        part[j] = gather(j)
        sends[j].start()

    def scatter(values, row, local):
        step = jnp.full(values.shape, step_ref[row], jnp.int32)
        reach = reach_ref[row]
        up = values
        down = values
        bit = 1
        while bit <= MOST_STEP:
            chosen = (step & bit) != 0
            up = jnp.where(chosen, jnp.roll(up, bit, axis=0), up)
            down = jnp.where(chosen, jnp.roll(down, -bit, axis=0), down)
            bit *= 2
        rolled = (down, values, up)
        for offset in range(-REACH, REACH + 1):
            live = jnp.where(abs(offset) <= reach, 1.0, 0.0).astype(jnp.float32)
            summed = None
            for side in range(3):
                term = coefs_ref[3 * (offset + REACH) + side, pl.ds(row, 1), :] * live * rolled[side]
                summed = term if summed is None else summed + term
            acc[local + offset + 2 * REACH] += summed

    for load in loads[3:]:
        load.wait()

    @pl.loop(0, rows, unroll=2)
    def _(i):
        scatter(grid_ref[i], lat * rows + i, i)

    halo_copy.wait_recv()

    @pl.loop(0, REACH)
    def _(i):
        local = rows * other - REACH * lat + i
        scatter(halo[i], lat * rows + local, local)

    acc_out[...] = acc[2 * REACH : 2 * REACH + rows]
    total = gather(0) * (1.0 / math.sqrt(2 * rows * all_lon))
    for i in range(full):
        gw_out[:, i * LANES : (i + 1) * LANES] = total[i * own : (i + 1) * own]
    if tail:
        packed = total[full * own :]
        gw_out[: own // 2, full * LANES :] = packed[:, :tail]
        gw_out[own // 2 :, full * LANES :] = packed[:, tail:]

    saved_copy.wait_send()
    pg_copy.wait_send()
    halo_copy.wait_send()
    for move in moves:
        move.wait_send()
    for j in range(1, n):
        sends[j].wait_send()


def write_out(acc_in, grad_in, acc_out, grad_out, sem):
    copies = [
        pltpu.make_async_copy(acc_in, acc_out, sem.at[0]),
        pltpu.make_async_copy(grad_in, grad_out, sem.at[1]),
    ]
    for copy in copies:
        copy.start()
    for copy in copies:
        copy.wait()


def kernel_body(saved, cotangent, weight, coefs, lon_step, row_reach):
    rows, cols, channels = saved.shape
    n = lax.axis_size("lon")
    own = channels // n
    half = channels // 2
    cells = rows * cols
    f32 = jnp.float32
    vmem = pl.BlockSpec(memory_space=pltpu.VMEM)
    anywhere = pl.BlockSpec(memory_space=pl.ANY)
    packed_rows = own * half // LANES
    acc, grad = pl.pallas_call(
        functools.partial(kernel, n),
        out_shape=(
            pltpu.VMEM((rows, n * cols, own), f32),
            pltpu.VMEM((own, half), f32),
        ),
        in_specs=[anywhere] * 6,
        out_specs=(vmem, vmem),
        scratch_shapes=[
            pltpu.SMEM(lon_step.shape, lon_step.dtype),
            pltpu.SMEM(row_reach.shape, row_reach.dtype),
            pltpu.VMEM(saved.shape, f32),
            pltpu.VMEM(cotangent.shape, f32),
            pltpu.VMEM(weight.shape, f32),
            pltpu.VMEM(coefs.shape, f32),
            pltpu.SemaphoreType.DMA((6,)),
            pltpu.VMEM((2, cells, half), f32),
            pltpu.VMEM((2, cells, half), f32),
            pltpu.VMEM((n, own, cells), f32),
            pltpu.VMEM((n, own, cells), f32),
            pltpu.VMEM((2, half, cells), f32),
            pltpu.VMEM((half, cells), f32),
            pltpu.VMEM((n, own, cells), f32),
            pltpu.VMEM((n, own, cells), f32),
            pltpu.VMEM((n, packed_rows, LANES), f32),
            pltpu.VMEM((n - 1, packed_rows, LANES), f32),
            pltpu.VMEM((rows, n * cols, own), f32),
            pltpu.VMEM((REACH, n * cols, own), f32),
            pltpu.VMEM((rows + 4 * REACH, n * cols, own), f32),
            pltpu.SemaphoreType.DMA((3,)),
            pltpu.SemaphoreType.DMA((3,)),
            pltpu.SemaphoreType.DMA((n - 1,)),
            pltpu.SemaphoreType.DMA((n - 1,)),
            pltpu.SemaphoreType.DMA((n - 1,)),
            pltpu.SemaphoreType.DMA((n - 1,)),
        ],
        compiler_params=pltpu.CompilerParams(
            collective_id=0, has_side_effects=True, vmem_limit_bytes=40 * 1024 * 1024
        ),
    )(*[
        pltpu.with_memory_space_constraint(x, pltpu.HBM)
        for x in (lon_step, row_reach, saved, cotangent, weight, coefs)
    ])
    acc, grad = pl.pallas_call(
        write_out,
        out_shape=(jax.ShapeDtypeStruct(acc.shape, f32), jax.ShapeDtypeStruct(grad.shape, f32)),
        in_specs=[vmem] * 2,
        out_specs=(anywhere,) * 2,
        scratch_shapes=[pltpu.SemaphoreType.DMA((2,))],
    )(acc, grad)
    return jnp.transpose(acc, (2, 0, 1)), grad


def with_halo(x, sides, width):
    for axis, dim in sides:
        peers, length = (lax.axis_size(axis), x.shape[dim])
        up = [(i, (i + 1) % peers) for i in range(peers - 1)]
        down = [(j, i) for i, j in up]
        last = lax.slice_in_dim(x, length - width, length, axis=dim)
        initial = lax.slice_in_dim(x, 0, width, axis=dim)
        before = lax.ppermute(last, axis, up)
        after = lax.ppermute(initial, axis, down)
        x = jnp.concatenate([before, x, after], axis=dim)
    return x


def shift_rows(gradient, shifts, direction):
    width = gradient.shape[2]
    if direction == 0:
        return gradient
    wrapped = jnp.concatenate([gradient[:, :, width - 8 :], gradient, gradient[:, :, :8]], axis=2)
    result = gradient
    for amount in range(1, 9):
        begin = 8 - direction * amount
        piece = wrapped[:, :, begin : begin + width]
        result = jnp.where((shifts == amount)[None, :, None], piece, result)
    return result


def tap_term(rolled, coefs, row_reach, offset):
    summed = jnp.zeros_like(rolled[0])
    for lon_side in range(3):
        tap_index = (offset + 4) * 3 + lon_side
        summed = summed + jnp.transpose(coefs[tap_index])[:, :, None] * rolled[lon_side]
    live_rows = (abs(offset) <= row_reach).astype(jnp.float32)
    return summed * live_rows[None, :, None]


def collective_body(saved, cotangent, weight, coefs, lon_step, row_reach):
    lat_rows, lon_cols, channels = saved.shape
    lon_devices = lax.axis_size("lon")
    lat_devices = lax.axis_size("lat")
    own_channels = channels // lon_devices
    all_lon = lon_devices * lon_cols
    flat_rows = saved.reshape(lat_rows * lon_cols, channels)
    hidden = jnp.dot(
        flat_rows, weight, precision=lax.Precision.HIGHEST, preferred_element_type=jnp.float32
    )
    pre_grad = cotangent.reshape(lat_rows * lon_cols, channels) * gelu_slope(hidden)
    scale_factor = 1.0 / math.sqrt(lat_rows * lat_devices * all_lon)
    cell_grad = lax.dot_general(
        weight,
        pre_grad,
        (((1,), (1,)), ((), ())),
        precision=lax.Precision.HIGHEST,
        preferred_element_type=jnp.float32,
    )
    moved = lax.all_to_all(cell_grad, "lon", split_axis=0, concat_axis=1, tiled=True)
    gradient = (
        moved.reshape(own_channels, lon_devices, lat_rows, lon_cols)
        .transpose(0, 2, 1, 3)
        .reshape(own_channels, lat_rows, all_lon)
    )
    own_block = lax.psum_scatter(
        lax.dot_general(
            flat_rows,
            pre_grad,
            (((0,), (0,)), ((), ())),
            precision=lax.Precision.HIGHEST,
            preferred_element_type=jnp.float32,
        ),
        "lon",
        scatter_dimension=0,
        tiled=True,
    )
    grad_weight = lax.psum_scatter(own_block, "lat", scatter_dimension=1, tiled=True) * scale_factor
    row_start = lax.axis_index("lat") * lat_rows
    extended = with_halo(gradient, (("lat", 1),), 4)
    steps_padded = jnp.pad(lon_step, 4, constant_values=1)
    reach_padded = jnp.pad(row_reach, 4)
    coefs_padded = jnp.pad(coefs, ((0, 0), (4, 4), (0, 0)))
    wide_steps = lax.dynamic_slice_in_dim(steps_padded, row_start, lat_rows + 8)
    wide_reach = lax.dynamic_slice_in_dim(reach_padded, row_start, lat_rows + 8)
    wide_coefs = lax.dynamic_slice_in_dim(coefs_padded, row_start, lat_rows + 8, 1)
    rolled = [shift_rows(extended, wide_steps, lon_side) for lon_side in (-1, 0, 1)]
    result = jnp.zeros((own_channels, lat_rows, all_lon), jnp.float32)
    for offset in range(-4, 5):
        tap_sum = tap_term(rolled, wide_coefs, wide_reach, offset)
        result = result + tap_sum[:, 4 - offset : 4 - offset + lat_rows]
    return (result, grad_weight)


def body(saved, cotangent, weight, coefs, lon_step, row_reach):
    rows, cols, channels = saved.shape
    n = lax.axis_size("lon")
    fits = (
        lax.axis_size("lat") == 2
        and 4 <= n <= 16
        and n & (n - 1) == 0
        and channels % (16 * n) == 0
        and channels % LANES == 0
        and (rows * cols) % 128 == 0
        and rows >= REACH
        and n * cols >= MOST_STEP
    )
    run = kernel_body if fits else collective_body
    return run(saved, cotangent, weight, coefs, lon_step, row_reach)


def solution(mesh):
    placed = (
        P(("member", "lat"), "lon", None),
        P(("member", "lat"), "lon", None),
        P(),
        P(None, None, "lon"),
        P(),
        P(),
    )
    return jax.shard_map(
        body,
        mesh=mesh,
        in_specs=placed,
        out_specs=(P("lon", ("member", "lat"), None), P(("member", "lon"), "lat")),
        check_vma=False,
    )
```

```python
import functools
import math

import jax
import jax.numpy as jnp
from jax import lax
from jax.experimental import pallas as pl
from jax.experimental.pallas import tpu as pltpu
from jax.sharding import PartitionSpec as P

MESH = pl.DeviceIdType.MESH
REACH = 4
MOST_STEP = 8
WEIGHT_PARTS = 4
SUBLANES = 8
LANES = 128


def gelu_slope(values):
    cumulative = 0.5 * (1.0 + lax.erf(values * (1.0 / math.sqrt(2.0))))
    density = jnp.exp(-0.5 * values * values) * (1.0 / math.sqrt(2.0 * math.pi))
    return cumulative + values * density


def halves(x):
    high = x.astype(jnp.bfloat16)
    low = (x - high.astype(jnp.float32)).astype(jnp.bfloat16)
    return high, low


def dot3(a, b, dims):
    (ah, al), (bh, bl) = a, b
    dot = lambda p, q: lax.dot_general(p, q, (dims, ((), ())), preferred_element_type=jnp.float32)
    return dot(ah, bh) + (dot(ah, bl) + dot(al, bh))


def flipped(me, j, n):
    result = 0
    bit = 1
    while bit < n:
        mine = lax.rem(lax.div(me, bit), 2)
        result = result + bit * ((1 - mine) if j & bit else mine)
        bit *= 2
    return result


def zeros_below(j):
    return (j & -j).bit_length() - 1


def kernel(
    n,
    step_in, reach_in, saved_in, cot_in, weight_in, coefs_in,
    acc_out, gw_out,
    step_ref, reach_ref, saved_ref, cot_ref, weight_ref, coefs_ref, load_sem,
    s_t, s_t_peer, pg_t, pg_t_peer, cell, arrived, part, landed, grid_ref, halo, taps, rolled,
    lat_send, lat_recv, a2a_send, a2a_recv, gw_send, gw_recv,
):
    me = lax.axis_index("lon")
    lat = lax.axis_index("lat")
    other = 1 - lat
    rows, cols, channels = saved_ref.shape
    cells = rows * cols
    own = channels // n
    half = channels // 2
    all_lon = n * cols
    bits = n.bit_length() - 1
    full, tail = divmod(half, LANES)

    slab = channels // WEIGHT_PARTS
    pairs = [(saved_in, saved_ref)]
    pairs += [(weight_in.at[pl.ds(i * slab, slab)], weight_ref.at[pl.ds(i * slab, slab)]) for i in range(WEIGHT_PARTS)]
    pairs += [(cot_in, cot_ref), (coefs_in, coefs_ref), (step_in, step_ref), (reach_in, reach_ref)]
    loads = [pltpu.make_async_copy(src, dst, load_sem.at[i]) for i, (src, dst) in enumerate(pairs)]
    late = WEIGHT_PARTS + 2
    for load in loads[:late]:
        load.start()

    barrier = pltpu.get_barrier_semaphore()
    for s in range(1, n):
        pl.semaphore_signal(barrier, inc=1, device_id={"lon": lax.rem(me + s, n)}, device_id_type=MESH)
    pl.semaphore_signal(barrier, inc=1, device_id={"lat": other}, device_id_type=MESH)

    loads[0].wait()
    saved = saved_ref[...].reshape(cells, channels)
    s_t[...] = saved.T.reshape(n, own, cells)
    for load in loads[1 : 1 + WEIGHT_PARTS]:
        load.wait()
    for load in loads[late:]:
        load.start()
    weight = halves(weight_ref[...])
    hidden = dot3(halves(saved), weight, ((1,), (0,)))
    pl.semaphore_wait(barrier, n)

    def to_peer(src, dst, slot):
        return pltpu.make_async_remote_copy(
            src_ref=src, dst_ref=dst, send_sem=lat_send.at[slot], recv_sem=lat_recv.at[slot],
            device_id={"lat": other}, device_id_type=MESH,
        )

    saved_copy = to_peer(s_t, s_t_peer, 0)
    saved_copy.start()

    loads[1 + WEIGHT_PARTS].wait()
    pre_grad = cot_ref[...].reshape(cells, channels) * gelu_slope(hidden)
    turned = pre_grad.T
    pg_t[...] = turned.reshape(2, half, cells)
    pg_copy = to_peer(pg_t.at[other], pg_t_peer, 1)
    pg_copy.start()

    cell[...] = dot3(weight, halves(turned), ((1,), (0,))).reshape(n, own, cells)

    def across(s):
        dest = lax.rem(me + s, n)
        return pltpu.make_async_remote_copy(
            src_ref=cell.at[dest], dst_ref=arrived.at[me], send_sem=a2a_send.at[s - 1], recv_sem=a2a_recv.at[s - 1],
            device_id={"lon": dest}, device_id_type=MESH,
        )

    moves = [across(s) for s in range(1, n)]
    for move in moves:
        move.start()

    def slot_of(stage, j):
        return n - (n >> stage) + j // (2 << stage)

    def hand_on(j):
        stage = zeros_below(j)
        slot = slot_of(stage, j)
        return pltpu.make_async_remote_copy(
            src_ref=part.at[j], dst_ref=landed.at[slot], send_sem=gw_send.at[slot], recv_sem=gw_recv.at[slot],
            device_id={"lon": flipped(me, 1 << stage, n)}, device_id_type=MESH,
        )

    order = sorted(range(n), key=lambda j: -int(format(j, "b").zfill(bits)[::-1], 2))
    sends = {j: hand_on(j) for j in range(1, n)}
    saved_copy.wait_recv()
    pg_copy.wait_recv()
    columns = halves(jnp.concatenate([pg_t[lat], pg_t_peer[...]], axis=1))
    for members in (order[: n // 2], order[n // 2 :]):
        owners = [flipped(me, j, n) for j in members]
        own_cells = jnp.concatenate([s_t[k] for k in owners], axis=0)
        peer_cells = jnp.concatenate([s_t_peer[k] for k in owners], axis=0)
        product = dot3(halves(jnp.concatenate([own_cells, peer_cells], axis=1)), columns, ((1,), (1,)))
        for at, j in enumerate(members):
            block = product[at * own : (at + 1) * own]
            for i in range(full):
                part[j, i * own : (i + 1) * own] = block[:, i * LANES : (i + 1) * LANES]
            if tail:
                rest = block[:, full * LANES :]
                part[j, full * own :] = jnp.concatenate([rest[: own // 2], rest[own // 2 :]], axis=1)
            if j % 2:
                sends[j].start()

    def gather(j):
        total = part[j]
        for stage in range(bits if j == 0 else zeros_below(j)):
            came = j + (1 << stage)
            sends[came].wait_recv()
            total = total + landed[slot_of(stage, j)]
        return total

    for load in loads[late:]:
        load.wait()

    def taps_of(place):
        row = lat * rows + place - REACH
        for tap in range(3 * (2 * REACH + 1)):
            live = jnp.where(abs(tap // 3 - REACH) <= reach_ref[row], 1.0, 0.0).astype(jnp.float32)
            taps[place, tap] = jnp.broadcast_to(coefs_ref[tap, pl.ds(row, 1), :] * live, (SUBLANES, own))

    beyond = (rows + REACH) * lat
    halo_at = (rows + REACH) * other

    @pl.loop(0, REACH)
    def _(i):
        taps[beyond + i] = jnp.zeros(taps.shape[1:], jnp.float32)
        rolled[beyond + i] = jnp.zeros(rolled.shape[1:], jnp.float32)
        taps_of(halo_at + i)

    @pl.loop(0, rows)
    def _(i):
        taps_of(REACH + i)

    later = [j for j in order if j % 2 == 0 and j]
    first = [j for j in later if j % 4]
    rest = [j for j in later if not j % 4]
    for j in first:
        part[j] = gather(j)
        sends[j].start()

    arrived[me] = cell[me]
    for move in moves:
        move.wait_recv()
    for source in range(n):
        grid_ref[:, source * cols : (source + 1) * cols, :] = arrived[source].T.reshape(rows, cols, own)

    halo_copy = pltpu.make_async_remote_copy(
        src_ref=grid_ref.at[pl.ds((rows - REACH) * other, REACH)], dst_ref=halo,
        send_sem=lat_send.at[2], recv_sem=lat_recv.at[2],
        device_id={"lat": other}, device_id_type=MESH,
    )
    halo_copy.start()

    for j in rest:
        part[j] = gather(j)
        sends[j].start()

    def roll_row(values, place):
        step = jnp.full(values.shape, step_ref[lat * rows + place - REACH], jnp.int32)
        up = values
        down = values
        bit = 1
        while bit <= MOST_STEP:
            chosen = (step & bit) != 0
            up = jnp.where(chosen, jnp.roll(up, bit, axis=0), up)
            down = jnp.where(chosen, jnp.roll(down, -bit, axis=0), down)
            bit *= 2
        rolled[place, 0] = down
        rolled[place, 1] = values
        rolled[place, 2] = up

    def sum_rows(group):
        base = group * REACH
        sums = [None] * REACH
        for away in range(3 * REACH):
            sources = [rolled[base + away, side].reshape(all_lon // SUBLANES, SUBLANES, own) for side in range(3)]
            for q in range(REACH):
                offset = q + REACH - away
                if abs(offset) > REACH:
                    continue
                for side in range(3):
                    term = taps[base + away, 3 * (offset + REACH) + side][None] * sources[side]
                    sums[q] = term if sums[q] is None else sums[q] + term
        for q in range(REACH):
            acc_out[base + q] = sums[q].reshape(all_lon, own)

    @pl.loop(0, rows, unroll=2)
    def _(i):
        roll_row(grid_ref[i], REACH + i)

    groups = rows // REACH

    @pl.loop(0, groups - 1)
    def _(i):
        sum_rows(lax.rem(i + lat, groups))

    halo_copy.wait_recv()

    @pl.loop(0, REACH)
    def _(i):
        roll_row(halo[i], halo_at + i)

    sum_rows(lax.rem(groups - 1 + lat, groups))

    total = gather(0) * (1.0 / math.sqrt(2 * rows * all_lon))
    for i in range(full):
        gw_out[:, i * LANES : (i + 1) * LANES] = total[i * own : (i + 1) * own]
    if tail:
        packed = total[full * own :]
        gw_out[: own // 2, full * LANES :] = packed[:, :tail]
        gw_out[own // 2 :, full * LANES :] = packed[:, tail:]

    saved_copy.wait_send()
    pg_copy.wait_send()
    halo_copy.wait_send()
    for move in moves:
        move.wait_send()
    for j in range(1, n):
        sends[j].wait_send()


def kernel_body(saved, cotangent, weight, coefs, lon_step, row_reach):
    rows, cols, channels = saved.shape
    n = lax.axis_size("lon")
    own = channels // n
    half = channels // 2
    cells = rows * cols
    f32 = jnp.float32
    vmem = pl.BlockSpec(memory_space=pltpu.VMEM)
    anywhere = pl.BlockSpec(memory_space=pl.ANY)
    packed_rows = own * half // LANES
    acc, grad = pl.pallas_call(
        functools.partial(kernel, n),
        out_shape=(
            pltpu.VMEM((rows, n * cols, own), f32),
            pltpu.VMEM((own, half), f32),
        ),
        in_specs=[anywhere] * 6,
        out_specs=(vmem, vmem),
        scratch_shapes=[
            pltpu.SMEM(lon_step.shape, lon_step.dtype),
            pltpu.SMEM(row_reach.shape, row_reach.dtype),
            pltpu.VMEM(saved.shape, f32),
            pltpu.VMEM(cotangent.shape, f32),
            pltpu.VMEM(weight.shape, f32),
            pltpu.VMEM(coefs.shape, f32),
            pltpu.SemaphoreType.DMA((WEIGHT_PARTS + 5,)),
            pltpu.VMEM((n, own, cells), f32),
            pltpu.VMEM((n, own, cells), f32),
            pltpu.VMEM((2, half, cells), f32),
            pltpu.VMEM((half, cells), f32),
            pltpu.VMEM((n, own, cells), f32),
            pltpu.VMEM((n, own, cells), f32),
            pltpu.VMEM((n, packed_rows, LANES), f32),
            pltpu.VMEM((n - 1, packed_rows, LANES), f32),
            pltpu.VMEM((rows, n * cols, own), f32),
            pltpu.VMEM((REACH, n * cols, own), f32),
            pltpu.VMEM((rows + 2 * REACH, coefs.shape[0], SUBLANES, own), f32),
            pltpu.VMEM((rows + 2 * REACH, 3, n * cols, own), f32),
            pltpu.SemaphoreType.DMA((3,)),
            pltpu.SemaphoreType.DMA((3,)),
            pltpu.SemaphoreType.DMA((n - 1,)),
            pltpu.SemaphoreType.DMA((n - 1,)),
            pltpu.SemaphoreType.DMA((n - 1,)),
            pltpu.SemaphoreType.DMA((n - 1,)),
        ],
        compiler_params=pltpu.CompilerParams(
            collective_id=0, has_side_effects=True, vmem_limit_bytes=40 * 1024 * 1024
        ),
    )(*[
        pltpu.with_memory_space_constraint(x, pltpu.HBM)
        for x in (lon_step, row_reach, saved, cotangent, weight, coefs)
    ])
    return jnp.transpose(acc, (2, 0, 1)), grad


def with_halo(x, sides, width):
    for axis, dim in sides:
        peers, length = (lax.axis_size(axis), x.shape[dim])
        up = [(i, (i + 1) % peers) for i in range(peers - 1)]
        down = [(j, i) for i, j in up]
        last = lax.slice_in_dim(x, length - width, length, axis=dim)
        initial = lax.slice_in_dim(x, 0, width, axis=dim)
        before = lax.ppermute(last, axis, up)
        after = lax.ppermute(initial, axis, down)
        x = jnp.concatenate([before, x, after], axis=dim)
    return x


def shift_rows(gradient, shifts, direction):
    width = gradient.shape[2]
    if direction == 0:
        return gradient
    wrapped = jnp.concatenate([gradient[:, :, width - 8 :], gradient, gradient[:, :, :8]], axis=2)
    result = gradient
    for amount in range(1, 9):
        begin = 8 - direction * amount
        piece = wrapped[:, :, begin : begin + width]
        result = jnp.where((shifts == amount)[None, :, None], piece, result)
    return result


def tap_term(rolled, coefs, row_reach, offset):
    summed = jnp.zeros_like(rolled[0])
    for lon_side in range(3):
        tap_index = (offset + 4) * 3 + lon_side
        summed = summed + jnp.transpose(coefs[tap_index])[:, :, None] * rolled[lon_side]
    live_rows = (abs(offset) <= row_reach).astype(jnp.float32)
    return summed * live_rows[None, :, None]


def collective_body(saved, cotangent, weight, coefs, lon_step, row_reach):
    lat_rows, lon_cols, channels = saved.shape
    lon_devices = lax.axis_size("lon")
    lat_devices = lax.axis_size("lat")
    own_channels = channels // lon_devices
    all_lon = lon_devices * lon_cols
    flat_rows = saved.reshape(lat_rows * lon_cols, channels)
    hidden = jnp.dot(
        flat_rows, weight, precision=lax.Precision.HIGHEST, preferred_element_type=jnp.float32
    )
    pre_grad = cotangent.reshape(lat_rows * lon_cols, channels) * gelu_slope(hidden)
    scale_factor = 1.0 / math.sqrt(lat_rows * lat_devices * all_lon)
    cell_grad = lax.dot_general(
        weight,
        pre_grad,
        (((1,), (1,)), ((), ())),
        precision=lax.Precision.HIGHEST,
        preferred_element_type=jnp.float32,
    )
    moved = lax.all_to_all(cell_grad, "lon", split_axis=0, concat_axis=1, tiled=True)
    gradient = (
        moved.reshape(own_channels, lon_devices, lat_rows, lon_cols)
        .transpose(0, 2, 1, 3)
        .reshape(own_channels, lat_rows, all_lon)
    )
    own_block = lax.psum_scatter(
        lax.dot_general(
            flat_rows,
            pre_grad,
            (((0,), (0,)), ((), ())),
            precision=lax.Precision.HIGHEST,
            preferred_element_type=jnp.float32,
        ),
        "lon",
        scatter_dimension=0,
        tiled=True,
    )
    grad_weight = lax.psum_scatter(own_block, "lat", scatter_dimension=1, tiled=True) * scale_factor
    row_start = lax.axis_index("lat") * lat_rows
    extended = with_halo(gradient, (("lat", 1),), 4)
    steps_padded = jnp.pad(lon_step, 4, constant_values=1)
    reach_padded = jnp.pad(row_reach, 4)
    coefs_padded = jnp.pad(coefs, ((0, 0), (4, 4), (0, 0)))
    wide_steps = lax.dynamic_slice_in_dim(steps_padded, row_start, lat_rows + 8)
    wide_reach = lax.dynamic_slice_in_dim(reach_padded, row_start, lat_rows + 8)
    wide_coefs = lax.dynamic_slice_in_dim(coefs_padded, row_start, lat_rows + 8, 1)
    rolled = [shift_rows(extended, wide_steps, lon_side) for lon_side in (-1, 0, 1)]
    result = jnp.zeros((own_channels, lat_rows, all_lon), jnp.float32)
    for offset in range(-4, 5):
        tap_sum = tap_term(rolled, wide_coefs, wide_reach, offset)
        result = result + tap_sum[:, 4 - offset : 4 - offset + lat_rows]
    return (result, grad_weight)


def body(saved, cotangent, weight, coefs, lon_step, row_reach):
    rows, cols, channels = saved.shape
    n = lax.axis_size("lon")
    fits = (
        lax.axis_size("lat") == 2
        and 4 <= n <= 16
        and n & (n - 1) == 0
        and channels % (16 * n) == 0
        and channels % LANES == 0
        and (rows * cols) % 128 == 0
        and rows % REACH == 0
        and rows >= 2 * REACH
        and n * cols % SUBLANES == 0
        and n * cols >= 2 * MOST_STEP
        and channels % (SUBLANES * WEIGHT_PARTS) == 0
    )
    run = kernel_body if fits else collective_body
    return run(saved, cotangent, weight, coefs, lon_step, row_reach)


def solution(mesh):
    placed = (
        P(("member", "lat"), "lon", None),
        P(("member", "lat"), "lon", None),
        P(),
        P(None, None, "lon"),
        P(),
        P(),
    )
    return jax.shard_map(
        body,
        mesh=mesh,
        in_specs=placed,
        out_specs=(P("lon", ("member", "lat"), None), P(("member", "lon"), "lat")),
        check_vma=False,
    )
```

```python
import functools
import math

import jax
import jax.numpy as jnp
from jax import lax
from jax.experimental import pallas as pl
from jax.experimental.pallas import tpu as pltpu
from jax.sharding import PartitionSpec as P

MESH = pl.DeviceIdType.MESH
REACH = 4
MOST_STEP = 8
WEIGHT_PARTS = 4
SUBLANES = 8
LANES = 128


def gelu_slope(values):
    cumulative = 0.5 * (1.0 + lax.erf(values * (1.0 / math.sqrt(2.0))))
    density = jnp.exp(-0.5 * values * values) * (1.0 / math.sqrt(2.0 * math.pi))
    return cumulative + values * density


def halves(x):
    high = x.astype(jnp.bfloat16)
    low = (x - high.astype(jnp.float32)).astype(jnp.bfloat16)
    return high, low


def dot3(a, b, dims):
    (ah, al), (bh, bl) = a, b
    dot = lambda p, q: lax.dot_general(p, q, (dims, ((), ())), preferred_element_type=jnp.float32)
    return dot(ah, bh) + (dot(ah, bl) + dot(al, bh))


def flipped(me, j, n):
    result = 0
    bit = 1
    while bit < n:
        mine = lax.rem(lax.div(me, bit), 2)
        result = result + bit * ((1 - mine) if j & bit else mine)
        bit *= 2
    return result


def zeros_below(j):
    return (j & -j).bit_length() - 1


def kernel(
    n,
    step_in, reach_in, saved_in, cot_in, weight_in, coefs_in,
    acc_out, gw_out,
    step_ref, reach_ref, saved_ref, cot_ref, weight_ref, coefs_ref, load_sem,
    s_t, s_t_peer, pg_t, pg_t_peer, cell, arrived, part, landed, grid_ref, halo, taps, rolled,
    lat_send, lat_recv, a2a_send, a2a_recv, gw_send, gw_recv,
):
    me = lax.axis_index("lon")
    lat = lax.axis_index("lat")
    other = 1 - lat
    rows, cols, channels = saved_ref.shape
    cells = rows * cols
    own = channels // n
    half = channels // 2
    all_lon = n * cols
    bits = n.bit_length() - 1
    full, tail = divmod(half, LANES)

    slab = channels // WEIGHT_PARTS
    pairs = [(saved_in, saved_ref)]
    pairs += [(weight_in.at[pl.ds(i * slab, slab)], weight_ref.at[pl.ds(i * slab, slab)]) for i in range(WEIGHT_PARTS)]
    pairs += [(cot_in, cot_ref), (coefs_in, coefs_ref), (step_in, step_ref), (reach_in, reach_ref)]
    loads = [pltpu.make_async_copy(src, dst, load_sem.at[i]) for i, (src, dst) in enumerate(pairs)]
    late = WEIGHT_PARTS + 2
    for load in loads[:late]:
        load.start()

    barrier = pltpu.get_barrier_semaphore()
    for s in range(1, n):
        pl.semaphore_signal(barrier, inc=1, device_id={"lon": lax.rem(me + s, n)}, device_id_type=MESH)
    pl.semaphore_signal(barrier, inc=1, device_id={"lat": other}, device_id_type=MESH)

    loads[0].wait()
    saved = saved_ref[...].reshape(cells, channels)
    s_t[...] = saved.T.reshape(n, own, cells)
    for load in loads[1 : 1 + WEIGHT_PARTS]:
        load.wait()
    for load in loads[late:]:
        load.start()
    weight = halves(weight_ref[...])
    hidden = dot3(halves(saved), weight, ((1,), (0,)))
    pl.semaphore_wait(barrier, n)

    def to_peer(src, dst, slot):
        return pltpu.make_async_remote_copy(
            src_ref=src, dst_ref=dst, send_sem=lat_send.at[slot], recv_sem=lat_recv.at[slot],
            device_id={"lat": other}, device_id_type=MESH,
        )

    saved_copy = to_peer(s_t, s_t_peer, 0)
    saved_copy.start()

    loads[1 + WEIGHT_PARTS].wait()
    pre_grad = cot_ref[...].reshape(cells, channels) * gelu_slope(hidden)
    turned = pre_grad.T
    pg_t[...] = turned.reshape(2, half, cells)
    pg_copy = to_peer(pg_t.at[other], pg_t_peer, 1)
    pg_copy.start()

    cell[...] = dot3(weight, halves(turned), ((1,), (0,))).reshape(n, own, cells)

    def across(s):
        dest = lax.rem(me + s, n)
        return pltpu.make_async_remote_copy(
            src_ref=cell.at[dest], dst_ref=arrived.at[me], send_sem=a2a_send.at[s - 1], recv_sem=a2a_recv.at[s - 1],
            device_id={"lon": dest}, device_id_type=MESH,
        )

    moves = [across(s) for s in range(1, n)]
    for move in moves:
        move.start()

    def slot_of(stage, j):
        return n - (n >> stage) + j // (2 << stage)

    def hand_on(j):
        stage = zeros_below(j)
        slot = slot_of(stage, j)
        return pltpu.make_async_remote_copy(
            src_ref=part.at[j], dst_ref=landed.at[slot], send_sem=gw_send.at[slot], recv_sem=gw_recv.at[slot],
            device_id={"lon": flipped(me, 1 << stage, n)}, device_id_type=MESH,
        )

    order = sorted(range(n), key=lambda j: -int(format(j, "b").zfill(bits)[::-1], 2))
    sends = {j: hand_on(j) for j in range(1, n)}
    saved_copy.wait_recv()
    pg_copy.wait_recv()
    columns = halves(jnp.concatenate([pg_t[lat], pg_t_peer[...]], axis=1))
    for members in (order[: n // 2], order[n // 2 :]):
        owners = [flipped(me, j, n) for j in members]
        own_cells = jnp.concatenate([s_t[k] for k in owners], axis=0)
        peer_cells = jnp.concatenate([s_t_peer[k] for k in owners], axis=0)
        product = dot3(halves(jnp.concatenate([own_cells, peer_cells], axis=1)), columns, ((1,), (1,)))
        for at, j in enumerate(members):
            block = product[at * own : (at + 1) * own]
            for i in range(full):
                part[j, i * own : (i + 1) * own] = block[:, i * LANES : (i + 1) * LANES]
            if tail:
                rest = block[:, full * LANES :]
                part[j, full * own :] = jnp.concatenate([rest[: own // 2], rest[own // 2 :]], axis=1)
            if j % 2:
                sends[j].start()

    def gather(j):
        total = part[j]
        for stage in range(bits if j == 0 else zeros_below(j)):
            came = j + (1 << stage)
            sends[came].wait_recv()
            total = total + landed[slot_of(stage, j)]
        return total

    for load in loads[late:]:
        load.wait()

    def taps_of(place):
        row = lat * rows + place - REACH
        for tap in range(3 * (2 * REACH + 1)):
            live = jnp.where(abs(tap // 3 - REACH) <= reach_ref[row], 1.0, 0.0).astype(jnp.float32)
            taps[place, tap] = jnp.broadcast_to(coefs_ref[tap, pl.ds(row, 1), :] * live, (SUBLANES, own))

    beyond = (rows + REACH) * lat
    halo_at = (rows + REACH) * other

    @pl.loop(0, REACH)
    def _(i):
        taps[beyond + i] = jnp.zeros(taps.shape[1:], jnp.float32)
        rolled[beyond + i] = jnp.zeros(rolled.shape[1:], jnp.float32)
        taps_of(halo_at + i)

    @pl.loop(0, rows)
    def _(i):
        taps_of(REACH + i)

    for j in order[n // 2 : -1]:
        part[j] = gather(j)
        sends[j].start()

    arrived[me] = cell[me]
    for move in moves:
        move.wait_recv()
    for source in range(n):
        grid_ref[:, source * cols : (source + 1) * cols, :] = arrived[source].T.reshape(rows, cols, own)

    halo_copy = pltpu.make_async_remote_copy(
        src_ref=grid_ref.at[pl.ds((rows - REACH) * other, REACH)], dst_ref=halo,
        send_sem=lat_send.at[2], recv_sem=lat_recv.at[2],
        device_id={"lat": other}, device_id_type=MESH,
    )
    halo_copy.start()

    def roll_row(values, place):
        step = jnp.full(values.shape, step_ref[lat * rows + place - REACH], jnp.int32)
        up = values
        down = values
        bit = 1
        while bit <= MOST_STEP:
            chosen = (step & bit) != 0
            up = jnp.where(chosen, jnp.roll(up, bit, axis=0), up)
            down = jnp.where(chosen, jnp.roll(down, -bit, axis=0), down)
            bit *= 2
        rolled[place, 0] = down
        rolled[place, 1] = values
        rolled[place, 2] = up

    def sum_rows(group):
        base = group * REACH
        sums = [None] * REACH
        for away in range(3 * REACH):
            sources = [rolled[base + away, side].reshape(all_lon // SUBLANES, SUBLANES, own) for side in range(3)]
            for q in range(REACH):
                offset = q + REACH - away
                if abs(offset) > REACH:
                    continue
                for side in range(3):
                    term = taps[base + away, 3 * (offset + REACH) + side][None] * sources[side]
                    sums[q] = term if sums[q] is None else sums[q] + term
        for q in range(REACH):
            acc_out[base + q] = sums[q].reshape(all_lon, own)

    @pl.loop(0, rows, unroll=2)
    def _(i):
        roll_row(grid_ref[i], REACH + i)

    groups = rows // REACH

    @pl.loop(0, groups - 1)
    def _(i):
        sum_rows(lax.rem(i + lat, groups))

    halo_copy.wait_recv()

    @pl.loop(0, REACH)
    def _(i):
        roll_row(halo[i], halo_at + i)

    sum_rows(lax.rem(groups - 1 + lat, groups))

    total = gather(0) * (1.0 / math.sqrt(2 * rows * all_lon))
    for i in range(full):
        gw_out[:, i * LANES : (i + 1) * LANES] = total[i * own : (i + 1) * own]
    if tail:
        packed = total[full * own :]
        gw_out[: own // 2, full * LANES :] = packed[:, :tail]
        gw_out[own // 2 :, full * LANES :] = packed[:, tail:]

    saved_copy.wait_send()
    pg_copy.wait_send()
    halo_copy.wait_send()
    for move in moves:
        move.wait_send()
    for j in range(1, n):
        sends[j].wait_send()


def kernel_body(saved, cotangent, weight, coefs, lon_step, row_reach):
    rows, cols, channels = saved.shape
    n = lax.axis_size("lon")
    own = channels // n
    half = channels // 2
    cells = rows * cols
    f32 = jnp.float32
    vmem = pl.BlockSpec(memory_space=pltpu.VMEM)
    anywhere = pl.BlockSpec(memory_space=pl.ANY)
    packed_rows = own * half // LANES
    acc, grad = pl.pallas_call(
        functools.partial(kernel, n),
        out_shape=(
            pltpu.VMEM((rows, n * cols, own), f32),
            pltpu.VMEM((own, half), f32),
        ),
        in_specs=[anywhere] * 6,
        out_specs=(vmem, vmem),
        scratch_shapes=[
            pltpu.SMEM(lon_step.shape, lon_step.dtype),
            pltpu.SMEM(row_reach.shape, row_reach.dtype),
            pltpu.VMEM(saved.shape, f32),
            pltpu.VMEM(cotangent.shape, f32),
            pltpu.VMEM(weight.shape, f32),
            pltpu.VMEM(coefs.shape, f32),
            pltpu.SemaphoreType.DMA((WEIGHT_PARTS + 5,)),
            pltpu.VMEM((n, own, cells), f32),
            pltpu.VMEM((n, own, cells), f32),
            pltpu.VMEM((2, half, cells), f32),
            pltpu.VMEM((half, cells), f32),
            pltpu.VMEM((n, own, cells), f32),
            pltpu.VMEM((n, own, cells), f32),
            pltpu.VMEM((n, packed_rows, LANES), f32),
            pltpu.VMEM((n - 1, packed_rows, LANES), f32),
            pltpu.VMEM((rows, n * cols, own), f32),
            pltpu.VMEM((REACH, n * cols, own), f32),
            pltpu.VMEM((rows + 2 * REACH, coefs.shape[0], SUBLANES, own), f32),
            pltpu.VMEM((rows + 2 * REACH, 3, n * cols, own), f32),
            pltpu.SemaphoreType.DMA((3,)),
            pltpu.SemaphoreType.DMA((3,)),
            pltpu.SemaphoreType.DMA((n - 1,)),
            pltpu.SemaphoreType.DMA((n - 1,)),
            pltpu.SemaphoreType.DMA((n - 1,)),
            pltpu.SemaphoreType.DMA((n - 1,)),
        ],
        compiler_params=pltpu.CompilerParams(
            collective_id=0, has_side_effects=True, vmem_limit_bytes=40 * 1024 * 1024
        ),
    )(*[
        pltpu.with_memory_space_constraint(x, pltpu.HBM)
        for x in (lon_step, row_reach, saved, cotangent, weight, coefs)
    ])
    return jnp.transpose(acc, (2, 0, 1)), grad


def with_halo(x, sides, width):
    for axis, dim in sides:
        peers, length = (lax.axis_size(axis), x.shape[dim])
        up = [(i, (i + 1) % peers) for i in range(peers - 1)]
        down = [(j, i) for i, j in up]
        last = lax.slice_in_dim(x, length - width, length, axis=dim)
        initial = lax.slice_in_dim(x, 0, width, axis=dim)
        before = lax.ppermute(last, axis, up)
        after = lax.ppermute(initial, axis, down)
        x = jnp.concatenate([before, x, after], axis=dim)
    return x


def shift_rows(gradient, shifts, direction):
    width = gradient.shape[2]
    if direction == 0:
        return gradient
    wrapped = jnp.concatenate([gradient[:, :, width - 8 :], gradient, gradient[:, :, :8]], axis=2)
    result = gradient
    for amount in range(1, 9):
        begin = 8 - direction * amount
        piece = wrapped[:, :, begin : begin + width]
        result = jnp.where((shifts == amount)[None, :, None], piece, result)
    return result


def tap_term(rolled, coefs, row_reach, offset):
    summed = jnp.zeros_like(rolled[0])
    for lon_side in range(3):
        tap_index = (offset + 4) * 3 + lon_side
        summed = summed + jnp.transpose(coefs[tap_index])[:, :, None] * rolled[lon_side]
    live_rows = (abs(offset) <= row_reach).astype(jnp.float32)
    return summed * live_rows[None, :, None]


def collective_body(saved, cotangent, weight, coefs, lon_step, row_reach):
    lat_rows, lon_cols, channels = saved.shape
    lon_devices = lax.axis_size("lon")
    lat_devices = lax.axis_size("lat")
    own_channels = channels // lon_devices
    all_lon = lon_devices * lon_cols
    flat_rows = saved.reshape(lat_rows * lon_cols, channels)
    hidden = jnp.dot(
        flat_rows, weight, precision=lax.Precision.HIGHEST, preferred_element_type=jnp.float32
    )
    pre_grad = cotangent.reshape(lat_rows * lon_cols, channels) * gelu_slope(hidden)
    scale_factor = 1.0 / math.sqrt(lat_rows * lat_devices * all_lon)
    cell_grad = lax.dot_general(
        weight,
        pre_grad,
        (((1,), (1,)), ((), ())),
        precision=lax.Precision.HIGHEST,
        preferred_element_type=jnp.float32,
    )
    moved = lax.all_to_all(cell_grad, "lon", split_axis=0, concat_axis=1, tiled=True)
    gradient = (
        moved.reshape(own_channels, lon_devices, lat_rows, lon_cols)
        .transpose(0, 2, 1, 3)
        .reshape(own_channels, lat_rows, all_lon)
    )
    own_block = lax.psum_scatter(
        lax.dot_general(
            flat_rows,
            pre_grad,
            (((0,), (0,)), ((), ())),
            precision=lax.Precision.HIGHEST,
            preferred_element_type=jnp.float32,
        ),
        "lon",
        scatter_dimension=0,
        tiled=True,
    )
    grad_weight = lax.psum_scatter(own_block, "lat", scatter_dimension=1, tiled=True) * scale_factor
    row_start = lax.axis_index("lat") * lat_rows
    extended = with_halo(gradient, (("lat", 1),), 4)
    steps_padded = jnp.pad(lon_step, 4, constant_values=1)
    reach_padded = jnp.pad(row_reach, 4)
    coefs_padded = jnp.pad(coefs, ((0, 0), (4, 4), (0, 0)))
    wide_steps = lax.dynamic_slice_in_dim(steps_padded, row_start, lat_rows + 8)
    wide_reach = lax.dynamic_slice_in_dim(reach_padded, row_start, lat_rows + 8)
    wide_coefs = lax.dynamic_slice_in_dim(coefs_padded, row_start, lat_rows + 8, 1)
    rolled = [shift_rows(extended, wide_steps, lon_side) for lon_side in (-1, 0, 1)]
    result = jnp.zeros((own_channels, lat_rows, all_lon), jnp.float32)
    for offset in range(-4, 5):
        tap_sum = tap_term(rolled, wide_coefs, wide_reach, offset)
        result = result + tap_sum[:, 4 - offset : 4 - offset + lat_rows]
    return (result, grad_weight)


def body(saved, cotangent, weight, coefs, lon_step, row_reach):
    rows, cols, channels = saved.shape
    n = lax.axis_size("lon")
    fits = (
        lax.axis_size("lat") == 2
        and 4 <= n <= 16
        and n & (n - 1) == 0
        and channels % (16 * n) == 0
        and channels % LANES == 0
        and (rows * cols) % 128 == 0
        and rows % REACH == 0
        and rows >= 2 * REACH
        and n * cols % SUBLANES == 0
        and n * cols >= 2 * MOST_STEP
        and channels % (SUBLANES * WEIGHT_PARTS) == 0
    )
    run = kernel_body if fits else collective_body
    return run(saved, cotangent, weight, coefs, lon_step, row_reach)


def solution(mesh):
    placed = (
        P(("member", "lat"), "lon", None),
        P(("member", "lat"), "lon", None),
        P(),
        P(None, None, "lon"),
        P(),
        P(),
    )
    return jax.shard_map(
        body,
        mesh=mesh,
        in_specs=placed,
        out_specs=(P("lon", ("member", "lat"), None), P(("member", "lon"), "lat")),
        check_vma=False,
    )
```

```python
import functools
import math

import jax
import jax.numpy as jnp
from jax import lax
from jax.experimental import pallas as pl
from jax.experimental.pallas import tpu as pltpu
from jax.sharding import PartitionSpec as P

MESH = pl.DeviceIdType.MESH
REACH = 4
MOST_STEP = 8
WEIGHT_PARTS = 4
SUBLANES = 8
LANES = 128


def gelu_slope(values):
    cumulative = 0.5 * (1.0 + lax.erf(values * (1.0 / math.sqrt(2.0))))
    density = jnp.exp(-0.5 * values * values) * (1.0 / math.sqrt(2.0 * math.pi))
    return cumulative + values * density


def halves(x):
    high = x.astype(jnp.bfloat16)
    low = (x - high.astype(jnp.float32)).astype(jnp.bfloat16)
    return high, low


def dot3(a, b, dims):
    (ah, al), (bh, bl) = a, b
    dot = lambda p, q: lax.dot_general(p, q, (dims, ((), ())), preferred_element_type=jnp.float32)
    return dot(ah, bh) + (dot(ah, bl) + dot(al, bh))


def flipped(me, j, n):
    result = 0
    bit = 1
    while bit < n:
        mine = lax.rem(lax.div(me, bit), 2)
        result = result + bit * ((1 - mine) if j & bit else mine)
        bit *= 2
    return result


def zeros_below(j):
    return (j & -j).bit_length() - 1


def kernel(
    n,
    step_in, reach_in, saved_in, cot_in, weight_in, coefs_in,
    acc_out, gw_out,
    step_ref, reach_ref, saved_ref, cot_ref, weight_ref, coefs_ref, load_sem,
    s_t, s_t_peer, pg_t, pg_t_peer, cell, arrived, part, landed, weight_high, weight_low, slots, edge, halo, taps, rolled,
    lat_send, lat_recv, a2a_send, a2a_recv, gw_send, gw_recv,
):
    me = lax.axis_index("lon")
    lat = lax.axis_index("lat")
    other = 1 - lat
    rows, cols, channels = saved_ref.shape
    cells = rows * cols
    own = channels // n
    half = channels // 2
    all_lon = n * cols
    bits = n.bit_length() - 1
    full, tail = divmod(half, LANES)

    slab = channels // WEIGHT_PARTS
    pairs = [(saved_in, saved_ref)]
    pairs += [(weight_in.at[pl.ds(i * slab, slab)], weight_ref.at[pl.ds(i * slab, slab)]) for i in range(WEIGHT_PARTS)]
    pairs += [(cot_in, cot_ref), (coefs_in, coefs_ref), (step_in, step_ref), (reach_in, reach_ref)]
    loads = [pltpu.make_async_copy(src, dst, load_sem.at[i]) for i, (src, dst) in enumerate(pairs)]
    late = WEIGHT_PARTS + 2
    for load in loads[:late]:
        load.start()

    barrier = pltpu.get_barrier_semaphore()
    for s in range(1, n):
        pl.semaphore_signal(barrier, inc=1, device_id={"lon": lax.rem(me + s, n)}, device_id_type=MESH)
    pl.semaphore_signal(barrier, inc=1, device_id={"lat": other}, device_id_type=MESH)

    loads[0].wait()
    saved = saved_ref[...].reshape(cells, channels)
    s_t[...] = saved.T.reshape(n, own, cells)
    for load in loads[1 : 1 + WEIGHT_PARTS]:
        load.wait()
    for load in loads[late:]:
        load.start()
    weight = halves(weight_ref[...])
    weight_high[...] = weight[0].reshape(n, own, channels)
    weight_low[...] = weight[1].reshape(n, own, channels)
    hidden = dot3(halves(saved), weight, ((1,), (0,)))
    pl.semaphore_wait(barrier, n)

    def to_peer(src, dst, slot):
        return pltpu.make_async_remote_copy(
            src_ref=src, dst_ref=dst, send_sem=lat_send.at[slot], recv_sem=lat_recv.at[slot],
            device_id={"lat": other}, device_id_type=MESH,
        )

    saved_copy = to_peer(s_t, s_t_peer, 0)
    saved_copy.start()

    loads[1 + WEIGHT_PARTS].wait()
    pre_grad = cot_ref[...].reshape(cells, channels) * gelu_slope(hidden)
    turned = pre_grad.T
    pg_t[...] = turned.reshape(2, half, cells)
    pg_copy = to_peer(pg_t.at[other], pg_t_peer, 1)
    pg_copy.start()

    def across(s):
        dest = lax.rem(me + s, n)
        return pltpu.make_async_remote_copy(
            src_ref=cell.at[dest], dst_ref=arrived.at[me], send_sem=a2a_send.at[s - 1], recv_sem=a2a_recv.at[s - 1],
            device_id={"lon": dest}, device_id_type=MESH,
        )

    moves = {s: across(s) for s in range(1, n)}
    spans = list(range(n // 4, 3 * n // 4)), list(range(3 * n // 4, n)) + list(range(n // 4))
    right = halves(turned)
    for span in spans:
        owners = [lax.rem(me + s, n) for s in span]
        left = tuple(jnp.concatenate([ref[k] for k in owners], axis=0) for ref in (weight_high, weight_low))
        made = dot3(left, right, ((1,), (0,)))
        for at, s in enumerate(span):
            cell[owners[at]] = made[at * own : (at + 1) * own]
            if s:
                moves[s].start()

    def slot_of(stage, j):
        return n - (n >> stage) + j // (2 << stage)

    def hand_on(j):
        stage = zeros_below(j)
        slot = slot_of(stage, j)
        return pltpu.make_async_remote_copy(
            src_ref=part.at[j], dst_ref=landed.at[slot], send_sem=gw_send.at[slot], recv_sem=gw_recv.at[slot],
            device_id={"lon": flipped(me, 1 << stage, n)}, device_id_type=MESH,
        )

    order = sorted(range(n), key=lambda j: -int(format(j, "b").zfill(bits)[::-1], 2))
    sends = {j: hand_on(j) for j in range(1, n)}
    saved_copy.wait_recv()
    pg_copy.wait_recv()
    columns = halves(jnp.concatenate([pg_t[lat], pg_t_peer[...]], axis=1))
    for members in (order[: n // 2], order[n // 2 :]):
        owners = [flipped(me, j, n) for j in members]
        own_cells = jnp.concatenate([s_t[k] for k in owners], axis=0)
        peer_cells = jnp.concatenate([s_t_peer[k] for k in owners], axis=0)
        product = dot3(halves(jnp.concatenate([own_cells, peer_cells], axis=1)), columns, ((1,), (1,)))
        for at, j in enumerate(members):
            block = product[at * own : (at + 1) * own]
            for i in range(full):
                part[j, i * own : (i + 1) * own] = block[:, i * LANES : (i + 1) * LANES]
            if tail:
                rest = block[:, full * LANES :]
                part[j, full * own :] = jnp.concatenate([rest[: own // 2], rest[own // 2 :]], axis=1)
            if j % 2:
                sends[j].start()

    def gather(j):
        total = part[j]
        for stage in range(bits if j == 0 else zeros_below(j)):
            came = j + (1 << stage)
            sends[came].wait_recv()
            total = total + landed[slot_of(stage, j)]
        return total

    for load in loads[late:]:
        load.wait()

    def taps_of(place):
        row = lat * rows + place - REACH
        for tap in range(3 * (2 * REACH + 1)):
            live = jnp.where(abs(tap // 3 - REACH) <= reach_ref[row], 1.0, 0.0).astype(jnp.float32)
            taps[place, tap] = jnp.broadcast_to(coefs_ref[tap, pl.ds(row, 1), :] * live, (SUBLANES, own))

    beyond = (rows + REACH) * lat
    halo_at = (rows + REACH) * other

    @pl.loop(0, REACH)
    def _(i):
        taps[beyond + i] = jnp.zeros(taps.shape[1:], jnp.float32)
        rolled[beyond + i] = jnp.zeros(rolled.shape[1:], jnp.float32)
        taps_of(halo_at + i)

    @pl.loop(0, rows)
    def _(i):
        taps_of(REACH + i)

    chained = order[n // 2]
    part[chained] = gather(chained)
    sends[chained].start()

    slots[me] = cell[me].T
    for s in range(1, n):
        moves[s].wait_recv()
        source = lax.rem(me - s + n, n)
        slots[source] = arrived[source].T

    def row_pair(pair):
        at = pl.ds(pl.multiple_of(pair * SUBLANES, SUBLANES), SUBLANES)
        low = lax.broadcasted_iota(jnp.int32, (SUBLANES, own), 0) < cols
        even, odd = [], []
        for k in range(0, n, 2):
            a, b = slots[k, at, :], slots[k + 1, at, :]
            even.append(jnp.where(low, a, jnp.roll(b, cols, axis=0)))
            odd.append(jnp.where(low, jnp.roll(a, cols, axis=0), b))
        return jnp.concatenate(even, axis=0), jnp.concatenate(odd, axis=0)

    for i in range(0, REACH, 2):
        edge[i], edge[i + 1] = row_pair((rows - REACH) // 2 * other + i // 2)

    halo_copy = pltpu.make_async_remote_copy(
        src_ref=edge, dst_ref=halo, send_sem=lat_send.at[2], recv_sem=lat_recv.at[2],
        device_id={"lat": other}, device_id_type=MESH,
    )
    halo_copy.start()

    for j in order[n // 2 + 1 : -1]:
        part[j] = gather(j)
        sends[j].start()

    def roll_row(values, place):
        step = jnp.full(values.shape, step_ref[lat * rows + place - REACH], jnp.int32)
        up = values
        down = values
        bit = 1
        while bit <= MOST_STEP:
            chosen = (step & bit) != 0
            up = jnp.where(chosen, jnp.roll(up, bit, axis=0), up)
            down = jnp.where(chosen, jnp.roll(down, -bit, axis=0), down)
            bit *= 2
        rolled[place, 0] = down
        rolled[place, 1] = values
        rolled[place, 2] = up

    def sum_rows(group):
        base = group * REACH
        sums = [None] * REACH
        for away in range(3 * REACH):
            sources = [rolled[base + away, side].reshape(all_lon // SUBLANES, SUBLANES, own) for side in range(3)]
            for q in range(REACH):
                offset = q + REACH - away
                if abs(offset) > REACH:
                    continue
                for side in range(3):
                    term = taps[base + away, 3 * (offset + REACH) + side][None] * sources[side]
                    sums[q] = term if sums[q] is None else sums[q] + term
        for q in range(REACH):
            acc_out[base + q] = sums[q].reshape(all_lon, own)

    @pl.loop(0, rows // 2)
    def _(pair):
        even, odd = row_pair(pair)
        roll_row(even, REACH + 2 * pair)
        roll_row(odd, REACH + 2 * pair + 1)

    groups = rows // REACH

    @pl.loop(0, groups - 1)
    def _(i):
        sum_rows(lax.rem(i + lat, groups))

    halo_copy.wait_recv()

    @pl.loop(0, REACH)
    def _(i):
        roll_row(halo[i], halo_at + i)

    sum_rows(lax.rem(groups - 1 + lat, groups))

    total = gather(0) * (1.0 / math.sqrt(2 * rows * all_lon))
    for i in range(full):
        gw_out[:, i * LANES : (i + 1) * LANES] = total[i * own : (i + 1) * own]
    if tail:
        packed = total[full * own :]
        gw_out[: own // 2, full * LANES :] = packed[:, :tail]
        gw_out[own // 2 :, full * LANES :] = packed[:, tail:]

    saved_copy.wait_send()
    pg_copy.wait_send()
    halo_copy.wait_send()
    for s in range(1, n):
        moves[s].wait_send()
    for j in range(1, n):
        sends[j].wait_send()


def kernel_body(saved, cotangent, weight, coefs, lon_step, row_reach):
    rows, cols, channels = saved.shape
    n = lax.axis_size("lon")
    own = channels // n
    half = channels // 2
    cells = rows * cols
    f32 = jnp.float32
    vmem = pl.BlockSpec(memory_space=pltpu.VMEM)
    anywhere = pl.BlockSpec(memory_space=pl.ANY)
    packed_rows = own * half // LANES
    acc, grad = pl.pallas_call(
        functools.partial(kernel, n),
        out_shape=(
            pltpu.VMEM((rows, n * cols, own), f32),
            pltpu.VMEM((own, half), f32),
        ),
        in_specs=[anywhere] * 6,
        out_specs=(vmem, vmem),
        scratch_shapes=[
            pltpu.SMEM(lon_step.shape, lon_step.dtype),
            pltpu.SMEM(row_reach.shape, row_reach.dtype),
            pltpu.VMEM(saved.shape, f32),
            pltpu.VMEM(cotangent.shape, f32),
            pltpu.VMEM(weight.shape, f32),
            pltpu.VMEM(coefs.shape, f32),
            pltpu.SemaphoreType.DMA((WEIGHT_PARTS + 5,)),
            pltpu.VMEM((n, own, cells), f32),
            pltpu.VMEM((n, own, cells), f32),
            pltpu.VMEM((2, half, cells), f32),
            pltpu.VMEM((half, cells), f32),
            pltpu.VMEM((n, own, cells), f32),
            pltpu.VMEM((n, own, cells), f32),
            pltpu.VMEM((n, packed_rows, LANES), f32),
            pltpu.VMEM((n - 1, packed_rows, LANES), f32),
            pltpu.VMEM((n, own, channels), jnp.bfloat16),
            pltpu.VMEM((n, own, channels), jnp.bfloat16),
            pltpu.VMEM((n, cells, own), f32),
            pltpu.VMEM((REACH, n * cols, own), f32),
            pltpu.VMEM((REACH, n * cols, own), f32),
            pltpu.VMEM((rows + 2 * REACH, coefs.shape[0], SUBLANES, own), f32),
            pltpu.VMEM((rows + 2 * REACH, 3, n * cols, own), f32),
            pltpu.SemaphoreType.DMA((3,)),
            pltpu.SemaphoreType.DMA((3,)),
            pltpu.SemaphoreType.DMA((n - 1,)),
            pltpu.SemaphoreType.DMA((n - 1,)),
            pltpu.SemaphoreType.DMA((n - 1,)),
            pltpu.SemaphoreType.DMA((n - 1,)),
        ],
        compiler_params=pltpu.CompilerParams(
            collective_id=0, has_side_effects=True, vmem_limit_bytes=40 * 1024 * 1024
        ),
    )(*[
        pltpu.with_memory_space_constraint(x, pltpu.HBM)
        for x in (lon_step, row_reach, saved, cotangent, weight, coefs)
    ])
    return jnp.transpose(acc, (2, 0, 1)), grad


def with_halo(x, sides, width):
    for axis, dim in sides:
        peers, length = (lax.axis_size(axis), x.shape[dim])
        up = [(i, (i + 1) % peers) for i in range(peers - 1)]
        down = [(j, i) for i, j in up]
        last = lax.slice_in_dim(x, length - width, length, axis=dim)
        initial = lax.slice_in_dim(x, 0, width, axis=dim)
        before = lax.ppermute(last, axis, up)
        after = lax.ppermute(initial, axis, down)
        x = jnp.concatenate([before, x, after], axis=dim)
    return x


def shift_rows(gradient, shifts, direction):
    width = gradient.shape[2]
    if direction == 0:
        return gradient
    wrapped = jnp.concatenate([gradient[:, :, width - 8 :], gradient, gradient[:, :, :8]], axis=2)
    result = gradient
    for amount in range(1, 9):
        begin = 8 - direction * amount
        piece = wrapped[:, :, begin : begin + width]
        result = jnp.where((shifts == amount)[None, :, None], piece, result)
    return result


def tap_term(rolled, coefs, row_reach, offset):
    summed = jnp.zeros_like(rolled[0])
    for lon_side in range(3):
        tap_index = (offset + 4) * 3 + lon_side
        summed = summed + jnp.transpose(coefs[tap_index])[:, :, None] * rolled[lon_side]
    live_rows = (abs(offset) <= row_reach).astype(jnp.float32)
    return summed * live_rows[None, :, None]


def collective_body(saved, cotangent, weight, coefs, lon_step, row_reach):
    lat_rows, lon_cols, channels = saved.shape
    lon_devices = lax.axis_size("lon")
    lat_devices = lax.axis_size("lat")
    own_channels = channels // lon_devices
    all_lon = lon_devices * lon_cols
    flat_rows = saved.reshape(lat_rows * lon_cols, channels)
    hidden = jnp.dot(
        flat_rows, weight, precision=lax.Precision.HIGHEST, preferred_element_type=jnp.float32
    )
    pre_grad = cotangent.reshape(lat_rows * lon_cols, channels) * gelu_slope(hidden)
    scale_factor = 1.0 / math.sqrt(lat_rows * lat_devices * all_lon)
    cell_grad = lax.dot_general(
        weight,
        pre_grad,
        (((1,), (1,)), ((), ())),
        precision=lax.Precision.HIGHEST,
        preferred_element_type=jnp.float32,
    )
    moved = lax.all_to_all(cell_grad, "lon", split_axis=0, concat_axis=1, tiled=True)
    gradient = (
        moved.reshape(own_channels, lon_devices, lat_rows, lon_cols)
        .transpose(0, 2, 1, 3)
        .reshape(own_channels, lat_rows, all_lon)
    )
    own_block = lax.psum_scatter(
        lax.dot_general(
            flat_rows,
            pre_grad,
            (((0,), (0,)), ((), ())),
            precision=lax.Precision.HIGHEST,
            preferred_element_type=jnp.float32,
        ),
        "lon",
        scatter_dimension=0,
        tiled=True,
    )
    grad_weight = lax.psum_scatter(own_block, "lat", scatter_dimension=1, tiled=True) * scale_factor
    row_start = lax.axis_index("lat") * lat_rows
    extended = with_halo(gradient, (("lat", 1),), 4)
    steps_padded = jnp.pad(lon_step, 4, constant_values=1)
    reach_padded = jnp.pad(row_reach, 4)
    coefs_padded = jnp.pad(coefs, ((0, 0), (4, 4), (0, 0)))
    wide_steps = lax.dynamic_slice_in_dim(steps_padded, row_start, lat_rows + 8)
    wide_reach = lax.dynamic_slice_in_dim(reach_padded, row_start, lat_rows + 8)
    wide_coefs = lax.dynamic_slice_in_dim(coefs_padded, row_start, lat_rows + 8, 1)
    rolled = [shift_rows(extended, wide_steps, lon_side) for lon_side in (-1, 0, 1)]
    result = jnp.zeros((own_channels, lat_rows, all_lon), jnp.float32)
    for offset in range(-4, 5):
        tap_sum = tap_term(rolled, wide_coefs, wide_reach, offset)
        result = result + tap_sum[:, 4 - offset : 4 - offset + lat_rows]
    return (result, grad_weight)


def body(saved, cotangent, weight, coefs, lon_step, row_reach):
    rows, cols, channels = saved.shape
    n = lax.axis_size("lon")
    fits = (
        lax.axis_size("lat") == 2
        and 4 <= n <= 16
        and n & (n - 1) == 0
        and channels % (16 * n) == 0
        and channels % LANES == 0
        and (rows * cols) % 128 == 0
        and rows % REACH == 0
        and rows >= 2 * REACH
        and 2 * cols == SUBLANES
        and n * cols >= 2 * MOST_STEP
        and channels % (SUBLANES * WEIGHT_PARTS) == 0
    )
    run = kernel_body if fits else collective_body
    return run(saved, cotangent, weight, coefs, lon_step, row_reach)


def solution(mesh):
    placed = (
        P(("member", "lat"), "lon", None),
        P(("member", "lat"), "lon", None),
        P(),
        P(None, None, "lon"),
        P(),
        P(),
    )
    return jax.shard_map(
        body,
        mesh=mesh,
        in_specs=placed,
        out_specs=(P("lon", ("member", "lat"), None), P(("member", "lon"), "lat")),
        check_vma=False,
    )
```

```python
import functools
import math

import jax
import jax.numpy as jnp
from jax import lax
from jax.experimental import pallas as pl
from jax.experimental.pallas import tpu as pltpu
from jax.sharding import PartitionSpec as P

MESH = pl.DeviceIdType.MESH
REACH = 4
MOST_STEP = 8
WEIGHT_PARTS = 4
SUBLANES = 8
LANES = 128


def gelu_slope(values):
    cumulative = 0.5 * (1.0 + lax.erf(values * (1.0 / math.sqrt(2.0))))
    density = jnp.exp(-0.5 * values * values) * (1.0 / math.sqrt(2.0 * math.pi))
    return cumulative + values * density


def halves(x):
    high = x.astype(jnp.bfloat16)
    low = (x - high.astype(jnp.float32)).astype(jnp.bfloat16)
    return high, low


def dot3(a, b, dims):
    (ah, al), (bh, bl) = a, b
    dot = lambda p, q: lax.dot_general(p, q, (dims, ((), ())), preferred_element_type=jnp.float32)
    return dot(ah, bh) + (dot(ah, bl) + dot(al, bh))


def flipped(me, j, n):
    result = 0
    bit = 1
    while bit < n:
        mine = lax.rem(lax.div(me, bit), 2)
        result = result + bit * ((1 - mine) if j & bit else mine)
        bit *= 2
    return result


def zeros_below(j):
    return (j & -j).bit_length() - 1


def kernel(
    n,
    step_in, reach_in, saved_in, cot_in, weight_in, coefs_in,
    acc_out, gw_out,
    step_ref, reach_ref, saved_ref, cot_ref, weight_ref, coefs_ref, load_sem,
    s_t, s_t_peer, pg_t, pg_t_peer, cell, arrived, part, landed, weight_high, weight_low, slots, edge, halo, taps, rolled,
    lat_send, lat_recv, a2a_send, a2a_recv, gw_send, gw_recv,
):
    me = lax.axis_index("lon")
    lat = lax.axis_index("lat")
    other = 1 - lat
    rows, cols, channels = saved_ref.shape
    cells = rows * cols
    own = channels // n
    half = channels // 2
    all_lon = n * cols
    bits = n.bit_length() - 1
    full, tail = divmod(half, LANES)

    slab = channels // WEIGHT_PARTS
    pairs = [(saved_in, saved_ref)]
    pairs += [(weight_in.at[pl.ds(i * slab, slab)], weight_ref.at[pl.ds(i * slab, slab)]) for i in range(WEIGHT_PARTS)]
    pairs += [(cot_in, cot_ref), (coefs_in, coefs_ref), (step_in, step_ref), (reach_in, reach_ref)]
    loads = [pltpu.make_async_copy(src, dst, load_sem.at[i]) for i, (src, dst) in enumerate(pairs)]
    late = WEIGHT_PARTS + 2
    for load in loads[:late]:
        load.start()

    barrier = pltpu.get_barrier_semaphore()
    for s in range(1, n):
        pl.semaphore_signal(barrier, inc=1, device_id={"lon": lax.rem(me + s, n)}, device_id_type=MESH)
    pl.semaphore_signal(barrier, inc=1, device_id={"lat": other}, device_id_type=MESH)

    loads[0].wait()
    saved = saved_ref[...].reshape(cells, channels)
    s_t[...] = saved.T.reshape(n, own, cells)
    for load in loads[1 : 1 + WEIGHT_PARTS]:
        load.wait()
    for load in loads[late:]:
        load.start()
    weight = halves(weight_ref[...])
    weight_high[...] = weight[0].reshape(n, own, channels)
    weight_low[...] = weight[1].reshape(n, own, channels)
    hidden = dot3(halves(saved), weight, ((1,), (0,)))
    pl.semaphore_wait(barrier, n)

    def to_peer(src, dst, slot):
        return pltpu.make_async_remote_copy(
            src_ref=src, dst_ref=dst, send_sem=lat_send.at[slot], recv_sem=lat_recv.at[slot],
            device_id={"lat": other}, device_id_type=MESH,
        )

    saved_copy = to_peer(s_t, s_t_peer, 0)
    saved_copy.start()

    loads[1 + WEIGHT_PARTS].wait()
    pre_grad = cot_ref[...].reshape(cells, channels) * gelu_slope(hidden)
    turned = pre_grad.T
    pg_t[...] = turned.reshape(2, half, cells)
    pg_copy = to_peer(pg_t.at[other], pg_t_peer, 1)
    pg_copy.start()

    def across(s):
        dest = lax.rem(me + s, n)
        return pltpu.make_async_remote_copy(
            src_ref=cell.at[dest], dst_ref=arrived.at[me], send_sem=a2a_send.at[s - 1], recv_sem=a2a_recv.at[s - 1],
            device_id={"lon": dest}, device_id_type=MESH,
        )

    moves = {s: across(s) for s in range(1, n)}
    spans = list(range(n // 4, 3 * n // 4)), list(range(3 * n // 4, n)) + list(range(n // 4))
    right = halves(turned)
    for span in spans:
        owners = [lax.rem(me + s, n) for s in span]
        left = tuple(jnp.concatenate([ref[k] for k in owners], axis=0) for ref in (weight_high, weight_low))
        made = dot3(left, right, ((1,), (0,)))
        for at, s in enumerate(span):
            cell[owners[at]] = made[at * own : (at + 1) * own]
            if s:
                moves[s].start()

    def slot_of(stage, j):
        return n - (n >> stage) + j // (2 << stage)

    def hand_on(j):
        stage = zeros_below(j)
        slot = slot_of(stage, j)
        return pltpu.make_async_remote_copy(
            src_ref=part.at[j], dst_ref=landed.at[slot], send_sem=gw_send.at[slot], recv_sem=gw_recv.at[slot],
            device_id={"lon": flipped(me, 1 << stage, n)}, device_id_type=MESH,
        )

    order = sorted(range(n), key=lambda j: -int(format(j, "b").zfill(bits)[::-1], 2))
    sends = {j: hand_on(j) for j in range(1, n)}
    saved_copy.wait_recv()
    pg_copy.wait_recv()
    columns = halves(jnp.concatenate([pg_t[lat], pg_t_peer[...]], axis=1))
    for members in (order[: n // 2], order[n // 2 :]):
        owners = [flipped(me, j, n) for j in members]
        own_cells = jnp.concatenate([s_t[k] for k in owners], axis=0)
        peer_cells = jnp.concatenate([s_t_peer[k] for k in owners], axis=0)
        product = dot3(halves(jnp.concatenate([own_cells, peer_cells], axis=1)), columns, ((1,), (1,)))
        for at, j in enumerate(members):
            block = product[at * own : (at + 1) * own]
            for i in range(full):
                part[j, i * own : (i + 1) * own] = block[:, i * LANES : (i + 1) * LANES]
            if tail:
                rest = block[:, full * LANES :]
                part[j, full * own :] = jnp.concatenate([rest[: own // 2], rest[own // 2 :]], axis=1)
            if at == 0 and j % 2:
                sends[j].start()

    def gather(j):
        total = part[j]
        for stage in range(bits if j == 0 else zeros_below(j)):
            came = j + (1 << stage)
            sends[came].wait_recv()
            total = total + landed[slot_of(stage, j)]
        return total

    for load in loads[late:]:
        load.wait()

    def taps_of(place):
        row = lat * rows + place - REACH
        for tap in range(3 * (2 * REACH + 1)):
            live = jnp.where(abs(tap // 3 - REACH) <= reach_ref[row], 1.0, 0.0).astype(jnp.float32)
            taps[place, tap] = jnp.broadcast_to(coefs_ref[tap, pl.ds(row, 1), :] * live, (SUBLANES, own))

    beyond = (rows + REACH) * lat
    halo_at = (rows + REACH) * other

    @pl.loop(0, REACH)
    def _(i):
        taps[beyond + i] = jnp.zeros(taps.shape[1:], jnp.float32)
        rolled[beyond + i] = jnp.zeros(rolled.shape[1:], jnp.float32)
        taps_of(halo_at + i)

    @pl.loop(0, rows)
    def _(i):
        taps_of(REACH + i)

    for before, odd, even in zip(order, order[1 : n // 2], order[n // 2 : -1]):
        sends[before].wait_send()
        sends[odd].start()
        part[even] = gather(even)
        sends[even].start()

    slots[me] = cell[me].T
    for s in range(1, n):
        moves[s].wait_recv()
        source = lax.rem(me - s + n, n)
        slots[source] = arrived[source].T

    def row_pair(pair):
        at = pl.ds(pl.multiple_of(pair * SUBLANES, SUBLANES), SUBLANES)
        low = lax.broadcasted_iota(jnp.int32, (SUBLANES, own), 0) < cols
        even, odd = [], []
        for k in range(0, n, 2):
            a, b = slots[k, at, :], slots[k + 1, at, :]
            even.append(jnp.where(low, a, jnp.roll(b, cols, axis=0)))
            odd.append(jnp.where(low, jnp.roll(a, cols, axis=0), b))
        return jnp.concatenate(even, axis=0), jnp.concatenate(odd, axis=0)

    for i in range(0, REACH, 2):
        edge[i], edge[i + 1] = row_pair((rows - REACH) // 2 * other + i // 2)

    halo_copy = pltpu.make_async_remote_copy(
        src_ref=edge, dst_ref=halo, send_sem=lat_send.at[2], recv_sem=lat_recv.at[2],
        device_id={"lat": other}, device_id_type=MESH,
    )
    halo_copy.start()

    def roll_row(values, place):
        step = jnp.full(values.shape, step_ref[lat * rows + place - REACH], jnp.int32)
        up = values
        down = values
        bit = 1
        while bit <= MOST_STEP:
            chosen = (step & bit) != 0
            up = jnp.where(chosen, jnp.roll(up, bit, axis=0), up)
            down = jnp.where(chosen, jnp.roll(down, -bit, axis=0), down)
            bit *= 2
        rolled[place, 0] = down
        rolled[place, 1] = values
        rolled[place, 2] = up

    def sum_rows(group):
        base = group * REACH
        sums = [None] * REACH
        for away in range(3 * REACH):
            sources = [rolled[base + away, side].reshape(all_lon // SUBLANES, SUBLANES, own) for side in range(3)]
            for q in range(REACH):
                offset = q + REACH - away
                if abs(offset) > REACH:
                    continue
                for side in range(3):
                    term = taps[base + away, 3 * (offset + REACH) + side][None] * sources[side]
                    sums[q] = term if sums[q] is None else sums[q] + term
        for q in range(REACH):
            acc_out[base + q] = sums[q].reshape(all_lon, own)

    @pl.loop(0, rows // 2)
    def _(pair):
        even, odd = row_pair(pair)
        roll_row(even, REACH + 2 * pair)
        roll_row(odd, REACH + 2 * pair + 1)

    groups = rows // REACH

    @pl.loop(0, groups - 1)
    def _(i):
        sum_rows(lax.rem(i + lat, groups))

    halo_copy.wait_recv()

    @pl.loop(0, REACH)
    def _(i):
        roll_row(halo[i], halo_at + i)

    sum_rows(lax.rem(groups - 1 + lat, groups))

    total = gather(0) * (1.0 / math.sqrt(2 * rows * all_lon))
    for i in range(full):
        gw_out[:, i * LANES : (i + 1) * LANES] = total[i * own : (i + 1) * own]
    if tail:
        packed = total[full * own :]
        gw_out[: own // 2, full * LANES :] = packed[:, :tail]
        gw_out[own // 2 :, full * LANES :] = packed[:, tail:]

    saved_copy.wait_send()
    pg_copy.wait_send()
    halo_copy.wait_send()
    for s in range(1, n):
        moves[s].wait_send()
    for j in order[n // 2 - 1 : -1]:
        sends[j].wait_send()


def kernel_body(saved, cotangent, weight, coefs, lon_step, row_reach):
    rows, cols, channels = saved.shape
    n = lax.axis_size("lon")
    own = channels // n
    half = channels // 2
    cells = rows * cols
    f32 = jnp.float32
    vmem = pl.BlockSpec(memory_space=pltpu.VMEM)
    anywhere = pl.BlockSpec(memory_space=pl.ANY)
    packed_rows = own * half // LANES
    acc, grad = pl.pallas_call(
        functools.partial(kernel, n),
        out_shape=(
            pltpu.VMEM((rows, n * cols, own), f32),
            pltpu.VMEM((own, half), f32),
        ),
        in_specs=[anywhere] * 6,
        out_specs=(vmem, vmem),
        scratch_shapes=[
            pltpu.SMEM(lon_step.shape, lon_step.dtype),
            pltpu.SMEM(row_reach.shape, row_reach.dtype),
            pltpu.VMEM(saved.shape, f32),
            pltpu.VMEM(cotangent.shape, f32),
            pltpu.VMEM(weight.shape, f32),
            pltpu.VMEM(coefs.shape, f32),
            pltpu.SemaphoreType.DMA((WEIGHT_PARTS + 5,)),
            pltpu.VMEM((n, own, cells), f32),
            pltpu.VMEM((n, own, cells), f32),
            pltpu.VMEM((2, half, cells), f32),
            pltpu.VMEM((half, cells), f32),
            pltpu.VMEM((n, own, cells), f32),
            pltpu.VMEM((n, own, cells), f32),
            pltpu.VMEM((n, packed_rows, LANES), f32),
            pltpu.VMEM((n - 1, packed_rows, LANES), f32),
            pltpu.VMEM((n, own, channels), jnp.bfloat16),
            pltpu.VMEM((n, own, channels), jnp.bfloat16),
            pltpu.VMEM((n, cells, own), f32),
            pltpu.VMEM((REACH, n * cols, own), f32),
            pltpu.VMEM((REACH, n * cols, own), f32),
            pltpu.VMEM((rows + 2 * REACH, coefs.shape[0], SUBLANES, own), f32),
            pltpu.VMEM((rows + 2 * REACH, 3, n * cols, own), f32),
            pltpu.SemaphoreType.DMA((3,)),
            pltpu.SemaphoreType.DMA((3,)),
            pltpu.SemaphoreType.DMA((n - 1,)),
            pltpu.SemaphoreType.DMA((n - 1,)),
            pltpu.SemaphoreType.DMA((n - 1,)),
            pltpu.SemaphoreType.DMA((n - 1,)),
        ],
        compiler_params=pltpu.CompilerParams(
            collective_id=0, has_side_effects=True, vmem_limit_bytes=40 * 1024 * 1024
        ),
    )(*[
        pltpu.with_memory_space_constraint(x, pltpu.HBM)
        for x in (lon_step, row_reach, saved, cotangent, weight, coefs)
    ])
    return jnp.transpose(acc, (2, 0, 1)), grad


def with_halo(x, sides, width):
    for axis, dim in sides:
        peers, length = (lax.axis_size(axis), x.shape[dim])
        up = [(i, (i + 1) % peers) for i in range(peers - 1)]
        down = [(j, i) for i, j in up]
        last = lax.slice_in_dim(x, length - width, length, axis=dim)
        initial = lax.slice_in_dim(x, 0, width, axis=dim)
        before = lax.ppermute(last, axis, up)
        after = lax.ppermute(initial, axis, down)
        x = jnp.concatenate([before, x, after], axis=dim)
    return x


def shift_rows(gradient, shifts, direction):
    width = gradient.shape[2]
    if direction == 0:
        return gradient
    wrapped = jnp.concatenate([gradient[:, :, width - 8 :], gradient, gradient[:, :, :8]], axis=2)
    result = gradient
    for amount in range(1, 9):
        begin = 8 - direction * amount
        piece = wrapped[:, :, begin : begin + width]
        result = jnp.where((shifts == amount)[None, :, None], piece, result)
    return result


def tap_term(rolled, coefs, row_reach, offset):
    summed = jnp.zeros_like(rolled[0])
    for lon_side in range(3):
        tap_index = (offset + 4) * 3 + lon_side
        summed = summed + jnp.transpose(coefs[tap_index])[:, :, None] * rolled[lon_side]
    live_rows = (abs(offset) <= row_reach).astype(jnp.float32)
    return summed * live_rows[None, :, None]


def collective_body(saved, cotangent, weight, coefs, lon_step, row_reach):
    lat_rows, lon_cols, channels = saved.shape
    lon_devices = lax.axis_size("lon")
    lat_devices = lax.axis_size("lat")
    own_channels = channels // lon_devices
    all_lon = lon_devices * lon_cols
    flat_rows = saved.reshape(lat_rows * lon_cols, channels)
    hidden = jnp.dot(
        flat_rows, weight, precision=lax.Precision.HIGHEST, preferred_element_type=jnp.float32
    )
    pre_grad = cotangent.reshape(lat_rows * lon_cols, channels) * gelu_slope(hidden)
    scale_factor = 1.0 / math.sqrt(lat_rows * lat_devices * all_lon)
    cell_grad = lax.dot_general(
        weight,
        pre_grad,
        (((1,), (1,)), ((), ())),
        precision=lax.Precision.HIGHEST,
        preferred_element_type=jnp.float32,
    )
    moved = lax.all_to_all(cell_grad, "lon", split_axis=0, concat_axis=1, tiled=True)
    gradient = (
        moved.reshape(own_channels, lon_devices, lat_rows, lon_cols)
        .transpose(0, 2, 1, 3)
        .reshape(own_channels, lat_rows, all_lon)
    )
    own_block = lax.psum_scatter(
        lax.dot_general(
            flat_rows,
            pre_grad,
            (((0,), (0,)), ((), ())),
            precision=lax.Precision.HIGHEST,
            preferred_element_type=jnp.float32,
        ),
        "lon",
        scatter_dimension=0,
        tiled=True,
    )
    grad_weight = lax.psum_scatter(own_block, "lat", scatter_dimension=1, tiled=True) * scale_factor
    row_start = lax.axis_index("lat") * lat_rows
    extended = with_halo(gradient, (("lat", 1),), 4)
    steps_padded = jnp.pad(lon_step, 4, constant_values=1)
    reach_padded = jnp.pad(row_reach, 4)
    coefs_padded = jnp.pad(coefs, ((0, 0), (4, 4), (0, 0)))
    wide_steps = lax.dynamic_slice_in_dim(steps_padded, row_start, lat_rows + 8)
    wide_reach = lax.dynamic_slice_in_dim(reach_padded, row_start, lat_rows + 8)
    wide_coefs = lax.dynamic_slice_in_dim(coefs_padded, row_start, lat_rows + 8, 1)
    rolled = [shift_rows(extended, wide_steps, lon_side) for lon_side in (-1, 0, 1)]
    result = jnp.zeros((own_channels, lat_rows, all_lon), jnp.float32)
    for offset in range(-4, 5):
        tap_sum = tap_term(rolled, wide_coefs, wide_reach, offset)
        result = result + tap_sum[:, 4 - offset : 4 - offset + lat_rows]
    return (result, grad_weight)


def body(saved, cotangent, weight, coefs, lon_step, row_reach):
    rows, cols, channels = saved.shape
    n = lax.axis_size("lon")
    fits = (
        lax.axis_size("lat") == 2
        and 4 <= n <= 16
        and n & (n - 1) == 0
        and channels % (16 * n) == 0
        and channels % LANES == 0
        and (rows * cols) % 128 == 0
        and rows % REACH == 0
        and rows >= 2 * REACH
        and 2 * cols == SUBLANES
        and n * cols >= 2 * MOST_STEP
        and channels % (SUBLANES * WEIGHT_PARTS) == 0
    )
    run = kernel_body if fits else collective_body
    return run(saved, cotangent, weight, coefs, lon_step, row_reach)


def solution(mesh):
    placed = (
        P(("member", "lat"), "lon", None),
        P(("member", "lat"), "lon", None),
        P(),
        P(None, None, "lon"),
        P(),
        P(),
    )
    return jax.shard_map(
        body,
        mesh=mesh,
        in_specs=placed,
        out_specs=(P("lon", ("member", "lat"), None), P(("member", "lon"), "lat")),
        check_vma=False,
    )
```

```python
import functools
import math

import jax
import jax.numpy as jnp
from jax import lax
from jax.experimental import pallas as pl
from jax.experimental.pallas import tpu as pltpu
from jax.sharding import PartitionSpec as P

MESH = pl.DeviceIdType.MESH
REACH = 4
MOST_STEP = 8
WEIGHT_PARTS = 4
SUBLANES = 8
WINDOW = 2
LANES = 128


def gelu_slope(values):
    cumulative = 0.5 * (1.0 + lax.erf(values * (1.0 / math.sqrt(2.0))))
    density = jnp.exp(-0.5 * values * values) * (1.0 / math.sqrt(2.0 * math.pi))
    return cumulative + values * density


def halves(x):
    high = x.astype(jnp.bfloat16)
    low = (x - high.astype(jnp.float32)).astype(jnp.bfloat16)
    return high, low


def dot3(a, b, dims):
    (ah, al), (bh, bl) = a, b
    dot = lambda p, q: lax.dot_general(p, q, (dims, ((), ())), preferred_element_type=jnp.float32)
    return dot(ah, bh) + (dot(ah, bl) + dot(al, bh))


def flipped(me, j, n):
    result = 0
    bit = 1
    while bit < n:
        mine = lax.rem(lax.div(me, bit), 2)
        result = result + bit * ((1 - mine) if j & bit else mine)
        bit *= 2
    return result


def zeros_below(j):
    return (j & -j).bit_length() - 1


def kernel(
    n,
    step_in, reach_in, saved_in, cot_in, weight_in, coefs_in,
    acc_out, gw_out,
    step_ref, reach_ref, saved_ref, cot_ref, weight_ref, coefs_ref, load_sem,
    s_t, s_t_peer, pg_t, pg_t_peer, cell, arrived, part, landed, weight_high, weight_low, slots, edge, halo, taps, rolled,
    lat_send, lat_recv, a2a_send, a2a_recv, gw_send, gw_recv,
):
    me = lax.axis_index("lon")
    lat = lax.axis_index("lat")
    other = 1 - lat
    rows, cols, channels = saved_ref.shape
    cells = rows * cols
    own = channels // n
    half = channels // 2
    all_lon = n * cols
    bits = n.bit_length() - 1
    full, tail = divmod(half, LANES)

    slab = channels // WEIGHT_PARTS
    pairs = [(saved_in, saved_ref)]
    pairs += [(weight_in.at[pl.ds(i * slab, slab)], weight_ref.at[pl.ds(i * slab, slab)]) for i in range(WEIGHT_PARTS)]
    pairs += [(cot_in, cot_ref), (coefs_in, coefs_ref), (step_in, step_ref), (reach_in, reach_ref)]
    loads = [pltpu.make_async_copy(src, dst, load_sem.at[i]) for i, (src, dst) in enumerate(pairs)]
    late = WEIGHT_PARTS + 2
    for load in loads[:late]:
        load.start()

    barrier = pltpu.get_barrier_semaphore()
    for s in range(1, n):
        pl.semaphore_signal(barrier, inc=1, device_id={"lon": lax.rem(me + s, n)}, device_id_type=MESH)
    pl.semaphore_signal(barrier, inc=1, device_id={"lat": other}, device_id_type=MESH)

    loads[0].wait()
    saved = saved_ref[...].reshape(cells, channels)
    s_t[...] = saved.T.reshape(n, own, cells)
    for load in loads[1 : 1 + WEIGHT_PARTS]:
        load.wait()
    for load in loads[late:]:
        load.start()
    weight = halves(weight_ref[...])
    weight_high[...] = weight[0].reshape(n, own, channels)
    weight_low[...] = weight[1].reshape(n, own, channels)
    hidden = dot3(halves(saved), weight, ((1,), (0,)))
    pl.semaphore_wait(barrier, n)

    def to_peer(src, dst, slot):
        return pltpu.make_async_remote_copy(
            src_ref=src, dst_ref=dst, send_sem=lat_send.at[slot], recv_sem=lat_recv.at[slot],
            device_id={"lat": other}, device_id_type=MESH,
        )

    saved_copy = to_peer(s_t, s_t_peer, 0)
    saved_copy.start()

    loads[1 + WEIGHT_PARTS].wait()
    pre_grad = cot_ref[...].reshape(cells, channels) * gelu_slope(hidden)
    turned = pre_grad.T
    pg_t[...] = turned.reshape(2, half, cells)
    pg_copy = to_peer(pg_t.at[other], pg_t_peer, 1)
    pg_copy.start()

    def across(s):
        dest = lax.rem(me + s, n)
        return pltpu.make_async_remote_copy(
            src_ref=cell.at[dest], dst_ref=arrived.at[me], send_sem=a2a_send.at[s - 1], recv_sem=a2a_recv.at[s - 1],
            device_id={"lon": dest}, device_id_type=MESH,
        )

    moves = {s: across(s) for s in range(1, n)}
    spans = list(range(n // 4, 3 * n // 4)), list(range(3 * n // 4, n)) + list(range(n // 4))
    right = halves(turned)
    for span in spans:
        owners = [lax.rem(me + s, n) for s in span]
        left = tuple(jnp.concatenate([ref[k] for k in owners], axis=0) for ref in (weight_high, weight_low))
        made = dot3(left, right, ((1,), (0,)))
        for at, s in enumerate(span):
            cell[owners[at]] = made[at * own : (at + 1) * own]
            if s:
                moves[s].start()

    def slot_of(stage, j):
        return n - (n >> stage) + j // (2 << stage)

    def hand_on(j):
        stage = zeros_below(j)
        slot = slot_of(stage, j)
        return pltpu.make_async_remote_copy(
            src_ref=part.at[j], dst_ref=landed.at[slot], send_sem=gw_send.at[slot], recv_sem=gw_recv.at[slot],
            device_id={"lon": flipped(me, 1 << stage, n)}, device_id_type=MESH,
        )

    order = sorted(range(n), key=lambda j: -int(format(j, "b").zfill(bits)[::-1], 2))
    sends = {j: hand_on(j) for j in range(1, n)}
    saved_copy.wait_recv()
    pg_copy.wait_recv()
    columns = halves(jnp.concatenate([pg_t[lat], pg_t_peer[...]], axis=1))
    for members in (order[: n // 2], order[n // 2 :]):
        owners = [flipped(me, j, n) for j in members]
        own_cells = jnp.concatenate([s_t[k] for k in owners], axis=0)
        peer_cells = jnp.concatenate([s_t_peer[k] for k in owners], axis=0)
        product = dot3(halves(jnp.concatenate([own_cells, peer_cells], axis=1)), columns, ((1,), (1,)))
        for at, j in enumerate(members):
            block = product[at * own : (at + 1) * own]
            for i in range(full):
                part[j, i * own : (i + 1) * own] = block[:, i * LANES : (i + 1) * LANES]
            if tail:
                rest = block[:, full * LANES :]
                part[j, full * own :] = jnp.concatenate([rest[: own // 2], rest[own // 2 :]], axis=1)
            if at < WINDOW and j % 2:
                sends[j].start()

    def gather(j):
        total = part[j]
        for stage in range(bits if j == 0 else zeros_below(j)):
            came = j + (1 << stage)
            sends[came].wait_recv()
            total = total + landed[slot_of(stage, j)]
        return total

    for load in loads[late:]:
        load.wait()

    def taps_of(place):
        row = lat * rows + place - REACH
        for tap in range(3 * (2 * REACH + 1)):
            live = jnp.where(abs(tap // 3 - REACH) <= reach_ref[row], 1.0, 0.0).astype(jnp.float32)
            taps[place, tap] = jnp.broadcast_to(coefs_ref[tap, pl.ds(row, 1), :] * live, (SUBLANES, own))

    beyond = (rows + REACH) * lat
    halo_at = (rows + REACH) * other

    @pl.loop(0, REACH)
    def _(i):
        taps[beyond + i] = jnp.zeros(taps.shape[1:], jnp.float32)
        rolled[beyond + i] = jnp.zeros(rolled.shape[1:], jnp.float32)
        taps_of(halo_at + i)

    @pl.loop(0, rows)
    def _(i):
        taps_of(REACH + i)

    for at, even in enumerate(order[n // 2 : -1]):
        if at + WINDOW < n // 2:
            sends[order[at]].wait_send()
            sends[order[at + WINDOW]].start()
        part[even] = gather(even)
        sends[even].start()

    slots[me] = cell[me].T
    for s in range(1, n):
        moves[s].wait_recv()
        source = lax.rem(me - s + n, n)
        slots[source] = arrived[source].T

    def row_pair(pair):
        at = pl.ds(pl.multiple_of(pair * SUBLANES, SUBLANES), SUBLANES)
        low = lax.broadcasted_iota(jnp.int32, (SUBLANES, own), 0) < cols
        even, odd = [], []
        for k in range(0, n, 2):
            a, b = slots[k, at, :], slots[k + 1, at, :]
            even.append(jnp.where(low, a, jnp.roll(b, cols, axis=0)))
            odd.append(jnp.where(low, jnp.roll(a, cols, axis=0), b))
        return jnp.concatenate(even, axis=0), jnp.concatenate(odd, axis=0)

    for i in range(0, REACH, 2):
        edge[i], edge[i + 1] = row_pair((rows - REACH) // 2 * other + i // 2)

    halo_copy = pltpu.make_async_remote_copy(
        src_ref=edge, dst_ref=halo, send_sem=lat_send.at[2], recv_sem=lat_recv.at[2],
        device_id={"lat": other}, device_id_type=MESH,
    )
    halo_copy.start()

    def roll_row(values, place):
        step = jnp.full(values.shape, step_ref[lat * rows + place - REACH], jnp.int32)
        up = values
        down = values
        bit = 1
        while bit <= MOST_STEP:
            chosen = (step & bit) != 0
            up = jnp.where(chosen, jnp.roll(up, bit, axis=0), up)
            down = jnp.where(chosen, jnp.roll(down, -bit, axis=0), down)
            bit *= 2
        rolled[place, 0] = down
        rolled[place, 1] = values
        rolled[place, 2] = up

    def sum_rows(group):
        base = group * REACH
        sums = [None] * REACH
        for away in range(3 * REACH):
            sources = [rolled[base + away, side].reshape(all_lon // SUBLANES, SUBLANES, own) for side in range(3)]
            for q in range(REACH):
                offset = q + REACH - away
                if abs(offset) > REACH:
                    continue
                for side in range(3):
                    term = taps[base + away, 3 * (offset + REACH) + side][None] * sources[side]
                    sums[q] = term if sums[q] is None else sums[q] + term
        for q in range(REACH):
            acc_out[base + q] = sums[q].reshape(all_lon, own)

    @pl.loop(0, rows // 2)
    def _(pair):
        even, odd = row_pair(pair)
        roll_row(even, REACH + 2 * pair)
        roll_row(odd, REACH + 2 * pair + 1)

    groups = rows // REACH

    @pl.loop(0, groups - 1)
    def _(i):
        sum_rows(lax.rem(i + lat, groups))

    halo_copy.wait_recv()

    @pl.loop(0, REACH)
    def _(i):
        roll_row(halo[i], halo_at + i)

    sum_rows(lax.rem(groups - 1 + lat, groups))

    total = gather(0) * (1.0 / math.sqrt(2 * rows * all_lon))
    for i in range(full):
        gw_out[:, i * LANES : (i + 1) * LANES] = total[i * own : (i + 1) * own]
    if tail:
        packed = total[full * own :]
        gw_out[: own // 2, full * LANES :] = packed[:, :tail]
        gw_out[own // 2 :, full * LANES :] = packed[:, tail:]

    saved_copy.wait_send()
    pg_copy.wait_send()
    halo_copy.wait_send()
    for s in range(1, n):
        moves[s].wait_send()
    for j in order[n // 2 - WINDOW : -1]:
        sends[j].wait_send()


def write_out(acc_in, grad_in, acc_out, grad_out, sem):
    copies = [
        pltpu.make_async_copy(acc_in, acc_out, sem.at[0]),
        pltpu.make_async_copy(grad_in, grad_out, sem.at[1]),
    ]
    for copy in copies:
        copy.start()
    for copy in copies:
        copy.wait()


def kernel_body(saved, cotangent, weight, coefs, lon_step, row_reach):
    rows, cols, channels = saved.shape
    n = lax.axis_size("lon")
    own = channels // n
    half = channels // 2
    cells = rows * cols
    f32 = jnp.float32
    vmem = pl.BlockSpec(memory_space=pltpu.VMEM)
    anywhere = pl.BlockSpec(memory_space=pl.ANY)
    packed_rows = own * half // LANES
    acc, grad = pl.pallas_call(
        functools.partial(kernel, n),
        out_shape=(
            pltpu.VMEM((rows, n * cols, own), f32),
            pltpu.VMEM((own, half), f32),
        ),
        in_specs=[anywhere] * 6,
        out_specs=(vmem, vmem),
        scratch_shapes=[
            pltpu.SMEM(lon_step.shape, lon_step.dtype),
            pltpu.SMEM(row_reach.shape, row_reach.dtype),
            pltpu.VMEM(saved.shape, f32),
            pltpu.VMEM(cotangent.shape, f32),
            pltpu.VMEM(weight.shape, f32),
            pltpu.VMEM(coefs.shape, f32),
            pltpu.SemaphoreType.DMA((WEIGHT_PARTS + 5,)),
            pltpu.VMEM((n, own, cells), f32),
            pltpu.VMEM((n, own, cells), f32),
            pltpu.VMEM((2, half, cells), f32),
            pltpu.VMEM((half, cells), f32),
            pltpu.VMEM((n, own, cells), f32),
            pltpu.VMEM((n, own, cells), f32),
            pltpu.VMEM((n, packed_rows, LANES), f32),
            pltpu.VMEM((n - 1, packed_rows, LANES), f32),
            pltpu.VMEM((n, own, channels), jnp.bfloat16),
            pltpu.VMEM((n, own, channels), jnp.bfloat16),
            pltpu.VMEM((n, cells, own), f32),
            pltpu.VMEM((REACH, n * cols, own), f32),
            pltpu.VMEM((REACH, n * cols, own), f32),
            pltpu.VMEM((rows + 2 * REACH, coefs.shape[0], SUBLANES, own), f32),
            pltpu.VMEM((rows + 2 * REACH, 3, n * cols, own), f32),
            pltpu.SemaphoreType.DMA((3,)),
            pltpu.SemaphoreType.DMA((3,)),
            pltpu.SemaphoreType.DMA((n - 1,)),
            pltpu.SemaphoreType.DMA((n - 1,)),
            pltpu.SemaphoreType.DMA((n - 1,)),
            pltpu.SemaphoreType.DMA((n - 1,)),
        ],
        compiler_params=pltpu.CompilerParams(
            collective_id=0, has_side_effects=True, vmem_limit_bytes=40 * 1024 * 1024
        ),
    )(*[
        pltpu.with_memory_space_constraint(x, pltpu.HBM)
        for x in (lon_step, row_reach, saved, cotangent, weight, coefs)
    ])
    acc, grad = pl.pallas_call(
        write_out,
        out_shape=(jax.ShapeDtypeStruct(acc.shape, f32), jax.ShapeDtypeStruct(grad.shape, f32)),
        in_specs=[vmem] * 2,
        out_specs=(anywhere,) * 2,
        scratch_shapes=[pltpu.SemaphoreType.DMA((2,))],
    )(*[pltpu.with_memory_space_constraint(x, pltpu.VMEM) for x in (acc, grad)])
    return jnp.transpose(acc, (2, 0, 1)), grad


def with_halo(x, sides, width):
    for axis, dim in sides:
        peers, length = (lax.axis_size(axis), x.shape[dim])
        up = [(i, (i + 1) % peers) for i in range(peers - 1)]
        down = [(j, i) for i, j in up]
        last = lax.slice_in_dim(x, length - width, length, axis=dim)
        initial = lax.slice_in_dim(x, 0, width, axis=dim)
        before = lax.ppermute(last, axis, up)
        after = lax.ppermute(initial, axis, down)
        x = jnp.concatenate([before, x, after], axis=dim)
    return x


def shift_rows(gradient, shifts, direction):
    width = gradient.shape[2]
    if direction == 0:
        return gradient
    wrapped = jnp.concatenate([gradient[:, :, width - 8 :], gradient, gradient[:, :, :8]], axis=2)
    result = gradient
    for amount in range(1, 9):
        begin = 8 - direction * amount
        piece = wrapped[:, :, begin : begin + width]
        result = jnp.where((shifts == amount)[None, :, None], piece, result)
    return result


def tap_term(rolled, coefs, row_reach, offset):
    summed = jnp.zeros_like(rolled[0])
    for lon_side in range(3):
        tap_index = (offset + 4) * 3 + lon_side
        summed = summed + jnp.transpose(coefs[tap_index])[:, :, None] * rolled[lon_side]
    live_rows = (abs(offset) <= row_reach).astype(jnp.float32)
    return summed * live_rows[None, :, None]


def collective_body(saved, cotangent, weight, coefs, lon_step, row_reach):
    lat_rows, lon_cols, channels = saved.shape
    lon_devices = lax.axis_size("lon")
    lat_devices = lax.axis_size("lat")
    own_channels = channels // lon_devices
    all_lon = lon_devices * lon_cols
    flat_rows = saved.reshape(lat_rows * lon_cols, channels)
    hidden = jnp.dot(
        flat_rows, weight, precision=lax.Precision.HIGHEST, preferred_element_type=jnp.float32
    )
    pre_grad = cotangent.reshape(lat_rows * lon_cols, channels) * gelu_slope(hidden)
    scale_factor = 1.0 / math.sqrt(lat_rows * lat_devices * all_lon)
    cell_grad = lax.dot_general(
        weight,
        pre_grad,
        (((1,), (1,)), ((), ())),
        precision=lax.Precision.HIGHEST,
        preferred_element_type=jnp.float32,
    )
    moved = lax.all_to_all(cell_grad, "lon", split_axis=0, concat_axis=1, tiled=True)
    gradient = (
        moved.reshape(own_channels, lon_devices, lat_rows, lon_cols)
        .transpose(0, 2, 1, 3)
        .reshape(own_channels, lat_rows, all_lon)
    )
    own_block = lax.psum_scatter(
        lax.dot_general(
            flat_rows,
            pre_grad,
            (((0,), (0,)), ((), ())),
            precision=lax.Precision.HIGHEST,
            preferred_element_type=jnp.float32,
        ),
        "lon",
        scatter_dimension=0,
        tiled=True,
    )
    grad_weight = lax.psum_scatter(own_block, "lat", scatter_dimension=1, tiled=True) * scale_factor
    row_start = lax.axis_index("lat") * lat_rows
    extended = with_halo(gradient, (("lat", 1),), 4)
    steps_padded = jnp.pad(lon_step, 4, constant_values=1)
    reach_padded = jnp.pad(row_reach, 4)
    coefs_padded = jnp.pad(coefs, ((0, 0), (4, 4), (0, 0)))
    wide_steps = lax.dynamic_slice_in_dim(steps_padded, row_start, lat_rows + 8)
    wide_reach = lax.dynamic_slice_in_dim(reach_padded, row_start, lat_rows + 8)
    wide_coefs = lax.dynamic_slice_in_dim(coefs_padded, row_start, lat_rows + 8, 1)
    rolled = [shift_rows(extended, wide_steps, lon_side) for lon_side in (-1, 0, 1)]
    result = jnp.zeros((own_channels, lat_rows, all_lon), jnp.float32)
    for offset in range(-4, 5):
        tap_sum = tap_term(rolled, wide_coefs, wide_reach, offset)
        result = result + tap_sum[:, 4 - offset : 4 - offset + lat_rows]
    return (result, grad_weight)


def body(saved, cotangent, weight, coefs, lon_step, row_reach):
    rows, cols, channels = saved.shape
    n = lax.axis_size("lon")
    fits = (
        lax.axis_size("lat") == 2
        and 4 <= n <= 16
        and n & (n - 1) == 0
        and channels % (16 * n) == 0
        and channels % LANES == 0
        and (rows * cols) % 128 == 0
        and rows % REACH == 0
        and rows >= 2 * REACH
        and 2 * cols == SUBLANES
        and n * cols >= 2 * MOST_STEP
        and channels % (SUBLANES * WEIGHT_PARTS) == 0
    )
    run = kernel_body if fits else collective_body
    return run(saved, cotangent, weight, coefs, lon_step, row_reach)


def solution(mesh):
    placed = (
        P(("member", "lat"), "lon", None),
        P(("member", "lat"), "lon", None),
        P(),
        P(None, None, "lon"),
        P(),
        P(),
    )
    return jax.shard_map(
        body,
        mesh=mesh,
        in_specs=placed,
        out_specs=(P("lon", ("member", "lat"), None), P(("member", "lon"), "lat")),
        check_vma=False,
    )
```

```python
import functools
import math

import jax
import jax.numpy as jnp
from jax import lax
from jax.experimental import pallas as pl
from jax.experimental.pallas import tpu as pltpu
from jax.sharding import PartitionSpec as P

MESH = pl.DeviceIdType.MESH
REACH = 4
MOST_STEP = 8
SLAB = 256
SUBLANES = 8
WINDOW = 1
LANES = 128


def gelu_slope(values):
    cumulative = 0.5 * (1.0 + lax.erf(values * (1.0 / math.sqrt(2.0))))
    density = jnp.exp(-0.5 * values * values) * (1.0 / math.sqrt(2.0 * math.pi))
    return cumulative + values * density


def halves(x):
    high = x.astype(jnp.bfloat16)
    low = (x - high.astype(jnp.float32)).astype(jnp.bfloat16)
    return high, low


def dot3(a, b, dims):
    (ah, al), (bh, bl) = a, b
    dot = lambda p, q: lax.dot_general(p, q, (dims, ((), ())), preferred_element_type=jnp.float32)
    return dot(ah, bh) + (dot(ah, bl) + dot(al, bh))


def flipped(me, j, n):
    result = 0
    bit = 1
    while bit < n:
        mine = lax.rem(lax.div(me, bit), 2)
        result = result + bit * ((1 - mine) if j & bit else mine)
        bit *= 2
    return result


def zeros_below(j):
    return (j & -j).bit_length() - 1


def kernel(
    n,
    step_in, reach_in, saved_in, cot_in, weight_in, coefs_in,
    acc_out, gw_out,
    step_ref, reach_ref, saved_ref, cot_ref, weight_ref, coefs_ref, load_sem,
    s_t, s_t_peer, pg_t, pg_t_peer, cell, arrived, part, landed, weight_high, weight_low, slots, edge, halo, taps, rolled,
    lat_send, lat_recv, a2a_send, a2a_recv, gw_send, gw_recv,
):
    me = lax.axis_index("lon")
    lat = lax.axis_index("lat")
    other = 1 - lat
    rows, cols, channels = saved_ref.shape
    cells = rows * cols
    own = channels // n
    half = channels // 2
    all_lon = n * cols
    bits = n.bit_length() - 1
    full, tail = divmod(half, LANES)

    slabs = [(at, min(SLAB, channels - at)) for at in range(0, channels, SLAB)]
    pairs = [(saved_in, saved_ref)]
    pairs += [(weight_in.at[pl.ds(at, size)], weight_ref.at[pl.ds(at, size)]) for at, size in slabs]
    pairs += [(cot_in, cot_ref), (coefs_in, coefs_ref), (step_in, step_ref), (reach_in, reach_ref)]
    loads = [pltpu.make_async_copy(src, dst, load_sem.at[i]) for i, (src, dst) in enumerate(pairs)]
    late = len(slabs) + 2
    for load in loads[:late]:
        load.start()

    barrier = pltpu.get_barrier_semaphore()
    for s in range(1, n):
        pl.semaphore_signal(barrier, inc=1, device_id={"lon": lax.rem(me + s, n)}, device_id_type=MESH)
    pl.semaphore_signal(barrier, inc=1, device_id={"lat": other}, device_id_type=MESH)

    loads[0].wait()
    saved = saved_ref[...].reshape(cells, channels)
    s_t[...] = saved.T.reshape(n, own, cells)
    pieces = []
    hidden = None
    for (at, size), load in zip(slabs, loads[1:]):
        load.wait()
        pieces.append(halves(weight_ref[at : at + size]))
        term = dot3(halves(saved[:, at : at + size]), pieces[-1], ((1,), (0,)))
        hidden = term if hidden is None else hidden + term
    weight_high[...] = jnp.concatenate([p[0] for p in pieces], axis=0).reshape(n, own, channels)
    weight_low[...] = jnp.concatenate([p[1] for p in pieces], axis=0).reshape(n, own, channels)
    for load in loads[late:]:
        load.start()
    pl.semaphore_wait(barrier, n)

    def to_peer(src, dst, slot):
        return pltpu.make_async_remote_copy(
            src_ref=src, dst_ref=dst, send_sem=lat_send.at[slot], recv_sem=lat_recv.at[slot],
            device_id={"lat": other}, device_id_type=MESH,
        )

    saved_copy = to_peer(s_t, s_t_peer, 0)
    saved_copy.start()

    loads[late - 1].wait()
    pre_grad = cot_ref[...].reshape(cells, channels) * gelu_slope(hidden)
    turned = pre_grad.T
    pg_t[...] = turned.reshape(2, half, cells)
    pg_copy = to_peer(pg_t.at[other], pg_t_peer, 1)
    pg_copy.start()

    def across(s):
        dest = lax.rem(me + s, n)
        return pltpu.make_async_remote_copy(
            src_ref=cell.at[dest], dst_ref=arrived.at[me], send_sem=a2a_send.at[s - 1], recv_sem=a2a_recv.at[s - 1],
            device_id={"lon": dest}, device_id_type=MESH,
        )

    moves = {s: across(s) for s in range(1, n)}
    spans = list(range(n // 4, 3 * n // 4)), list(range(3 * n // 4, n)) + list(range(n // 4))
    right = halves(turned)
    for span in spans:
        owners = [lax.rem(me + s, n) for s in span]
        left = tuple(jnp.concatenate([ref[k] for k in owners], axis=0) for ref in (weight_high, weight_low))
        made = dot3(left, right, ((1,), (0,)))
        for at, s in enumerate(span):
            cell[owners[at]] = made[at * own : (at + 1) * own]
            if s:
                moves[s].start()

    def slot_of(stage, j):
        return n - (n >> stage) + j // (2 << stage)

    def hand_on(j):
        stage = zeros_below(j)
        slot = slot_of(stage, j)
        return pltpu.make_async_remote_copy(
            src_ref=part.at[j], dst_ref=landed.at[slot], send_sem=gw_send.at[slot], recv_sem=gw_recv.at[slot],
            device_id={"lon": flipped(me, 1 << stage, n)}, device_id_type=MESH,
        )

    order = sorted(range(n), key=lambda j: -int(format(j, "b").zfill(bits)[::-1], 2))
    sends = {j: hand_on(j) for j in range(1, n)}
    saved_copy.wait_recv()
    pg_copy.wait_recv()
    columns = halves(jnp.concatenate([pg_t[lat], pg_t_peer[...]], axis=1))
    for members in (order[: n // 2], order[n // 2 :]):
        owners = [flipped(me, j, n) for j in members]
        own_cells = jnp.concatenate([s_t[k] for k in owners], axis=0)
        peer_cells = jnp.concatenate([s_t_peer[k] for k in owners], axis=0)
        product = dot3(halves(jnp.concatenate([own_cells, peer_cells], axis=1)), columns, ((1,), (1,)))
        for at, j in enumerate(members):
            block = product[at * own : (at + 1) * own]
            for i in range(full):
                part[j, i * own : (i + 1) * own] = block[:, i * LANES : (i + 1) * LANES]
            if tail:
                rest = block[:, full * LANES :]
                part[j, full * own :] = jnp.concatenate([rest[: own // 2], rest[own // 2 :]], axis=1)
            if at < WINDOW and j % 2:
                sends[j].start()

    def gather(j):
        total = part[j]
        for stage in range(bits if j == 0 else zeros_below(j)):
            came = j + (1 << stage)
            sends[came].wait_recv()
            total = total + landed[slot_of(stage, j)]
        return total

    for load in loads[late:]:
        load.wait()

    def taps_of(place):
        row = lat * rows + place - REACH
        for tap in range(3 * (2 * REACH + 1)):
            live = jnp.where(abs(tap // 3 - REACH) <= reach_ref[row], 1.0, 0.0).astype(jnp.float32)
            taps[place, tap] = jnp.broadcast_to(coefs_ref[tap, pl.ds(row, 1), :] * live, (SUBLANES, own))

    beyond = (rows + REACH) * lat
    halo_at = (rows + REACH) * other

    @pl.loop(0, REACH)
    def _(i):
        taps[beyond + i] = jnp.zeros(taps.shape[1:], jnp.float32)
        rolled[beyond + i] = jnp.zeros(rolled.shape[1:], jnp.float32)
        taps_of(halo_at + i)

    @pl.loop(0, rows)
    def _(i):
        taps_of(REACH + i)

    for at, even in enumerate(order[n // 2 : -1]):
        if at + WINDOW < n // 2:
            sends[order[at]].wait_send()
            sends[order[at + WINDOW]].start()
        part[even] = gather(even)
        sends[even].start()

    slots[me] = cell[me].T
    for s in range(1, n):
        moves[s].wait_recv()
        source = lax.rem(me - s + n, n)
        slots[source] = arrived[source].T

    def row_pair(pair):
        at = pl.ds(pl.multiple_of(pair * SUBLANES, SUBLANES), SUBLANES)
        low = lax.broadcasted_iota(jnp.int32, (SUBLANES, own), 0) < cols
        even, odd = [], []
        for k in range(0, n, 2):
            a, b = slots[k, at, :], slots[k + 1, at, :]
            even.append(jnp.where(low, a, jnp.roll(b, cols, axis=0)))
            odd.append(jnp.where(low, jnp.roll(a, cols, axis=0), b))
        return jnp.concatenate(even, axis=0), jnp.concatenate(odd, axis=0)

    for i in range(0, REACH, 2):
        edge[i], edge[i + 1] = row_pair((rows - REACH) // 2 * other + i // 2)

    halo_copy = pltpu.make_async_remote_copy(
        src_ref=edge, dst_ref=halo, send_sem=lat_send.at[2], recv_sem=lat_recv.at[2],
        device_id={"lat": other}, device_id_type=MESH,
    )
    halo_copy.start()

    def roll_row(values, place):
        step = jnp.full(values.shape, step_ref[lat * rows + place - REACH], jnp.int32)
        up = values
        down = values
        bit = 1
        while bit <= MOST_STEP:
            chosen = (step & bit) != 0
            up = jnp.where(chosen, jnp.roll(up, bit, axis=0), up)
            down = jnp.where(chosen, jnp.roll(down, -bit, axis=0), down)
            bit *= 2
        rolled[place, 0] = down
        rolled[place, 1] = values
        rolled[place, 2] = up

    def sum_rows(group):
        base = group * REACH
        sums = [None] * REACH
        for away in range(3 * REACH):
            sources = [rolled[base + away, side].reshape(all_lon // SUBLANES, SUBLANES, own) for side in range(3)]
            for q in range(REACH):
                offset = q + REACH - away
                if abs(offset) > REACH:
                    continue
                for side in range(3):
                    term = taps[base + away, 3 * (offset + REACH) + side][None] * sources[side]
                    sums[q] = term if sums[q] is None else sums[q] + term
        for q in range(REACH):
            acc_out[base + q] = sums[q].reshape(all_lon, own)

    @pl.loop(0, rows // 2)
    def _(pair):
        even, odd = row_pair(pair)
        roll_row(even, REACH + 2 * pair)
        roll_row(odd, REACH + 2 * pair + 1)

    groups = rows // REACH

    @pl.loop(0, groups - 1)
    def _(i):
        sum_rows(lax.rem(i + lat, groups))

    halo_copy.wait_recv()

    @pl.loop(0, REACH)
    def _(i):
        roll_row(halo[i], halo_at + i)

    sum_rows(lax.rem(groups - 1 + lat, groups))

    total = gather(0) * (1.0 / math.sqrt(2 * rows * all_lon))
    for i in range(full):
        gw_out[:, i * LANES : (i + 1) * LANES] = total[i * own : (i + 1) * own]
    if tail:
        packed = total[full * own :]
        gw_out[: own // 2, full * LANES :] = packed[:, :tail]
        gw_out[own // 2 :, full * LANES :] = packed[:, tail:]

    saved_copy.wait_send()
    pg_copy.wait_send()
    halo_copy.wait_send()
    for s in range(1, n):
        moves[s].wait_send()
    for j in order[n // 2 - WINDOW : -1]:
        sends[j].wait_send()


def write_out(acc_in, grad_in, acc_out, grad_out, sem):
    copies = [
        pltpu.make_async_copy(acc_in, acc_out, sem.at[0]),
        pltpu.make_async_copy(grad_in, grad_out, sem.at[1]),
    ]
    for copy in copies:
        copy.start()
    for copy in copies:
        copy.wait()


def kernel_body(saved, cotangent, weight, coefs, lon_step, row_reach):
    rows, cols, channels = saved.shape
    n = lax.axis_size("lon")
    own = channels // n
    half = channels // 2
    cells = rows * cols
    f32 = jnp.float32
    vmem = pl.BlockSpec(memory_space=pltpu.VMEM)
    anywhere = pl.BlockSpec(memory_space=pl.ANY)
    packed_rows = own * half // LANES
    acc, grad = pl.pallas_call(
        functools.partial(kernel, n),
        out_shape=(
            pltpu.VMEM((rows, n * cols, own), f32),
            pltpu.VMEM((own, half), f32),
        ),
        in_specs=[anywhere] * 6,
        out_specs=(vmem, vmem),
        scratch_shapes=[
            pltpu.SMEM(lon_step.shape, lon_step.dtype),
            pltpu.SMEM(row_reach.shape, row_reach.dtype),
            pltpu.VMEM(saved.shape, f32),
            pltpu.VMEM(cotangent.shape, f32),
            pltpu.VMEM(weight.shape, f32),
            pltpu.VMEM(coefs.shape, f32),
            pltpu.SemaphoreType.DMA((5 + -(-weight.shape[0] // SLAB),)),
            pltpu.VMEM((n, own, cells), f32),
            pltpu.VMEM((n, own, cells), f32),
            pltpu.VMEM((2, half, cells), f32),
            pltpu.VMEM((half, cells), f32),
            pltpu.VMEM((n, own, cells), f32),
            pltpu.VMEM((n, own, cells), f32),
            pltpu.VMEM((n, packed_rows, LANES), f32),
            pltpu.VMEM((n - 1, packed_rows, LANES), f32),
            pltpu.VMEM((n, own, channels), jnp.bfloat16),
            pltpu.VMEM((n, own, channels), jnp.bfloat16),
            pltpu.VMEM((n, cells, own), f32),
            pltpu.VMEM((REACH, n * cols, own), f32),
            pltpu.VMEM((REACH, n * cols, own), f32),
            pltpu.VMEM((rows + 2 * REACH, coefs.shape[0], SUBLANES, own), f32),
            pltpu.VMEM((rows + 2 * REACH, 3, n * cols, own), f32),
            pltpu.SemaphoreType.DMA((3,)),
            pltpu.SemaphoreType.DMA((3,)),
            pltpu.SemaphoreType.DMA((n - 1,)),
            pltpu.SemaphoreType.DMA((n - 1,)),
            pltpu.SemaphoreType.DMA((n - 1,)),
            pltpu.SemaphoreType.DMA((n - 1,)),
        ],
        compiler_params=pltpu.CompilerParams(
            collective_id=0, has_side_effects=True, vmem_limit_bytes=40 * 1024 * 1024
        ),
    )(*[
        pltpu.with_memory_space_constraint(x, pltpu.HBM)
        for x in (lon_step, row_reach, saved, cotangent, weight, coefs)
    ])
    acc, grad = pl.pallas_call(
        write_out,
        out_shape=(jax.ShapeDtypeStruct(acc.shape, f32), jax.ShapeDtypeStruct(grad.shape, f32)),
        in_specs=[vmem] * 2,
        out_specs=(anywhere,) * 2,
        scratch_shapes=[pltpu.SemaphoreType.DMA((2,))],
    )(*[pltpu.with_memory_space_constraint(x, pltpu.VMEM) for x in (acc, grad)])
    return jnp.transpose(acc, (2, 0, 1)), grad


def with_halo(x, sides, width):
    for axis, dim in sides:
        peers, length = (lax.axis_size(axis), x.shape[dim])
        up = [(i, (i + 1) % peers) for i in range(peers - 1)]
        down = [(j, i) for i, j in up]
        last = lax.slice_in_dim(x, length - width, length, axis=dim)
        initial = lax.slice_in_dim(x, 0, width, axis=dim)
        before = lax.ppermute(last, axis, up)
        after = lax.ppermute(initial, axis, down)
        x = jnp.concatenate([before, x, after], axis=dim)
    return x


def shift_rows(gradient, shifts, direction):
    width = gradient.shape[2]
    if direction == 0:
        return gradient
    wrapped = jnp.concatenate([gradient[:, :, width - 8 :], gradient, gradient[:, :, :8]], axis=2)
    result = gradient
    for amount in range(1, 9):
        begin = 8 - direction * amount
        piece = wrapped[:, :, begin : begin + width]
        result = jnp.where((shifts == amount)[None, :, None], piece, result)
    return result


def tap_term(rolled, coefs, row_reach, offset):
    summed = jnp.zeros_like(rolled[0])
    for lon_side in range(3):
        tap_index = (offset + 4) * 3 + lon_side
        summed = summed + jnp.transpose(coefs[tap_index])[:, :, None] * rolled[lon_side]
    live_rows = (abs(offset) <= row_reach).astype(jnp.float32)
    return summed * live_rows[None, :, None]


def collective_body(saved, cotangent, weight, coefs, lon_step, row_reach):
    lat_rows, lon_cols, channels = saved.shape
    lon_devices = lax.axis_size("lon")
    lat_devices = lax.axis_size("lat")
    own_channels = channels // lon_devices
    all_lon = lon_devices * lon_cols
    flat_rows = saved.reshape(lat_rows * lon_cols, channels)
    hidden = jnp.dot(
        flat_rows, weight, precision=lax.Precision.HIGHEST, preferred_element_type=jnp.float32
    )
    pre_grad = cotangent.reshape(lat_rows * lon_cols, channels) * gelu_slope(hidden)
    scale_factor = 1.0 / math.sqrt(lat_rows * lat_devices * all_lon)
    cell_grad = lax.dot_general(
        weight,
        pre_grad,
        (((1,), (1,)), ((), ())),
        precision=lax.Precision.HIGHEST,
        preferred_element_type=jnp.float32,
    )
    moved = lax.all_to_all(cell_grad, "lon", split_axis=0, concat_axis=1, tiled=True)
    gradient = (
        moved.reshape(own_channels, lon_devices, lat_rows, lon_cols)
        .transpose(0, 2, 1, 3)
        .reshape(own_channels, lat_rows, all_lon)
    )
    own_block = lax.psum_scatter(
        lax.dot_general(
            flat_rows,
            pre_grad,
            (((0,), (0,)), ((), ())),
            precision=lax.Precision.HIGHEST,
            preferred_element_type=jnp.float32,
        ),
        "lon",
        scatter_dimension=0,
        tiled=True,
    )
    grad_weight = lax.psum_scatter(own_block, "lat", scatter_dimension=1, tiled=True) * scale_factor
    row_start = lax.axis_index("lat") * lat_rows
    extended = with_halo(gradient, (("lat", 1),), 4)
    steps_padded = jnp.pad(lon_step, 4, constant_values=1)
    reach_padded = jnp.pad(row_reach, 4)
    coefs_padded = jnp.pad(coefs, ((0, 0), (4, 4), (0, 0)))
    wide_steps = lax.dynamic_slice_in_dim(steps_padded, row_start, lat_rows + 8)
    wide_reach = lax.dynamic_slice_in_dim(reach_padded, row_start, lat_rows + 8)
    wide_coefs = lax.dynamic_slice_in_dim(coefs_padded, row_start, lat_rows + 8, 1)
    rolled = [shift_rows(extended, wide_steps, lon_side) for lon_side in (-1, 0, 1)]
    result = jnp.zeros((own_channels, lat_rows, all_lon), jnp.float32)
    for offset in range(-4, 5):
        tap_sum = tap_term(rolled, wide_coefs, wide_reach, offset)
        result = result + tap_sum[:, 4 - offset : 4 - offset + lat_rows]
    return (result, grad_weight)


def body(saved, cotangent, weight, coefs, lon_step, row_reach):
    rows, cols, channels = saved.shape
    n = lax.axis_size("lon")
    fits = (
        lax.axis_size("lat") == 2
        and 4 <= n <= 16
        and n & (n - 1) == 0
        and channels % (16 * n) == 0
        and channels % LANES == 0
        and (rows * cols) % 128 == 0
        and rows % REACH == 0
        and rows >= 2 * REACH
        and 2 * cols == SUBLANES
        and n * cols >= 2 * MOST_STEP
    )
    run = kernel_body if fits else collective_body
    return run(saved, cotangent, weight, coefs, lon_step, row_reach)


def solution(mesh):
    placed = (
        P(("member", "lat"), "lon", None),
        P(("member", "lat"), "lon", None),
        P(),
        P(None, None, "lon"),
        P(),
        P(),
    )
    return jax.shard_map(
        body,
        mesh=mesh,
        in_specs=placed,
        out_specs=(P("lon", ("member", "lat"), None), P(("member", "lon"), "lat")),
        check_vma=False,
    )
```

```python
import functools
import math

import jax
import jax.numpy as jnp
from jax import lax
from jax.experimental import pallas as pl
from jax.experimental.pallas import tpu as pltpu
from jax.sharding import PartitionSpec as P

MESH = pl.DeviceIdType.MESH
REACH = 4
MOST_STEP = 8
SLAB = 256
SUBLANES = 8
WINDOW = 1
LANES = 128


def gelu_slope(values):
    cumulative = 0.5 * (1.0 + lax.erf(values * (1.0 / math.sqrt(2.0))))
    density = jnp.exp(-0.5 * values * values) * (1.0 / math.sqrt(2.0 * math.pi))
    return cumulative + values * density


def halves(x):
    high = x.astype(jnp.bfloat16)
    low = (x - high.astype(jnp.float32)).astype(jnp.bfloat16)
    return high, low


def dot3(a, b, dims):
    (ah, al), (bh, bl) = a, b
    dot = lambda p, q: lax.dot_general(p, q, (dims, ((), ())), preferred_element_type=jnp.float32)
    return dot(ah, bh) + (dot(ah, bl) + dot(al, bh))


def flipped(me, j, n):
    result = 0
    bit = 1
    while bit < n:
        mine = lax.rem(lax.div(me, bit), 2)
        result = result + bit * ((1 - mine) if j & bit else mine)
        bit *= 2
    return result


def zeros_below(j):
    return (j & -j).bit_length() - 1


def kernel(
    n,
    step_in, reach_in, saved_in, cot_in, weight_in, coefs_in,
    acc_out, gw_out,
    step_ref, reach_ref, saved_ref, cot_ref, weight_ref, coefs_ref, load_sem,
    s_t, s_t_peer, pg_t, pg_t_peer, cell, arrived, part, landed, weight_high, weight_low, slots, edge, halo, taps, rolled,
    lat_send, lat_recv, a2a_send, a2a_recv, gw_send, gw_recv,
):
    me = lax.axis_index("lon")
    lat = lax.axis_index("lat")
    other = 1 - lat
    rows, cols, channels = saved_ref.shape
    cells = rows * cols
    own = channels // n
    half = channels // 2
    all_lon = n * cols
    bits = n.bit_length() - 1
    full, tail = divmod(half, LANES)

    slabs = [(at, min(SLAB, channels - at)) for at in range(0, channels, SLAB)]
    pairs = [(saved_in, saved_ref)]
    pairs += [(weight_in.at[pl.ds(at, size)], weight_ref.at[pl.ds(at, size)]) for at, size in slabs]
    pairs += [(cot_in, cot_ref), (coefs_in, coefs_ref), (step_in, step_ref), (reach_in, reach_ref)]
    loads = [pltpu.make_async_copy(src, dst, load_sem.at[i]) for i, (src, dst) in enumerate(pairs)]
    late = len(slabs) + 2
    for load in loads[:late]:
        load.start()

    barrier = pltpu.get_barrier_semaphore()
    for s in range(1, n):
        pl.semaphore_signal(barrier, inc=1, device_id={"lon": lax.rem(me + s, n)}, device_id_type=MESH)
    pl.semaphore_signal(barrier, inc=1, device_id={"lat": other}, device_id_type=MESH)

    loads[0].wait()
    saved = saved_ref[...].reshape(cells, channels)
    s_t[...] = saved.T.reshape(n, own, cells)
    pieces = []
    hidden = None
    for (at, size), load in zip(slabs, loads[1:]):
        load.wait()
        pieces.append(halves(weight_ref[at : at + size]))
        term = dot3(halves(saved[:, at : at + size]), pieces[-1], ((1,), (0,)))
        hidden = term if hidden is None else hidden + term
    weight_high[...] = jnp.concatenate([p[0] for p in pieces], axis=0).reshape(n, own, channels)
    weight_low[...] = jnp.concatenate([p[1] for p in pieces], axis=0).reshape(n, own, channels)
    for load in loads[late:]:
        load.start()
    pl.semaphore_wait(barrier, n)

    def to_peer(src, dst, slot):
        return pltpu.make_async_remote_copy(
            src_ref=src, dst_ref=dst, send_sem=lat_send.at[slot], recv_sem=lat_recv.at[slot],
            device_id={"lat": other}, device_id_type=MESH,
        )

    saved_copy = to_peer(s_t, s_t_peer, 0)
    saved_copy.start()

    loads[late - 1].wait()
    pre_grad = cot_ref[...].reshape(cells, channels) * gelu_slope(hidden)
    turned = pre_grad.T
    pg_t[...] = turned.reshape(2, half, cells)
    pg_copy = to_peer(pg_t.at[other], pg_t_peer, 1)
    pg_copy.start()

    def across(s):
        dest = lax.rem(me + s, n)
        return pltpu.make_async_remote_copy(
            src_ref=cell.at[dest], dst_ref=arrived.at[me], send_sem=a2a_send.at[s - 1], recv_sem=a2a_recv.at[s - 1],
            device_id={"lon": dest}, device_id_type=MESH,
        )

    moves = {s: across(s) for s in range(1, n)}
    spans = list(range(n // 4, 3 * n // 4)), list(range(3 * n // 4, n)) + list(range(n // 4))
    right = halves(turned)
    for span in spans:
        owners = [lax.rem(me + s, n) for s in span]
        left = tuple(jnp.concatenate([ref[k] for k in owners], axis=0) for ref in (weight_high, weight_low))
        made = dot3(left, right, ((1,), (0,)))
        for at, s in enumerate(span):
            cell[owners[at]] = made[at * own : (at + 1) * own]
            if s:
                moves[s].start()

    def slot_of(stage, j):
        return n - (n >> stage) + j // (2 << stage)

    def hand_on(j):
        stage = zeros_below(j)
        slot = slot_of(stage, j)
        return pltpu.make_async_remote_copy(
            src_ref=part.at[j], dst_ref=landed.at[slot], send_sem=gw_send.at[slot], recv_sem=gw_recv.at[slot],
            device_id={"lon": flipped(me, 1 << stage, n)}, device_id_type=MESH,
        )

    order = sorted(range(n), key=lambda j: -int(format(j, "b").zfill(bits)[::-1], 2))
    sends = {j: hand_on(j) for j in range(1, n)}
    saved_copy.wait_recv()
    pg_copy.wait_recv()
    columns = halves(jnp.concatenate([pg_t[lat], pg_t_peer[...]], axis=1))
    for members in (order[: n // 2], order[n // 2 :]):
        owners = [flipped(me, j, n) for j in members]
        own_cells = jnp.concatenate([s_t[k] for k in owners], axis=0)
        peer_cells = jnp.concatenate([s_t_peer[k] for k in owners], axis=0)
        product = dot3(halves(jnp.concatenate([own_cells, peer_cells], axis=1)), columns, ((1,), (1,)))
        for at, j in enumerate(members):
            block = product[at * own : (at + 1) * own]
            for i in range(full):
                part[j, i * own : (i + 1) * own] = block[:, i * LANES : (i + 1) * LANES]
            if tail:
                rest = block[:, full * LANES :]
                part[j, full * own :] = jnp.concatenate([rest[: own // 2], rest[own // 2 :]], axis=1)
            if at < WINDOW and j % 2:
                sends[j].start()

    def gather(j):
        total = part[j]
        for stage in range(bits if j == 0 else zeros_below(j)):
            came = j + (1 << stage)
            sends[came].wait_recv()
            total = total + landed[slot_of(stage, j)]
        return total

    for load in loads[late:]:
        load.wait()

    def taps_of(place):
        row = lat * rows + place - REACH
        for tap in range(3 * (2 * REACH + 1)):
            live = jnp.where(abs(tap // 3 - REACH) <= reach_ref[row], 1.0, 0.0).astype(jnp.float32)
            taps[place, tap] = jnp.broadcast_to(coefs_ref[tap, pl.ds(row, 1), :] * live, (SUBLANES, own))

    beyond = (rows + REACH) * lat
    halo_at = (rows + REACH) * other

    @pl.loop(0, REACH)
    def _(i):
        taps[beyond + i] = jnp.zeros(taps.shape[1:], jnp.float32)
        rolled[beyond + i] = jnp.zeros(rolled.shape[1:], jnp.float32)
        taps_of(halo_at + i)

    @pl.loop(0, rows)
    def _(i):
        taps_of(REACH + i)

    def advance(at):
        if at + WINDOW < n // 2:
            sends[order[at]].wait_send()
            sends[order[at + WINDOW]].start()
        even = order[n // 2 + at]
        part[even] = gather(even)
        sends[even].start()

    for at in range(n // 2 - 2):
        advance(at)

    slots[me] = cell[me].T
    for s in range(1, n):
        moves[s].wait_recv()
        source = lax.rem(me - s + n, n)
        slots[source] = arrived[source].T

    def row_pair(pair):
        at = pl.ds(pl.multiple_of(pair * SUBLANES, SUBLANES), SUBLANES)
        low = lax.broadcasted_iota(jnp.int32, (SUBLANES, own), 0) < cols
        even, odd = [], []
        for k in range(0, n, 2):
            a, b = slots[k, at, :], slots[k + 1, at, :]
            even.append(jnp.where(low, a, jnp.roll(b, cols, axis=0)))
            odd.append(jnp.where(low, jnp.roll(a, cols, axis=0), b))
        return jnp.concatenate(even, axis=0), jnp.concatenate(odd, axis=0)

    for i in range(0, REACH, 2):
        edge[i], edge[i + 1] = row_pair((rows - REACH) // 2 * other + i // 2)

    halo_copy = pltpu.make_async_remote_copy(
        src_ref=edge, dst_ref=halo, send_sem=lat_send.at[2], recv_sem=lat_recv.at[2],
        device_id={"lat": other}, device_id_type=MESH,
    )
    halo_copy.start()
    advance(n // 2 - 2)

    def roll_row(values, place):
        step = jnp.full(values.shape, step_ref[lat * rows + place - REACH], jnp.int32)
        up = values
        down = values
        bit = 1
        while bit <= MOST_STEP:
            chosen = (step & bit) != 0
            up = jnp.where(chosen, jnp.roll(up, bit, axis=0), up)
            down = jnp.where(chosen, jnp.roll(down, -bit, axis=0), down)
            bit *= 2
        rolled[place, 0] = down
        rolled[place, 1] = values
        rolled[place, 2] = up

    def sum_rows(group):
        base = group * REACH
        sums = [None] * REACH
        for away in range(3 * REACH):
            sources = [rolled[base + away, side].reshape(all_lon // SUBLANES, SUBLANES, own) for side in range(3)]
            for q in range(REACH):
                offset = q + REACH - away
                if abs(offset) > REACH:
                    continue
                for side in range(3):
                    term = taps[base + away, 3 * (offset + REACH) + side][None] * sources[side]
                    sums[q] = term if sums[q] is None else sums[q] + term
        for q in range(REACH):
            acc_out[base + q] = sums[q].reshape(all_lon, own)

    @pl.loop(0, rows // 2)
    def _(pair):
        even, odd = row_pair(pair)
        roll_row(even, REACH + 2 * pair)
        roll_row(odd, REACH + 2 * pair + 1)

    groups = rows // REACH

    @pl.loop(0, groups - 1)
    def _(i):
        sum_rows(lax.rem(i + lat, groups))

    halo_copy.wait_recv()

    @pl.loop(0, REACH)
    def _(i):
        roll_row(halo[i], halo_at + i)

    sum_rows(lax.rem(groups - 1 + lat, groups))

    total = gather(0) * (1.0 / math.sqrt(2 * rows * all_lon))
    for i in range(full):
        gw_out[:, i * LANES : (i + 1) * LANES] = total[i * own : (i + 1) * own]
    if tail:
        packed = total[full * own :]
        gw_out[: own // 2, full * LANES :] = packed[:, :tail]
        gw_out[own // 2 :, full * LANES :] = packed[:, tail:]

    saved_copy.wait_send()
    pg_copy.wait_send()
    halo_copy.wait_send()
    for s in range(1, n):
        moves[s].wait_send()
    for j in order[n // 2 - WINDOW : -1]:
        sends[j].wait_send()


def write_out(acc_in, grad_in, acc_out, grad_out, sem):
    copies = [
        pltpu.make_async_copy(acc_in, acc_out, sem.at[0]),
        pltpu.make_async_copy(grad_in, grad_out, sem.at[1]),
    ]
    for copy in copies:
        copy.start()
    for copy in copies:
        copy.wait()


def kernel_body(saved, cotangent, weight, coefs, lon_step, row_reach):
    rows, cols, channels = saved.shape
    n = lax.axis_size("lon")
    own = channels // n
    half = channels // 2
    cells = rows * cols
    f32 = jnp.float32
    vmem = pl.BlockSpec(memory_space=pltpu.VMEM)
    anywhere = pl.BlockSpec(memory_space=pl.ANY)
    packed_rows = own * half // LANES
    acc, grad = pl.pallas_call(
        functools.partial(kernel, n),
        out_shape=(
            pltpu.VMEM((rows, n * cols, own), f32),
            pltpu.VMEM((own, half), f32),
        ),
        in_specs=[anywhere] * 6,
        out_specs=(vmem, vmem),
        scratch_shapes=[
            pltpu.SMEM(lon_step.shape, lon_step.dtype),
            pltpu.SMEM(row_reach.shape, row_reach.dtype),
            pltpu.VMEM(saved.shape, f32),
            pltpu.VMEM(cotangent.shape, f32),
            pltpu.VMEM(weight.shape, f32),
            pltpu.VMEM(coefs.shape, f32),
            pltpu.SemaphoreType.DMA((5 + -(-weight.shape[0] // SLAB),)),
            pltpu.VMEM((n, own, cells), f32),
            pltpu.VMEM((n, own, cells), f32),
            pltpu.VMEM((2, half, cells), f32),
            pltpu.VMEM((half, cells), f32),
            pltpu.VMEM((n, own, cells), f32),
            pltpu.VMEM((n, own, cells), f32),
            pltpu.VMEM((n, packed_rows, LANES), f32),
            pltpu.VMEM((n - 1, packed_rows, LANES), f32),
            pltpu.VMEM((n, own, channels), jnp.bfloat16),
            pltpu.VMEM((n, own, channels), jnp.bfloat16),
            pltpu.VMEM((n, cells, own), f32),
            pltpu.VMEM((REACH, n * cols, own), f32),
            pltpu.VMEM((REACH, n * cols, own), f32),
            pltpu.VMEM((rows + 2 * REACH, coefs.shape[0], SUBLANES, own), f32),
            pltpu.VMEM((rows + 2 * REACH, 3, n * cols, own), f32),
            pltpu.SemaphoreType.DMA((3,)),
            pltpu.SemaphoreType.DMA((3,)),
            pltpu.SemaphoreType.DMA((n - 1,)),
            pltpu.SemaphoreType.DMA((n - 1,)),
            pltpu.SemaphoreType.DMA((n - 1,)),
            pltpu.SemaphoreType.DMA((n - 1,)),
        ],
        compiler_params=pltpu.CompilerParams(
            collective_id=0, has_side_effects=True, vmem_limit_bytes=40 * 1024 * 1024
        ),
    )(*[
        pltpu.with_memory_space_constraint(x, pltpu.HBM)
        for x in (lon_step, row_reach, saved, cotangent, weight, coefs)
    ])
    acc, grad = pl.pallas_call(
        write_out,
        out_shape=(jax.ShapeDtypeStruct(acc.shape, f32), jax.ShapeDtypeStruct(grad.shape, f32)),
        in_specs=[vmem] * 2,
        out_specs=(anywhere,) * 2,
        scratch_shapes=[pltpu.SemaphoreType.DMA((2,))],
    )(*[pltpu.with_memory_space_constraint(x, pltpu.VMEM) for x in (acc, grad)])
    return jnp.transpose(acc, (2, 0, 1)), grad


def with_halo(x, sides, width):
    for axis, dim in sides:
        peers, length = (lax.axis_size(axis), x.shape[dim])
        up = [(i, (i + 1) % peers) for i in range(peers - 1)]
        down = [(j, i) for i, j in up]
        last = lax.slice_in_dim(x, length - width, length, axis=dim)
        initial = lax.slice_in_dim(x, 0, width, axis=dim)
        before = lax.ppermute(last, axis, up)
        after = lax.ppermute(initial, axis, down)
        x = jnp.concatenate([before, x, after], axis=dim)
    return x


def shift_rows(gradient, shifts, direction):
    width = gradient.shape[2]
    if direction == 0:
        return gradient
    wrapped = jnp.concatenate([gradient[:, :, width - 8 :], gradient, gradient[:, :, :8]], axis=2)
    result = gradient
    for amount in range(1, 9):
        begin = 8 - direction * amount
        piece = wrapped[:, :, begin : begin + width]
        result = jnp.where((shifts == amount)[None, :, None], piece, result)
    return result


def tap_term(rolled, coefs, row_reach, offset):
    summed = jnp.zeros_like(rolled[0])
    for lon_side in range(3):
        tap_index = (offset + 4) * 3 + lon_side
        summed = summed + jnp.transpose(coefs[tap_index])[:, :, None] * rolled[lon_side]
    live_rows = (abs(offset) <= row_reach).astype(jnp.float32)
    return summed * live_rows[None, :, None]


def collective_body(saved, cotangent, weight, coefs, lon_step, row_reach):
    lat_rows, lon_cols, channels = saved.shape
    lon_devices = lax.axis_size("lon")
    lat_devices = lax.axis_size("lat")
    own_channels = channels // lon_devices
    all_lon = lon_devices * lon_cols
    flat_rows = saved.reshape(lat_rows * lon_cols, channels)
    hidden = jnp.dot(
        flat_rows, weight, precision=lax.Precision.HIGHEST, preferred_element_type=jnp.float32
    )
    pre_grad = cotangent.reshape(lat_rows * lon_cols, channels) * gelu_slope(hidden)
    scale_factor = 1.0 / math.sqrt(lat_rows * lat_devices * all_lon)
    cell_grad = lax.dot_general(
        weight,
        pre_grad,
        (((1,), (1,)), ((), ())),
        precision=lax.Precision.HIGHEST,
        preferred_element_type=jnp.float32,
    )
    moved = lax.all_to_all(cell_grad, "lon", split_axis=0, concat_axis=1, tiled=True)
    gradient = (
        moved.reshape(own_channels, lon_devices, lat_rows, lon_cols)
        .transpose(0, 2, 1, 3)
        .reshape(own_channels, lat_rows, all_lon)
    )
    own_block = lax.psum_scatter(
        lax.dot_general(
            flat_rows,
            pre_grad,
            (((0,), (0,)), ((), ())),
            precision=lax.Precision.HIGHEST,
            preferred_element_type=jnp.float32,
        ),
        "lon",
        scatter_dimension=0,
        tiled=True,
    )
    grad_weight = lax.psum_scatter(own_block, "lat", scatter_dimension=1, tiled=True) * scale_factor
    row_start = lax.axis_index("lat") * lat_rows
    extended = with_halo(gradient, (("lat", 1),), 4)
    steps_padded = jnp.pad(lon_step, 4, constant_values=1)
    reach_padded = jnp.pad(row_reach, 4)
    coefs_padded = jnp.pad(coefs, ((0, 0), (4, 4), (0, 0)))
    wide_steps = lax.dynamic_slice_in_dim(steps_padded, row_start, lat_rows + 8)
    wide_reach = lax.dynamic_slice_in_dim(reach_padded, row_start, lat_rows + 8)
    wide_coefs = lax.dynamic_slice_in_dim(coefs_padded, row_start, lat_rows + 8, 1)
    rolled = [shift_rows(extended, wide_steps, lon_side) for lon_side in (-1, 0, 1)]
    result = jnp.zeros((own_channels, lat_rows, all_lon), jnp.float32)
    for offset in range(-4, 5):
        tap_sum = tap_term(rolled, wide_coefs, wide_reach, offset)
        result = result + tap_sum[:, 4 - offset : 4 - offset + lat_rows]
    return (result, grad_weight)


def body(saved, cotangent, weight, coefs, lon_step, row_reach):
    rows, cols, channels = saved.shape
    n = lax.axis_size("lon")
    fits = (
        lax.axis_size("lat") == 2
        and 4 <= n <= 16
        and n & (n - 1) == 0
        and channels % (16 * n) == 0
        and channels % LANES == 0
        and (rows * cols) % 128 == 0
        and rows % REACH == 0
        and rows >= 2 * REACH
        and 2 * cols == SUBLANES
        and n * cols >= 2 * MOST_STEP
    )
    run = kernel_body if fits else collective_body
    return run(saved, cotangent, weight, coefs, lon_step, row_reach)


def solution(mesh):
    placed = (
        P(("member", "lat"), "lon", None),
        P(("member", "lat"), "lon", None),
        P(),
        P(None, None, "lon"),
        P(),
        P(),
    )
    return jax.shard_map(
        body,
        mesh=mesh,
        in_specs=placed,
        out_specs=(P("lon", ("member", "lat"), None), P(("member", "lon"), "lat")),
        check_vma=False,
    )
```
